32 devices in a mesh: wide: 16 (over z, y, x), narrow: 2 (over core).
Axes of the slice: x: 2, y: 2, z: 4, core: 2. Of those that a mesh axis runs over, the one named last changes fastest.
Arguments:
- velocity: bfloat16 [16, 3, 16, 2, 4, 512], P(None, None, 'wide', 'narrow'), may hold values from -160 to 160
- extents: float32 [3, 16, 2, 4], P(None, 'wide', 'narrow'), may hold values from 0.5 to 2
Outputs:
- q_basis: bfloat16 [16, 3, 16, 2, 4, 512], P(None, None, 'wide', 'narrow')
- r_factor: float32 [16, 16], replicated
- dmd_operator: float32 [16, 15], replicated
The draws below stay inside these ranges and needn't reach their ends.
All inputs are finite; a program needn't handle non-finite values.
Results may differ from the reference program's by a relative error of at most 0.0055.
Values sent between devices are 32-bit elements; how exact they have to be, the bound alone decides.
A program may use at most 128 MiB of HBM per device.

```python
import math
import jax
import jax.numpy as jnp
import numpy as np
from jax import lax

SNAPS = 16
NODES = 512
ER = 4
NZC = 16
NTC = 2


def draw_velocity(key, part):
    base_key = jax.random.fold_in(key, 17)
    mode_key, noise_key, scale_key, freq_key, phase_key, decay_key = jax.random.split(base_key, 6)
    rest_shape = (3, NZC, NTC, ER, NODES)
    position = jnp.arange(NZC, dtype=jnp.float32) / max(NZC - 1, 1)
    modes = jnp.clip(jax.random.normal(mode_key, (6,) + rest_shape, jnp.float32), -6.0, 6.0)
    ramp = 1.0 + 2.0 * position
    rough = jnp.exp(jax.random.uniform(scale_key, (1, NZC, NTC, ER, 1), jnp.float32, math.log(0.5), math.log(2.0)))
    scaling = ramp.reshape(1, NZC, 1, 1, 1) * rough
    band_low = jnp.array([0.3, 0.9, 1.6], jnp.float32)
    band_high = jnp.array([0.6, 1.3, 2.2], jnp.float32)
    freqs = band_low + (band_high - band_low) * jax.random.uniform(freq_key, (3,), jnp.float32)
    phases = jax.random.uniform(phase_key, (3,), jnp.float32, -math.pi, math.pi)
    decays = jax.random.uniform(decay_key, (3,), jnp.float32, 0.0, 0.05)
    amplitudes = jnp.array([0.22, 0.16, 0.1], jnp.float32)
    times = jnp.arange(SNAPS, dtype=jnp.float32)
    angles = freqs[None, :] * times[:, None] + phases[None, :]
    envelope = amplitudes[None, :] * jnp.exp(-decays[None, :] * times[:, None])
    coeffs = jnp.concatenate([envelope * jnp.cos(angles), envelope * jnp.sin(angles)], axis=1)

    def one_snapshot(step):
        snap_index, coeff_row = step
        snap_key = jax.random.fold_in(noise_key, snap_index)
        noise = jnp.clip(jax.random.normal(snap_key, rest_shape, jnp.float32), -6.0, 6.0)
        field = jnp.tensordot(coeff_row, modes, axes=1) + 0.04 * noise
        return (field * scaling).astype(jnp.bfloat16)
    return lax.map(one_snapshot, (jnp.arange(SNAPS, dtype=jnp.int32), coeffs))


def block_levels(key, extent, shards, least, top_value):
    loudness, own = 1.0, jax.random.fold_in(key, 6)
    for dim, parts in shards:
        heights = jnp.exp(jax.random.uniform(jax.random.fold_in(own, dim), (parts,), jnp.float32, least / len(shards), top_value / len(shards)))
        loudness = loudness * jnp.repeat(heights, extent[dim] // parts).reshape([-1 if axis == dim else 1 for axis in range(len(extent))])
    return loudness


def setup_inputs(seed: int = 0) -> dict:
    key_of = jax.random.split(jax.random.key(seed), 3)
    velocity = draw_velocity(jax.random.fold_in(key_of[2], 71), 0)
    extents = jnp.clip(jnp.exp(math.log(2.0) - 1.3862944 * jax.random.uniform(key_of[1], (3, NZC, NTC, ER), jnp.float32) ** block_levels(key_of[1], (3, NZC, NTC, ER), ((1, 16), (2, 2)), -0.2, 0.2)), 0.5, 2.0)
    return {"velocity": velocity, "extents": extents}


def gll_tables():
    degree = 7
    node_count = 8
    gll_nodes = np.cos(np.pi * np.arange(node_count) / degree)
    legendre = np.zeros((node_count, node_count))
    for sweep_index in range(60):
        previous = gll_nodes.copy()
        legendre[:, 0] = 1.0
        legendre[:, 1] = previous
        for power in range(2, node_count):
            legendre[:, power] = ((2 * power - 1) * previous * legendre[:, power - 1] - (power - 1) * legendre[:, power - 2]) / power
        gll_nodes = previous - (previous * legendre[:, degree] - legendre[:, degree - 1]) / (node_count * legendre[:, degree])
    legendre[:, 0] = 1.0
    legendre[:, 1] = gll_nodes
    for power in range(2, node_count):
        legendre[:, power] = ((2 * power - 1) * gll_nodes * legendre[:, power - 1] - (power - 1) * legendre[:, power - 2]) / power
    top_poly = legendre[:, degree][::-1]
    weights = (2.0 / (degree * node_count * legendre[:, degree] ** 2))[::-1]
    ordered = gll_nodes[::-1]
    unit_diag = np.eye(node_count)
    spacing = ordered[:, None] - ordered[None, :] + unit_diag
    derivative = top_poly[:, None] / top_poly[None, :] / spacing
    derivative = derivative * (1.0 - unit_diag)
    derivative[0, 0] = -degree * node_count / 4.0
    derivative[-1, -1] = degree * node_count / 4.0
    return (derivative, weights)

def plane(field, along_axis):
    which = field.ndim + along_axis
    return (lax.index_in_dim(field, 0, which, keepdims=False), lax.index_in_dim(field, 7, which, keepdims=False))

def add_planes(field, along_axis, from_below, from_above):
    positions = jnp.arange(8)
    plane_shape = [8] + [1] * (-along_axis - 1)
    is_first = (positions == 0).astype(field.dtype).reshape(plane_shape)
    is_last = (positions == 7).astype(field.dtype).reshape(plane_shape)
    return field + is_first * jnp.expand_dims(from_below, along_axis) + is_last * jnp.expand_dims(from_above, along_axis)

def radial_pass(field):
    low_face, high_face = plane(field, -3)
    zero_plane = jnp.zeros_like(low_face[..., :1, :, :])
    from_below = jnp.concatenate([zero_plane, high_face[..., :-1, :, :]], axis=-3)
    from_above = jnp.concatenate([low_face[..., 1:, :, :], zero_plane], axis=-3)
    return add_planes(field, -3, from_below, from_above)

def assemble(field):
    field = radial_pass(field)
    low_face, high_face = plane(field, -1)
    field = add_planes(field, -1, jnp.roll(high_face, 1, axis=-5), jnp.roll(low_face, -1, axis=-5))
    low_face, high_face = plane(field, -2)
    field = add_planes(field, -2, jnp.roll(high_face, 1, axis=-4), jnp.roll(low_face, -1, axis=-4))
    return field

def reference(velocity, extents):
    derivative, weights = gll_tables()
    rounded = lax.optimization_barrier(jnp.asarray(derivative, jnp.float32).astype(jnp.bfloat16))
    unit_table = rounded.astype(jnp.float32)
    norm_weights = jnp.asarray(4.0 * weights, jnp.float32)
    cube_weights = norm_weights[:, None, None] * norm_weights[None, :, None] * norm_weights[None, None, :]
    scales = 2.0 / extents
    volume = extents[0] * extents[1] * extents[2]
    node_mass = volume[..., None, None, None] * cube_weights
    mass_total = assemble(node_mass)

    def one_snapshot(snapshot):
        field = snapshot.astype(jnp.float32).reshape(3, NZC, NTC, ER, 8, 8, 8)
        gradient = [scales[0][..., None, None, None] * jnp.einsum('ij,...jbc->...ibc', unit_table, field), scales[1][..., None, None, None] * jnp.einsum('ij,...ajc->...aic', unit_table, field), scales[2][..., None, None, None] * jnp.einsum('ij,...abj->...abi', unit_table, field)]
        vorticity = jnp.stack([gradient[(component + 1) % 3][(component + 2) % 3] - gradient[(component + 2) % 3][(component + 1) % 3] for component in range(3)])
        summed = assemble(node_mass * vorticity)
        return jnp.sqrt(node_mass) * (summed / mass_total)
    weighted = lax.map(one_snapshot, velocity)
    snapshot_rows = weighted.reshape(SNAPS, -1)
    row_count = snapshot_rows.shape[1]
    gram = jnp.dot(snapshot_rows, snapshot_rows.T, precision=lax.Precision.HIGHEST)
    upper_factor = jnp.linalg.cholesky(gram).T
    basis = lax.linalg.triangular_solve(upper_factor, snapshot_rows, left_side=True, lower=False, transpose_a=True)
    q_basis = (basis * math.sqrt(row_count)).astype(jnp.bfloat16).reshape(velocity.shape)
    r_factor = upper_factor / math.sqrt(row_count)
    dmd_operator = lax.linalg.triangular_solve(upper_factor[:SNAPS - 1, :SNAPS - 1], upper_factor[:, 1:], left_side=False, lower=False)
    return (q_basis, r_factor, dmd_operator)
```

```python
import functools
import math

import jax
import jax.numpy as jnp
import ml_dtypes
import numpy as np
from jax import lax
from jax.experimental import pallas as pl
from jax.experimental.pallas import tpu as pltpu
from jax.sharding import PartitionSpec as P

MESH = pl.DeviceIdType.MESH
F32 = jnp.float32
BF16 = jnp.bfloat16


def gll_tables():
    degree = 7
    node_count = 8
    gll_nodes = np.cos(np.pi * np.arange(node_count) / degree)
    legendre = np.zeros((node_count, node_count))
    for sweep_index in range(60):
        previous = gll_nodes.copy()
        legendre[:, 0] = 1.0
        legendre[:, 1] = previous
        for power in range(2, node_count):
            legendre[:, power] = (
                (2 * power - 1) * previous * legendre[:, power - 1]
                - (power - 1) * legendre[:, power - 2]
            ) / power
        gll_nodes = previous - (previous * legendre[:, degree] - legendre[:, degree - 1]) / (
            node_count * legendre[:, degree]
        )
    legendre[:, 0] = 1.0
    legendre[:, 1] = gll_nodes
    for power in range(2, node_count):
        legendre[:, power] = (
            (2 * power - 1) * gll_nodes * legendre[:, power - 1]
            - (power - 1) * legendre[:, power - 2]
        ) / power
    top_poly = legendre[:, degree][::-1]
    weights = (2.0 / (degree * node_count * legendre[:, degree] ** 2))[::-1]
    ordered = gll_nodes[::-1]
    unit_diag = np.eye(node_count)
    spacing = ordered[:, None] - ordered[None, :] + unit_diag
    derivative = top_poly[:, None] / top_poly[None, :] / spacing
    derivative = derivative * (1.0 - unit_diag)
    derivative[0, 0] = -degree * node_count / 4.0
    derivative[-1, -1] = degree * node_count / 4.0
    return (derivative, weights)


def tables():
    derivative, weights = gll_tables()
    d8 = derivative.astype(np.float32).astype(ml_dtypes.bfloat16).astype(np.float32)
    i8, i64 = np.eye(8, dtype=np.float32), np.eye(64, dtype=np.float32)
    full = [
        np.kron(d8, i64).T,
        np.kron(i8, np.kron(d8, i8)).T,
        np.kron(i64, d8).T,
    ]
    node = np.arange(512)
    i2, i3 = (node // 8) % 8, node % 8
    picks = np.concatenate([node[i3 == 0], node[i3 == 7], node[i2 == 0], node[i2 == 7]])
    faces = np.concatenate([table[:, picks] for table in full], axis=0)
    spread = np.zeros((2, 128, 512), np.float32)
    for which in range(2):
        spread[which, np.arange(128), picks[128 * which : 128 * which + 128]] = 1.0
    spread = np.concatenate([spread, spread], axis=1)
    cube = weights[:, None, None] * weights[None, :, None] * weights[None, None, :] * 64.0
    root = np.sqrt(cube).reshape(1, 512).astype(np.float32)
    half = lambda table: table.astype(ml_dtypes.bfloat16)
    return (
        half(full[0]),
        half(np.stack([full[1][:256, :256], full[2][:256, :256]])),
        half(faces),
        half(spread),
        root,
    )


def dot(left, right):
    return jnp.dot(left, right, preferred_element_type=F32)


def split(value):
    high = value.astype(BF16)
    low = (value - high.astype(F32)).astype(BF16)
    return high, low


def kernel(
    wide_count,
    narrow_count,
    vel_ref,
    ext_ref,
    first_ref,
    near_ref,
    face_ref,
    spread_ref,
    root_ref,
    q_ref,
    r_ref,
    dmd_ref,
    rows_ref,
    vb_ref,
    send_narrow,
    recv_narrow,
    send_wide,
    recv_wide,
    gram_ref,
    narrow_gram,
    wide_gram,
    face_send_sem,
    face_recv_sem,
    narrow_send_sem,
    narrow_recv_sem,
    wide_send_sem,
    wide_recv_sem,
):
    snaps, _, radial, nodes = vel_ref.shape
    fields = 3 * radial
    blocks = fields + 2 - fields % 2
    pairs = blocks // 2
    row_count = fields * nodes * wide_count * narrow_count
    me_w, me_n = lax.axis_index("wide"), lax.axis_index("narrow")
    wide_at = lambda step: (lax.rem(me_w + step, wide_count), me_n)
    narrow_at = lambda step: (me_w, lax.rem(me_n + step, narrow_count))

    barrier = pltpu.get_barrier_semaphore()
    for step in range(1, narrow_count):
        pl.semaphore_signal(barrier, inc=1, device_id=narrow_at(step), device_id_type=MESH)
    for step in range(1, wide_count):
        pl.semaphore_signal(barrier, inc=1, device_id=wide_at(step), device_id_type=MESH)

    for s in range(snaps):
        for c in range(3):
            value = vel_ref[s, c].astype(F32)
            for j in range(nodes // 128):
                rows_ref[j, pl.ds((s * 3 + c) * radial, radial), :] = value[
                    :, 128 * j : 128 * j + 128
                ]
    for b in range(fields):
        for j in range(nodes // 128):
            vb_ref[pl.ds(b * snaps, snaps), pl.ds(128 * j, 128)] = rows_ref[
                j, pl.ds(b, snaps, stride=fields), :
            ].astype(BF16)
    gram_ref[...] = jnp.zeros_like(gram_ref)
    part = radial * snaps
    comp = lambda c: vb_ref[pl.ds(c * part, part), :]
    pair = [
        jnp.concatenate([comp((k + 1) % 3), comp((k + 2) % 3)], axis=0) for k in range(3)
    ]

    extent = [[ext_ref[k * radial + e] for e in range(radial)] for k in range(3)]
    volume = [extent[0][e] * extent[1][e] * extent[2][e] for e in range(radial)]

    def curl(grads):
        out = []
        for a in range(3):
            b, c = (a + 1) % 3, (a + 2) % 3
            for e in range(radial):
                one = grads[b][e * snaps : (e + 1) * snaps]
                two = grads[c][part + e * snaps : part + (e + 1) * snaps]
                lead = 2.0 * extent[a][e]
                out.append((lead * extent[c][e]) * one - (lead * extent[b][e]) * two)
        return out

    grads = [dot(pair[k], face_ref[pl.ds(k * nodes, nodes), :]) for k in range(3)]
    raw = curl(grads)
    lane = lax.broadcasted_iota(jnp.int32, (snaps, 128), 1)
    place = lane % 64
    at_low, at_high = place < 8, place >= 56
    faces = [[], []]
    for which in range(2):
        cut = [block[:, 128 * which : 128 * which + 128] for block in raw]
        for a in range(3):
            for e in range(radial):
                value = cut[a * radial + e]
                if e > 0:
                    value += jnp.where(at_low, pltpu.roll(cut[a * radial + e - 1], 72, 1), 0.0)
                if e < radial - 1:
                    value += jnp.where(at_high, pltpu.roll(cut[a * radial + e + 1], 56, 1), 0.0)
                faces[which].append(value)
    line = lax.broadcasted_iota(jnp.int32, (snaps, 128), 0)
    mass = jnp.zeros((snaps, 128), F32)
    for e in range(radial):
        row = jnp.full((snaps, 128), volume[e], F32)
        if e > 0:
            row += jnp.where(at_low, volume[e - 1], 0.0)
        if e < radial - 1:
            row += jnp.where(at_high, volume[e + 1], 0.0)
        mass = jnp.where(line == e, row, mass)
    blank = jnp.zeros((snaps, 128), F32)
    for which in range(2):
        faces[which].append(mass)
        while len(faces[which]) < blocks:
            faces[which].append(blank)
    left = lane < 64

    def packed(which, p):
        one, two = faces[which][p], faces[which][p + pairs]
        low = jnp.where(left, one, pltpu.roll(two, 64, 1))
        high = jnp.where(left, pltpu.roll(one, 64, 1), two)
        return low, high

    for p in range(pairs):
        low, high = packed(1, p)
        send_narrow[0, p] = high
        send_narrow[1, p] = low
    wide_faces = [packed(0, p) for p in range(pairs)]

    pl.semaphore_wait(barrier, wide_count + narrow_count - 2)

    def face_copies(source, target, at, count, first):
        return [
            pltpu.make_async_remote_copy(
                src_ref=source.at[way],
                dst_ref=target.at[way],
                send_sem=face_send_sem.at[first + way],
                recv_sem=face_recv_sem.at[first + way],
                device_id=at(1 if way == 0 else count - 1),
                device_id_type=MESH,
            )
            for way in range(2)
        ]

    narrow_copies = face_copies(send_narrow, recv_narrow, narrow_at, narrow_count, 0)
    for copy in narrow_copies:
        copy.start()

    for copy in narrow_copies:
        copy.wait()
    edge_low, edge_high = lane % 8 == 0, lane % 8 == 7
    for p in range(pairs):
        low, high = wide_faces[p]
        below, above = recv_narrow[0, p], recv_narrow[1, p]
        low = low + jnp.where(edge_low, below, 0.0) + jnp.where(
            edge_high, pltpu.roll(above, 7, 1), 0.0
        )
        high = high + jnp.where(edge_high, above, 0.0) + jnp.where(
            edge_low, pltpu.roll(below, 121, 1), 0.0
        )
        send_wide[0, p] = high
        send_wide[1, p] = low
    wide_copies = face_copies(send_wide, recv_wide, wide_at, wide_count, 2)
    for copy in wide_copies:
        copy.start()

    near = [near_ref[0], near_ref[1]]
    whole = [dot(pair[0], first_ref[...])]
    for k in range(2):
        whole.append(
            jnp.concatenate(
                [dot(pair[k + 1][:, :256], near[k]), dot(pair[k + 1][:, 256:], near[k])], axis=1
            )
        )
    raw = curl(whole)
    right = jnp.logical_not(left)
    field = []
    for a in range(3):
        for e in range(radial):
            value = raw[a * radial + e]
            head, tail = value[:, :128], value[:, nodes - 128 :]
            if e > 0:
                last = raw[a * radial + e - 1][:, nodes - 128 :]
                head = head + jnp.where(left, pltpu.roll(last, 64, 1), 0.0)
            if e < radial - 1:
                first = raw[a * radial + e + 1][:, :128]
                tail = tail + jnp.where(right, pltpu.roll(first, 64, 1), 0.0)
            field.append(jnp.concatenate([head, value[:, 128 : nodes - 128], tail], axis=1))
    long_lane = lax.broadcasted_iota(jnp.int32, (snaps, nodes), 1)
    long_line = lax.broadcasted_iota(jnp.int32, (snaps, nodes), 0)
    mass = jnp.ones((snaps, nodes), F32)
    root = jnp.zeros((snaps, nodes), F32)
    for e in range(radial):
        row = jnp.full((snaps, nodes), volume[e], F32)
        size = row
        if e > 0:
            row += jnp.where(long_lane < 64, volume[e - 1], 0.0)
        if e < radial - 1:
            row += jnp.where(long_lane >= nodes - 64, volume[e + 1], 0.0)
        mass = jnp.where(long_line == e, row, mass)
        root = jnp.where(long_line == e, size, root)
    root = jnp.sqrt(root) * root_ref[...]
    field.append(mass)

    def spread(received, which):
        highs, lows = [], []
        for part_of in range(2):
            for p in range(pairs):
                below, above = received[0, p], received[1, p]
                if part_of == 0:
                    both = jnp.where(left, below, pltpu.roll(above, 64, 1))
                else:
                    both = jnp.where(left, pltpu.roll(below, 64, 1), above)
                high, low = split(both)
                highs.append(high)
                lows.append(low)
        stacked = jnp.concatenate(
            [jnp.concatenate(highs, axis=0), jnp.concatenate(lows, axis=0)], axis=1
        )
        return dot(stacked, spread_ref[which])

    extra = spread(recv_narrow, 1)
    field = [value + extra[b * snaps : (b + 1) * snaps] for b, value in enumerate(field)]

    for copy in wide_copies:
        copy.wait()
    extra = spread(recv_wide, 0)
    field = [value + extra[b * snaps : (b + 1) * snaps] for b, value in enumerate(field)]

    scale = root / field[fields]
    highs, lows = [], []
    for b in range(fields):
        e = b % radial
        high, low = split(field[b] * scale[e : e + 1, :])
        highs.append(high)
        lows.append(low)
    high = jnp.concatenate(highs, axis=1)
    low = jnp.concatenate(lows, axis=1)
    both = jnp.concatenate([high, low], axis=0)
    product = lax.dot_general(
        both, both, (((1,), (1,)), ((), ())), preferred_element_type=F32
    )
    gram_ref[:, : 2 * snaps] = product
    product = gram_ref[...]
    top = product[:snaps]
    gram = top + pltpu.roll(top, 128 - snaps, 1) + product[snaps:]
    slim_lane = lax.broadcasted_iota(jnp.int32, (8, 128), 1)
    groups = snaps // 8
    compact = jnp.zeros((8, 128), F32)
    for g in range(groups):
        piece = gram[8 * g : 8 * g + 8]
        if g:
            piece = pltpu.roll(piece, g * snaps, 1)
        inside = jnp.logical_and(slim_lane >= g * snaps, slim_lane < (g + 1) * snaps)
        compact = jnp.where(inside, piece, compact)

    def total(own, buffer, me, at, count, send_sem, recv_sem):
        buffer[me] = own
        copies = [
            pltpu.make_async_remote_copy(
                src_ref=buffer.at[me],
                dst_ref=buffer.at[me],
                send_sem=send_sem.at[step - 1],
                recv_sem=recv_sem.at[step - 1],
                device_id=at(step),
                device_id_type=MESH,
            )
            for step in range(1, count)
        ]
        for copy in copies:
            copy.start()
        for copy in copies:
            copy.wait()
        terms = [buffer[i] for i in range(count)]
        while len(terms) > 1:
            terms = [
                terms[i] + terms[i + 1] if i + 1 < len(terms) else terms[i]
                for i in range(0, len(terms), 2)
            ]
        return terms[0]

    compact = total(
        compact, narrow_gram, me_n, narrow_at, narrow_count, narrow_send_sem, narrow_recv_sem
    )
    compact = total(
        compact, wide_gram, me_w, wide_at, wide_count, wide_send_sem, wide_recv_sem
    )

    lines = [compact]
    for g in range(1, groups):
        lines.append(pltpu.roll(compact, 128 - g * snaps, 1))
    work = jnp.concatenate(lines, axis=0)
    unit = jnp.logical_and(lane % snaps == line, lane < 4 * snaps)
    work = jnp.where(lane < snaps, work, jnp.where(unit, 1.0, 0.0))
    for k in range(snaps - 1):
        lead = work[k : k + 1, :]
        ratio = lead * (1.0 / work[k : k + 1, k : k + 1])
        work = work - jnp.where(line > k, work[:, k : k + 1], 0.0) * ratio
    pivot = jnp.sum(jnp.where(lane == line, work, 0.0), axis=1, keepdims=True)
    work = work * (1.0 / jnp.sqrt(pivot))
    norm = math.sqrt(row_count)
    inverse = pltpu.roll(work, 128 - snaps, 1)
    big, small = split(inverse * norm)
    weights = jnp.where(lane < 2 * snaps, big.astype(F32), small.astype(F32))
    weights = weights[:, : 3 * snaps].astype(BF16)
    basis = dot(weights, jnp.concatenate([both, high], axis=0))
    for b in range(fields):
        q_ref[pl.ds(b * snaps, snaps), :] = basis[:, b * nodes : (b + 1) * nodes].astype(BF16)
    upper = jnp.where(jnp.logical_and(lane >= line, lane < snaps), work, 0.0)
    r_ref[...] = upper[:, :snaps] / norm
    moved = jnp.where(lane < snaps - 1, pltpu.roll(upper, 127, 1), 0.0)
    back = jnp.where(lane < snaps - 1, inverse, 0.0)
    operator = lax.dot_general(
        moved,
        back,
        (((1,), (1,)), ((), ())),
        precision=lax.Precision.HIGHEST,
        preferred_element_type=F32,
    )
    dmd_ref[...] = operator[:, : snaps - 1]


def shards(wide_count, narrow_count, velocity, extents):
    snaps, _, _, _, radial, nodes = velocity.shape
    fields = 3 * radial
    pairs = (fields + 2) // 2
    vmem = pl.BlockSpec(memory_space=pltpu.VMEM)
    face = pltpu.VMEM((2, pairs, snaps, 128), F32)
    dma = pltpu.SemaphoreType.DMA
    q, r, dmd = pl.pallas_call(
        functools.partial(kernel, wide_count, narrow_count),
        out_shape=(
            jax.ShapeDtypeStruct((fields * snaps, nodes), BF16),
            jax.ShapeDtypeStruct((snaps, snaps), F32),
            jax.ShapeDtypeStruct((snaps, snaps - 1), F32),
        ),
        in_specs=[vmem, pl.BlockSpec(memory_space=pltpu.SMEM)] + [vmem] * 5,
        out_specs=(vmem, vmem, vmem),
        scratch_shapes=[
            pltpu.VMEM((nodes // 128, fields * snaps, 128), F32),
            pltpu.VMEM((fields * snaps, nodes), BF16),
            face,
            face,
            face,
            face,
            pltpu.VMEM((2 * snaps, 128), F32),
            pltpu.VMEM((narrow_count, 8, 128), F32),
            pltpu.VMEM((wide_count, 8, 128), F32),
            dma((4,)),
            dma((4,)),
            dma((narrow_count - 1,)),
            dma((narrow_count - 1,)),
            dma((wide_count - 1,)),
            dma((wide_count - 1,)),
        ],
        compiler_params=pltpu.CompilerParams(
            collective_id=0, has_side_effects=True, vmem_limit_bytes=32 * 1024 * 1024
        ),
        cost_estimate=pl.CostEstimate(
            flops=400_000_000, bytes_accessed=3_000_000, transcendentals=10_000
        ),
        name="pipe",
    )(
        velocity.reshape(snaps, 3, radial, nodes),
        extents.reshape(3 * radial),
        *[jnp.asarray(table) for table in tables()],
    )
    q = jnp.transpose(q.reshape(3, radial, snaps, nodes), (2, 0, 1, 3))
    return q.reshape(velocity.shape), r, dmd


def solution(mesh):
    return jax.shard_map(
        functools.partial(shards, mesh.shape["wide"], mesh.shape["narrow"]),
        mesh=mesh,
        in_specs=(P(None, None, "wide", "narrow", None, None), P(None, "wide", "narrow", None)),
        out_specs=(P(None, None, "wide", "narrow", None, None), P(), P()),
        check_vma=False,
    )
```

```python
import functools
import math

import jax
import jax.numpy as jnp
import ml_dtypes
import numpy as np
from jax import lax
from jax.experimental import pallas as pl
from jax.experimental.pallas import tpu as pltpu
from jax.sharding import PartitionSpec as P

MESH = pl.DeviceIdType.MESH
F32 = jnp.float32
BF16 = jnp.bfloat16


def gll_tables():
    degree = 7
    node_count = 8
    gll_nodes = np.cos(np.pi * np.arange(node_count) / degree)
    legendre = np.zeros((node_count, node_count))
    for sweep_index in range(60):
        previous = gll_nodes.copy()
        legendre[:, 0] = 1.0
        legendre[:, 1] = previous
        for power in range(2, node_count):
            legendre[:, power] = (
                (2 * power - 1) * previous * legendre[:, power - 1]
                - (power - 1) * legendre[:, power - 2]
            ) / power
        gll_nodes = previous - (previous * legendre[:, degree] - legendre[:, degree - 1]) / (
            node_count * legendre[:, degree]
        )
    legendre[:, 0] = 1.0
    legendre[:, 1] = gll_nodes
    for power in range(2, node_count):
        legendre[:, power] = (
            (2 * power - 1) * gll_nodes * legendre[:, power - 1]
            - (power - 1) * legendre[:, power - 2]
        ) / power
    top_poly = legendre[:, degree][::-1]
    weights = (2.0 / (degree * node_count * legendre[:, degree] ** 2))[::-1]
    ordered = gll_nodes[::-1]
    unit_diag = np.eye(node_count)
    spacing = ordered[:, None] - ordered[None, :] + unit_diag
    derivative = top_poly[:, None] / top_poly[None, :] / spacing
    derivative = derivative * (1.0 - unit_diag)
    derivative[0, 0] = -degree * node_count / 4.0
    derivative[-1, -1] = degree * node_count / 4.0
    return (derivative, weights)


def tables():
    derivative, weights = gll_tables()
    d8 = derivative.astype(np.float32).astype(ml_dtypes.bfloat16).astype(np.float32)
    i8, i64 = np.eye(8, dtype=np.float32), np.eye(64, dtype=np.float32)
    full = [
        np.kron(d8, i64).T,
        np.kron(i8, np.kron(d8, i8)).T,
        np.kron(i64, d8).T,
    ]
    node = np.arange(512)
    i2, i3 = (node // 8) % 8, node % 8
    picks = np.concatenate([node[i3 == 0], node[i3 == 7], node[i2 == 0], node[i2 == 7]])
    faces = np.concatenate([table[:, picks] for table in full], axis=0)
    spread = np.zeros((2, 128, 512), np.float32)
    for which in range(2):
        spread[which, np.arange(128), picks[128 * which : 128 * which + 128]] = 1.0
    spread = np.concatenate([spread, spread], axis=1)
    cube = weights[:, None, None] * weights[None, :, None] * weights[None, None, :] * 64.0
    root = np.sqrt(cube).reshape(1, 512).astype(np.float32)
    half = lambda table: table.astype(ml_dtypes.bfloat16)
    return (
        half(full[0]),
        half(np.stack([full[1][:256, :256], full[2][:256, :256]])),
        half(faces),
        half(spread),
        root,
    )


def dot(left, right):
    return jnp.dot(left, right, preferred_element_type=F32)


def split(value):
    high = value.astype(BF16)
    low = (value - high.astype(F32)).astype(BF16)
    return high, low


def kernel(
    wide_count,
    narrow_count,
    vel_in,
    ext_in,
    first_in,
    near_in,
    face_in,
    spread_in,
    root_in,
    q_ref,
    r_ref,
    dmd_ref,
    vel_ref,
    ext_ref,
    first_ref,
    near_ref,
    face_ref,
    spread_ref,
    root_ref,
    load_sem,
    rows_ref,
    vb_ref,
    send_narrow,
    recv_narrow,
    send_wide,
    recv_wide,
    send_edge,
    recv_edge,
    gram_ref,
    narrow_gram,
    wide_gram,
    face_send_sem,
    face_recv_sem,
    edge_send_sem,
    edge_recv_sem,
    narrow_send_sem,
    narrow_recv_sem,
    wide_send_sem,
    wide_recv_sem,
):
    snaps, _, radial, nodes = vel_ref.shape
    fields = 3 * radial
    blocks = fields + 2 - fields % 2
    pairs = blocks // 2
    row_count = fields * nodes * wide_count * narrow_count
    me_w, me_n = lax.axis_index("wide"), lax.axis_index("narrow")
    wide_at = lambda step: (lax.rem(me_w + step, wide_count), me_n)
    narrow_at = lambda step: (me_w, lax.rem(me_n + step, narrow_count))

    loads = [
        pltpu.make_async_copy(source, target, load_sem.at[i])
        for i, (source, target) in enumerate(
            [
                (vel_in, vel_ref),
                (ext_in, ext_ref),
                (face_in, face_ref),
                (first_in, first_ref),
                (near_in, near_ref),
                (spread_in, spread_ref),
                (root_in, root_ref),
            ]
        )
    ]
    for load in loads:
        load.start()

    barrier = pltpu.get_barrier_semaphore()
    for step in range(1, narrow_count):
        pl.semaphore_signal(barrier, inc=1, device_id=narrow_at(step), device_id_type=MESH)
    for step in range(1, wide_count):
        pl.semaphore_signal(barrier, inc=1, device_id=wide_at(step), device_id_type=MESH)
    turns = sorted({1, narrow_count - 1})
    corner_at = lambda step, turn: (
        lax.rem(me_w + step, wide_count),
        lax.rem(me_n + turn, narrow_count),
    )
    ways = (1, wide_count - 1)
    for step in ways:
        for turn in turns:
            pl.semaphore_signal(
                barrier, inc=1, device_id=corner_at(step, turn), device_id_type=MESH
            )
    loads[0].wait()
    for s in range(snaps):
        for c in range(3):
            value = vel_ref[s, c].astype(F32)
            for j in range(nodes // 128):
                rows_ref[j, pl.ds((s * 3 + c) * radial, radial), :] = value[
                    :, 128 * j : 128 * j + 128
                ]
    for b in range(fields):
        for j in range(nodes // 128):
            vb_ref[pl.ds(b * snaps, snaps), pl.ds(128 * j, 128)] = rows_ref[
                j, pl.ds(b, snaps, stride=fields), :
            ].astype(BF16)
    gram_ref[...] = jnp.zeros_like(gram_ref)
    part = radial * snaps
    comp = lambda c: vb_ref[pl.ds(c * part, part), :]
    pair = [
        jnp.concatenate([comp((k + 1) % 3), comp((k + 2) % 3)], axis=0) for k in range(3)
    ]

    loads[1].wait()
    extent = [[ext_ref[k * radial + e] for e in range(radial)] for k in range(3)]
    volume = [extent[0][e] * extent[1][e] * extent[2][e] for e in range(radial)]

    def curl(grads):
        out = []
        for a in range(3):
            b, c = (a + 1) % 3, (a + 2) % 3
            for e in range(radial):
                one = grads[b][e * snaps : (e + 1) * snaps]
                two = grads[c][part + e * snaps : part + (e + 1) * snaps]
                lead = 2.0 * extent[a][e]
                out.append((lead * extent[c][e]) * one - (lead * extent[b][e]) * two)
        return out

    loads[2].wait()
    grads = [dot(pair[k], face_ref[pl.ds(k * nodes, nodes), :]) for k in range(3)]
    raw = curl(grads)
    lane = lax.broadcasted_iota(jnp.int32, (snaps, 128), 1)
    place = lane % 64
    at_low, at_high = place < 8, place >= 56
    faces = [[], []]
    for which in range(2):
        cut = [block[:, 128 * which : 128 * which + 128] for block in raw]
        for a in range(3):
            for e in range(radial):
                value = cut[a * radial + e]
                if e > 0:
                    value += jnp.where(at_low, pltpu.roll(cut[a * radial + e - 1], 72, 1), 0.0)
                if e < radial - 1:
                    value += jnp.where(at_high, pltpu.roll(cut[a * radial + e + 1], 56, 1), 0.0)
                faces[which].append(value)
    line = lax.broadcasted_iota(jnp.int32, (snaps, 128), 0)
    mass = jnp.zeros((snaps, 128), F32)
    for e in range(radial):
        row = jnp.full((snaps, 128), volume[e], F32)
        if e > 0:
            row += jnp.where(at_low, volume[e - 1], 0.0)
        if e < radial - 1:
            row += jnp.where(at_high, volume[e + 1], 0.0)
        mass = jnp.where(line == e, row, mass)
    blank = jnp.zeros((snaps, 128), F32)
    for which in range(2):
        faces[which].append(mass)
        while len(faces[which]) < blocks:
            faces[which].append(blank)
    left = lane < 64

    def packed(which, p):
        one, two = faces[which][p], faces[which][p + pairs]
        low = jnp.where(left, one, pltpu.roll(two, 64, 1))
        high = jnp.where(left, pltpu.roll(one, 64, 1), two)
        return low, high

    for p in range(pairs):
        low, high = packed(1, p)
        send_narrow[0, p] = high
        send_narrow[1, p] = low
    groups_of = -(-pairs // 4)
    residue = lane % 8
    edge_of = [
        jnp.logical_or(residue == 2 * r, residue == (2 * r + 7) % 8) for r in range(4)
    ]
    for g in range(groups_of):
        edges = [blank, blank]
        for r in range(4):
            p = 4 * g + r
            if p >= pairs:
                continue
            low, high = packed(0, p)
            send_wide[0, p] = high
            send_wide[1, p] = low
            for way, value in enumerate((high, low)):
                if r:
                    value = pltpu.roll(value, 2 * r, 1)
                edges[way] = jnp.where(edge_of[r], value, edges[way])
        for way in range(2):
            send_edge[way, g] = edges[way]

    pl.semaphore_wait(barrier, wide_count + narrow_count - 2 + 2 * len(turns))

    def face_copies(source, target, at, count, first):
        return [
            pltpu.make_async_remote_copy(
                src_ref=source.at[way],
                dst_ref=target.at[way],
                send_sem=face_send_sem.at[first + way],
                recv_sem=face_recv_sem.at[first + way],
                device_id=at(1 if way == 0 else count - 1),
                device_id_type=MESH,
            )
            for way in range(2)
        ]

    wide_copies = face_copies(send_wide, recv_wide, wide_at, wide_count, 2)
    edge_copies = [
        pltpu.make_async_remote_copy(
            src_ref=send_edge.at[way],
            dst_ref=recv_edge.at[way, i],
            send_sem=edge_send_sem.at[way, i],
            recv_sem=edge_recv_sem.at[way, i],
            device_id=corner_at(ways[way], turn),
            device_id_type=MESH,
        )
        for way in range(2)
        for i, turn in enumerate(turns)
    ]
    narrow_copies = face_copies(send_narrow, recv_narrow, narrow_at, narrow_count, 0)
    for copy in wide_copies + edge_copies + narrow_copies:
        copy.start()

    for load in loads[3:]:
        load.wait()
    near = [near_ref[0], near_ref[1]]
    whole = [dot(pair[0], first_ref[...])]
    for k in range(2):
        whole.append(
            jnp.concatenate(
                [dot(pair[k + 1][:, :256], near[k]), dot(pair[k + 1][:, 256:], near[k])], axis=1
            )
        )
    raw = curl(whole)
    right = jnp.logical_not(left)
    field = []
    for a in range(3):
        for e in range(radial):
            value = raw[a * radial + e]
            head, tail = value[:, :128], value[:, nodes - 128 :]
            if e > 0:
                last = raw[a * radial + e - 1][:, nodes - 128 :]
                head = head + jnp.where(left, pltpu.roll(last, 64, 1), 0.0)
            if e < radial - 1:
                first = raw[a * radial + e + 1][:, :128]
                tail = tail + jnp.where(right, pltpu.roll(first, 64, 1), 0.0)
            field.append(jnp.concatenate([head, value[:, 128 : nodes - 128], tail], axis=1))
    long_lane = lax.broadcasted_iota(jnp.int32, (snaps, nodes), 1)
    long_line = lax.broadcasted_iota(jnp.int32, (snaps, nodes), 0)
    mass = jnp.ones((snaps, nodes), F32)
    root = jnp.zeros((snaps, nodes), F32)
    for e in range(radial):
        row = jnp.full((snaps, nodes), volume[e], F32)
        size = row
        if e > 0:
            row += jnp.where(long_lane < 64, volume[e - 1], 0.0)
        if e < radial - 1:
            row += jnp.where(long_lane >= nodes - 64, volume[e + 1], 0.0)
        mass = jnp.where(long_line == e, row, mass)
        root = jnp.where(long_line == e, size, root)
    root = jnp.sqrt(root) * root_ref[...]
    field.append(mass)

    edge_low, edge_high = residue == 0, residue == 7

    def with_edges(way, p):
        g, r = p // 4, p % 4
        pieces = []
        for slot, places, shift in ((0, edge_low, 121), (len(turns) - 1, edge_high, 7)):
            piece = pltpu.roll(recv_edge[way, slot, g], (shift - 2 * r) % 128, 1)
            pieces.append(jnp.where(places, piece, 0.0))
        return recv_wide[way, p] + (pieces[0] + pieces[1])

    def spread(received, which):
        highs, lows = [], []
        for part_of in range(2):
            for p in range(pairs):
                below, above = received(0, p), received(1, p)
                if part_of == 0:
                    both = jnp.where(left, below, pltpu.roll(above, 64, 1))
                else:
                    both = jnp.where(left, pltpu.roll(below, 64, 1), above)
                high, low = split(both)
                highs.append(high)
                lows.append(low)
        stacked = jnp.concatenate(
            [jnp.concatenate(highs, axis=0), jnp.concatenate(lows, axis=0)], axis=1
        )
        return dot(stacked, spread_ref[which])

    for copy in narrow_copies:
        copy.wait()
    extra = spread(lambda way, p: recv_narrow[way, p], 1)
    field = [value + extra[b * snaps : (b + 1) * snaps] for b, value in enumerate(field)]

    for copy in edge_copies + wide_copies:
        copy.wait()
    extra = spread(with_edges, 0)
    field = [value + extra[b * snaps : (b + 1) * snaps] for b, value in enumerate(field)]

    scale = root / field[fields]
    highs, lows = [], []
    for b in range(fields):
        e = b % radial
        high, low = split(field[b] * scale[e : e + 1, :])
        highs.append(high)
        lows.append(low)
    high = jnp.concatenate(highs, axis=1)
    low = jnp.concatenate(lows, axis=1)
    both = jnp.concatenate([high, low], axis=0)
    product = lax.dot_general(
        both, both, (((1,), (1,)), ((), ())), preferred_element_type=F32
    )
    gram_ref[:, : 2 * snaps] = product
    product = gram_ref[...]
    top = product[:snaps]
    gram = top + pltpu.roll(top, 128 - snaps, 1) + product[snaps:]
    slim_lane = lax.broadcasted_iota(jnp.int32, (8, 128), 1)
    groups = snaps // 8
    compact = jnp.zeros((8, 128), F32)
    for g in range(groups):
        piece = gram[8 * g : 8 * g + 8]
        if g:
            piece = pltpu.roll(piece, g * snaps, 1)
        inside = jnp.logical_and(slim_lane >= g * snaps, slim_lane < (g + 1) * snaps)
        compact = jnp.where(inside, piece, compact)

    def total(own, buffer, me, at, count, send_sem, recv_sem):
        buffer[me] = own
        copies = [
            pltpu.make_async_remote_copy(
                src_ref=buffer.at[me],
                dst_ref=buffer.at[me],
                send_sem=send_sem.at[step - 1],
                recv_sem=recv_sem.at[step - 1],
                device_id=at(step),
                device_id_type=MESH,
            )
            for step in range(1, count)
        ]
        for copy in copies:
            copy.start()
        for copy in copies:
            copy.wait()
        terms = [buffer[i] for i in range(count)]
        while len(terms) > 1:
            terms = [
                terms[i] + terms[i + 1] if i + 1 < len(terms) else terms[i]
                for i in range(0, len(terms), 2)
            ]
        return terms[0]

    compact = total(
        compact, narrow_gram, me_n, narrow_at, narrow_count, narrow_send_sem, narrow_recv_sem
    )
    compact = total(
        compact, wide_gram, me_w, wide_at, wide_count, wide_send_sem, wide_recv_sem
    )

    lines = [compact]
    for g in range(1, groups):
        lines.append(pltpu.roll(compact, 128 - g * snaps, 1))
    work = jnp.concatenate(lines, axis=0)
    unit = jnp.logical_and(lane % snaps == line, lane < 4 * snaps)
    work = jnp.where(lane < snaps, work, jnp.where(unit, 1.0, 0.0))
    for k in range(snaps - 1):
        lead = work[k : k + 1, :]
        ratio = lead * (1.0 / work[k : k + 1, k : k + 1])
        work = work - jnp.where(line > k, work[:, k : k + 1], 0.0) * ratio
    pivot = jnp.sum(jnp.where(lane == line, work, 0.0), axis=1, keepdims=True)
    work = work * (1.0 / jnp.sqrt(pivot))
    norm = math.sqrt(row_count)
    inverse = pltpu.roll(work, 128 - snaps, 1)
    big, small = split(inverse * norm)
    weights = jnp.where(lane < 2 * snaps, big.astype(F32), small.astype(F32))
    weights = weights[:, : 3 * snaps].astype(BF16)
    basis = dot(weights, jnp.concatenate([both, high], axis=0))
    for b in range(fields):
        q_ref[pl.ds(b * snaps, snaps), :] = basis[:, b * nodes : (b + 1) * nodes].astype(BF16)
    upper = jnp.where(jnp.logical_and(lane >= line, lane < snaps), work, 0.0)
    r_ref[...] = upper[:, :snaps] / norm
    moved = jnp.where(lane < snaps - 1, pltpu.roll(upper, 127, 1), 0.0)
    back = jnp.where(lane < snaps - 1, inverse, 0.0)
    operator = lax.dot_general(
        moved,
        back,
        (((1,), (1,)), ((), ())),
        precision=lax.Precision.HIGHEST,
        preferred_element_type=F32,
    )
    dmd_ref[...] = operator[:, : snaps - 1]


def shards(wide_count, narrow_count, velocity, extents):
    snaps, _, _, _, radial, nodes = velocity.shape
    fields = 3 * radial
    pairs = (fields + 2) // 2
    vmem = pl.BlockSpec(memory_space=pltpu.VMEM)
    operands = [
        velocity.reshape(snaps, 3, radial, nodes),
        extents.reshape(3 * radial),
        *[jnp.asarray(table) for table in tables()],
    ]
    corners = len({1, narrow_count - 1})
    edge = (-(-pairs // 4), snaps, 128)
    face = pltpu.VMEM((2, pairs, snaps, 128), F32)
    dma = pltpu.SemaphoreType.DMA
    q, r, dmd = pl.pallas_call(
        functools.partial(kernel, wide_count, narrow_count),
        out_shape=(
            jax.ShapeDtypeStruct((fields * snaps, nodes), BF16),
            jax.ShapeDtypeStruct((snaps, snaps), F32),
            jax.ShapeDtypeStruct((snaps, snaps - 1), F32),
        ),
        in_specs=[pl.BlockSpec(memory_space=pltpu.HBM)] * len(operands),
        out_specs=(vmem, vmem, vmem),
        scratch_shapes=[
            (pltpu.SMEM if i == 1 else pltpu.VMEM)(operand.shape, operand.dtype)
            for i, operand in enumerate(operands)
        ]
        + [
            dma((len(operands),)),
            pltpu.VMEM((nodes // 128, fields * snaps, 128), F32),
            pltpu.VMEM((fields * snaps, nodes), BF16),
            face,
            face,
            face,
            face,
            pltpu.VMEM((2,) + edge, F32),
            pltpu.VMEM((2, corners) + edge, F32),
            pltpu.VMEM((2 * snaps, 128), F32),
            pltpu.VMEM((narrow_count, 8, 128), F32),
            pltpu.VMEM((wide_count, 8, 128), F32),
            dma((4,)),
            dma((4,)),
            dma((2, corners)),
            dma((2, corners)),
            dma((narrow_count - 1,)),
            dma((narrow_count - 1,)),
            dma((wide_count - 1,)),
            dma((wide_count - 1,)),
        ],
        compiler_params=pltpu.CompilerParams(
            collective_id=0, has_side_effects=True, vmem_limit_bytes=60 * 1024 * 1024
        ),
        cost_estimate=pl.CostEstimate(
            flops=400_000_000, bytes_accessed=3_000_000, transcendentals=10_000
        ),
        name="pipe",
    )(*operands)
    q = jnp.transpose(q.reshape(3, radial, snaps, nodes), (2, 0, 1, 3))
    return q.reshape(velocity.shape), r, dmd


def solution(mesh):
    return jax.shard_map(
        functools.partial(shards, mesh.shape["wide"], mesh.shape["narrow"]),
        mesh=mesh,
        in_specs=(P(None, None, "wide", "narrow", None, None), P(None, "wide", "narrow", None)),
        out_specs=(P(None, None, "wide", "narrow", None, None), P(), P()),
        check_vma=False,
    )
```

```python
import functools
import math

import jax
import jax.numpy as jnp
import ml_dtypes
import numpy as np
from jax import lax
from jax.experimental import pallas as pl
from jax.experimental.pallas import tpu as pltpu
from jax.sharding import PartitionSpec as P

MESH = pl.DeviceIdType.MESH
F32 = jnp.float32
BF16 = jnp.bfloat16


def gll_tables():
    degree = 7
    node_count = 8
    gll_nodes = np.cos(np.pi * np.arange(node_count) / degree)
    legendre = np.zeros((node_count, node_count))
    for sweep_index in range(60):
        previous = gll_nodes.copy()
        legendre[:, 0] = 1.0
        legendre[:, 1] = previous
        for power in range(2, node_count):
            legendre[:, power] = (
                (2 * power - 1) * previous * legendre[:, power - 1]
                - (power - 1) * legendre[:, power - 2]
            ) / power
        gll_nodes = previous - (previous * legendre[:, degree] - legendre[:, degree - 1]) / (
            node_count * legendre[:, degree]
        )
    legendre[:, 0] = 1.0
    legendre[:, 1] = gll_nodes
    for power in range(2, node_count):
        legendre[:, power] = (
            (2 * power - 1) * gll_nodes * legendre[:, power - 1]
            - (power - 1) * legendre[:, power - 2]
        ) / power
    top_poly = legendre[:, degree][::-1]
    weights = (2.0 / (degree * node_count * legendre[:, degree] ** 2))[::-1]
    ordered = gll_nodes[::-1]
    unit_diag = np.eye(node_count)
    spacing = ordered[:, None] - ordered[None, :] + unit_diag
    derivative = top_poly[:, None] / top_poly[None, :] / spacing
    derivative = derivative * (1.0 - unit_diag)
    derivative[0, 0] = -degree * node_count / 4.0
    derivative[-1, -1] = degree * node_count / 4.0
    return (derivative, weights)


def tables():
    derivative, weights = gll_tables()
    d8 = derivative.astype(np.float32).astype(ml_dtypes.bfloat16).astype(np.float32)
    i8, i64 = np.eye(8, dtype=np.float32), np.eye(64, dtype=np.float32)
    full = [
        np.kron(d8, i64).T,
        np.kron(i8, np.kron(d8, i8)).T,
        np.kron(i64, d8).T,
    ]
    node = np.arange(512)
    i2, i3 = (node // 8) % 8, node % 8
    picks = np.concatenate([node[i3 == 0], node[i3 == 7], node[i2 == 0], node[i2 == 7]])
    faces = np.concatenate([table[:, picks] for table in full], axis=0)
    spread = np.zeros((2, 128, 512), np.float32)
    for which in range(2):
        spread[which, np.arange(128), picks[128 * which : 128 * which + 128]] = 1.0
    spread = np.concatenate([spread, spread], axis=1)
    cube = weights[:, None, None] * weights[None, :, None] * weights[None, None, :] * 64.0
    root = np.sqrt(cube).reshape(1, 512).astype(np.float32)
    half = lambda table: table.astype(ml_dtypes.bfloat16)
    return (
        half(full[0]),
        half(np.stack([full[1][:256, :256], full[2][:256, :256]])),
        half(faces),
        half(spread),
        root,
        np.concatenate([root[:, picks[:64]]] * 2, axis=1),
    )


def dot(left, right):
    return jnp.dot(left, right, preferred_element_type=F32)


def split(value):
    high = value.astype(BF16)
    low = (value - high.astype(F32)).astype(BF16)
    return high, low


def kernel(
    wide_count,
    narrow_count,
    vel_in,
    ext_in,
    first_in,
    near_in,
    face_in,
    spread_in,
    root_in,
    edge_root_in,
    z_out,
    total_ref,
    vel_ref,
    ext_ref,
    first_ref,
    near_ref,
    face_ref,
    spread_ref,
    root_ref,
    edge_root_ref,
    load_sem,
    rows_ref,
    vb_ref,
    z_ref,
    z_sem,
    send_narrow,
    recv_narrow,
    send_wide,
    recv_wide,
    send_edge,
    recv_edge,
    gram_ref,
    narrow_gram,
    wide_gram,
    face_send_sem,
    face_recv_sem,
    edge_send_sem,
    edge_recv_sem,
    narrow_send_sem,
    narrow_recv_sem,
    wide_send_sem,
    wide_recv_sem,
):
    snaps, _, radial, nodes = vel_ref.shape
    fields = 3 * radial
    blocks = fields + 2 - fields % 2
    pairs = blocks // 2
    me_w, me_n = lax.axis_index("wide"), lax.axis_index("narrow")
    wide_at = lambda step: (lax.rem(me_w + step, wide_count), me_n)
    narrow_at = lambda step: (me_w, lax.rem(me_n + step, narrow_count))

    loads = [
        pltpu.make_async_copy(source, target, load_sem.at[i])
        for i, (source, target) in enumerate(
            [
                (vel_in, vel_ref),
                (ext_in, ext_ref),
                (face_in, face_ref),
                (first_in, first_ref),
                (near_in, near_ref),
                (spread_in, spread_ref),
                (root_in, root_ref),
                (edge_root_in, edge_root_ref),
            ]
        )
    ]
    for load in loads:
        load.start()

    barrier = pltpu.get_barrier_semaphore()
    for step in range(1, narrow_count):
        pl.semaphore_signal(barrier, inc=1, device_id=narrow_at(step), device_id_type=MESH)
    for step in range(1, wide_count):
        pl.semaphore_signal(barrier, inc=1, device_id=wide_at(step), device_id_type=MESH)
    turns = sorted({1, narrow_count - 1})
    corner_at = lambda step, turn: (
        lax.rem(me_w + step, wide_count),
        lax.rem(me_n + turn, narrow_count),
    )
    ways = (1, wide_count - 1)
    for step in ways:
        for turn in turns:
            pl.semaphore_signal(
                barrier, inc=1, device_id=corner_at(step, turn), device_id_type=MESH
            )
    loads[0].wait()
    for s in range(snaps):
        for c in range(3):
            value = vel_ref[s, c].astype(F32)
            for j in range(nodes // 128):
                rows_ref[j, pl.ds((s * 3 + c) * radial, radial), :] = value[
                    :, 128 * j : 128 * j + 128
                ]
    for b in range(fields):
        for j in range(nodes // 128):
            vb_ref[pl.ds(b * snaps, snaps), pl.ds(128 * j, 128)] = rows_ref[
                j, pl.ds(b, snaps, stride=fields), :
            ].astype(BF16)
    gram_ref[...] = jnp.zeros_like(gram_ref)
    part = radial * snaps
    comp = lambda c: vb_ref[pl.ds(c * part, part), :]
    pair = [
        jnp.concatenate([comp((k + 1) % 3), comp((k + 2) % 3)], axis=0) for k in range(3)
    ]

    loads[1].wait()
    extent = [[ext_ref[k, 0, 0, e] for e in range(radial)] for k in range(3)]
    volume = [extent[0][e] * extent[1][e] * extent[2][e] for e in range(radial)]

    def curl(grads):
        out = []
        for a in range(3):
            b, c = (a + 1) % 3, (a + 2) % 3
            for e in range(radial):
                one = grads[b][e * snaps : (e + 1) * snaps]
                two = grads[c][part + e * snaps : part + (e + 1) * snaps]
                lead = 2.0 * extent[a][e]
                out.append((lead * extent[c][e]) * one - (lead * extent[b][e]) * two)
        return out

    loads[2].wait()
    grads = [dot(pair[k], face_ref[pl.ds(k * nodes, nodes), :]) for k in range(3)]
    raw = curl(grads)
    lane = lax.broadcasted_iota(jnp.int32, (snaps, 128), 1)
    place = lane % 64
    at_low, at_high = place < 8, place >= 56
    faces = [[], []]
    for which in range(2):
        cut = [block[:, 128 * which : 128 * which + 128] for block in raw]
        for a in range(3):
            for e in range(radial):
                value = cut[a * radial + e]
                if e > 0:
                    value += jnp.where(at_low, pltpu.roll(cut[a * radial + e - 1], 72, 1), 0.0)
                if e < radial - 1:
                    value += jnp.where(at_high, pltpu.roll(cut[a * radial + e + 1], 56, 1), 0.0)
                faces[which].append(value)
    line = lax.broadcasted_iota(jnp.int32, (snaps, 128), 0)
    mass = jnp.zeros((snaps, 128), F32)
    for e in range(radial):
        row = jnp.full((snaps, 128), volume[e], F32)
        if e > 0:
            row += jnp.where(at_low, volume[e - 1], 0.0)
        if e < radial - 1:
            row += jnp.where(at_high, volume[e + 1], 0.0)
        mass = jnp.where(line == e, row, mass)
    blank = jnp.zeros((snaps, 128), F32)
    for which in range(2):
        faces[which].append(mass)
        while len(faces[which]) < blocks:
            faces[which].append(blank)
    left = lane < 64

    def packed(which, p):
        one, two = faces[which][p], faces[which][p + pairs]
        low = jnp.where(left, one, pltpu.roll(two, 64, 1))
        high = jnp.where(left, pltpu.roll(one, 64, 1), two)
        return low, high

    for p in range(pairs):
        low, high = packed(1, p)
        send_narrow[0, p] = high
        send_narrow[1, p] = low
    groups_of = -(-pairs // 4)
    residue = lane % 8
    edge_of = [
        jnp.logical_or(residue == 2 * r, residue == (2 * r + 7) % 8) for r in range(4)
    ]
    for g in range(groups_of):
        edges = [blank, blank]
        for r in range(4):
            p = 4 * g + r
            if p >= pairs:
                continue
            low, high = packed(0, p)
            send_wide[0, p] = high
            send_wide[1, p] = low
            for way, value in enumerate((high, low)):
                if r:
                    value = pltpu.roll(value, 2 * r, 1)
                edges[way] = jnp.where(edge_of[r], value, edges[way])
        for way in range(2):
            send_edge[way, g] = edges[way]

    pl.semaphore_wait(barrier, wide_count + narrow_count - 2 + 2 * len(turns))

    def face_copies(source, target, at, count, first):
        return [
            pltpu.make_async_remote_copy(
                src_ref=source.at[way],
                dst_ref=target.at[way],
                send_sem=face_send_sem.at[first + way],
                recv_sem=face_recv_sem.at[first + way],
                device_id=at(1 if way == 0 else count - 1),
                device_id_type=MESH,
            )
            for way in range(2)
        ]

    wide_copies = face_copies(send_wide, recv_wide, wide_at, wide_count, 2)
    edge_copies = [
        pltpu.make_async_remote_copy(
            src_ref=send_edge.at[way],
            dst_ref=recv_edge.at[way, i],
            send_sem=edge_send_sem.at[way, i],
            recv_sem=edge_recv_sem.at[way, i],
            device_id=corner_at(ways[way], turn),
            device_id_type=MESH,
        )
        for way in range(2)
        for i, turn in enumerate(turns)
    ]
    narrow_copies = face_copies(send_narrow, recv_narrow, narrow_at, narrow_count, 0)
    for copy in wide_copies + edge_copies + narrow_copies:
        copy.start()

    for load in loads[3:]:
        load.wait()
    near = [near_ref[0], near_ref[1]]
    whole = [dot(pair[0], first_ref[...])]
    for k in range(2):
        whole.append(
            jnp.concatenate(
                [dot(pair[k + 1][:, :256], near[k]), dot(pair[k + 1][:, 256:], near[k])], axis=1
            )
        )
    raw = curl(whole)
    right = jnp.logical_not(left)
    field = []
    for a in range(3):
        for e in range(radial):
            value = raw[a * radial + e]
            head, tail = value[:, :128], value[:, nodes - 128 :]
            if e > 0:
                last = raw[a * radial + e - 1][:, nodes - 128 :]
                head = head + jnp.where(left, pltpu.roll(last, 64, 1), 0.0)
            if e < radial - 1:
                first = raw[a * radial + e + 1][:, :128]
                tail = tail + jnp.where(right, pltpu.roll(first, 64, 1), 0.0)
            field.append(jnp.concatenate([head, value[:, 128 : nodes - 128], tail], axis=1))
    long_lane = lax.broadcasted_iota(jnp.int32, (snaps, nodes), 1)
    long_line = lax.broadcasted_iota(jnp.int32, (snaps, nodes), 0)
    mass = jnp.ones((snaps, nodes), F32)
    root = jnp.zeros((snaps, nodes), F32)
    for e in range(radial):
        row = jnp.full((snaps, nodes), volume[e], F32)
        size = row
        if e > 0:
            row += jnp.where(long_lane < 64, volume[e - 1], 0.0)
        if e < radial - 1:
            row += jnp.where(long_lane >= nodes - 64, volume[e + 1], 0.0)
        mass = jnp.where(long_line == e, row, mass)
        root = jnp.where(long_line == e, size, root)
    root = jnp.sqrt(root) * root_ref[...]
    field.append(mass)

    edge_low, edge_high = residue == 0, residue == 7

    for copy in narrow_copies:
        copy.wait()
    highs, lows = [], []
    for part_of in range(2):
        for p in range(pairs):
            below, above = recv_narrow[0, p], recv_narrow[1, p]
            if part_of == 0:
                both = jnp.where(left, below, pltpu.roll(above, 64, 1))
            else:
                both = jnp.where(left, pltpu.roll(below, 64, 1), above)
            high, low = split(both)
            highs.append(high)
            lows.append(low)
    stacked = jnp.concatenate(
        [jnp.concatenate(highs, axis=0), jnp.concatenate(lows, axis=0)], axis=1
    )
    extra = dot(stacked, spread_ref[1])
    field = [value + extra[b * snaps : (b + 1) * snaps] for b, value in enumerate(field)]
    inner = jnp.logical_and(long_lane % 8 != 0, long_lane % 8 != 7)
    scale = jnp.where(inner, root / field[fields], 0.0)
    for b in range(fields):
        e = b % radial
        high, low = split(field[b] * scale[e : e + 1, :])
        z_ref[0:snaps, pl.ds(b * nodes, nodes)] = high
        z_ref[snaps : 2 * snaps, pl.ds(b * nodes, nodes)] = low

    def products(both):
        return lax.dot_general(
            both, both, (((1,), (1,)), ((), ())), preferred_element_type=F32
        )

    inside = products(z_ref[...])
    own = [[], []]
    for p in range(pairs):
        below, above = recv_narrow[0, p], recv_narrow[1, p]
        own[0].append(
            send_wide[1, p]
            + jnp.where(edge_low, below, 0.0)
            + jnp.where(edge_high, pltpu.roll(above, 7, 1), 0.0)
        )
        own[1].append(
            send_wide[0, p]
            + jnp.where(edge_high, above, 0.0)
            + jnp.where(edge_low, pltpu.roll(below, 121, 1), 0.0)
        )
    edge_size = jnp.zeros((snaps, 128), F32)
    for e in range(radial):
        edge_size = jnp.where(line == e, jnp.full((snaps, 128), volume[e], F32), edge_size)
    edge_root = jnp.sqrt(edge_size) * edge_root_ref[...]

    for copy in edge_copies + wide_copies:
        copy.wait()

    def arrived(way, p):
        g, r = p // 4, p % 4
        pieces = []
        for slot, places, shift in ((0, edge_low, 121), (len(turns) - 1, edge_high, 7)):
            piece = pltpu.roll(recv_edge[way, slot, g], (shift - 2 * r) % 128, 1)
            pieces.append(jnp.where(places, piece, 0.0))
        return own[way][p] + (recv_wide[way, p] + (pieces[0] + pieces[1]))

    mass_pair, mass_left = fields % pairs, fields < pairs
    ends = [[], []]
    for way in range(2):
        values = [arrived(way, p) for p in range(pairs)]
        mass = values[mass_pair]
        turned = pltpu.roll(mass, 64, 1)
        mass = jnp.where(left, mass, turned) if mass_left else jnp.where(left, turned, mass)
        scale = edge_root / mass
        for p in range(pairs):
            one, two = p % radial, (p + pairs) % radial
            factor = jnp.where(left, scale[one : one + 1, :], scale[two : two + 1, :])
            if p >= fields:
                factor = jnp.zeros_like(factor)
            elif p + pairs >= fields:
                factor = jnp.where(left, factor, 0.0)
            ends[way].append(split(values[p] * factor))
    ends = ends[0] + ends[1]
    both = jnp.concatenate(
        [jnp.concatenate([end[i] for end in ends], axis=1) for i in range(2)], axis=0
    )
    gram_ref[:, : 2 * snaps] = inside + products(both)
    product = gram_ref[...]
    top = product[:snaps]
    gram = top + pltpu.roll(top, 128 - snaps, 1) + product[snaps:]
    slim_lane = lax.broadcasted_iota(jnp.int32, (8, 128), 1)
    groups = snaps // 8
    compact = jnp.zeros((8, 128), F32)
    for g in range(groups):
        piece = gram[8 * g : 8 * g + 8]
        if g:
            piece = pltpu.roll(piece, g * snaps, 1)
        inside = jnp.logical_and(slim_lane >= g * snaps, slim_lane < (g + 1) * snaps)
        compact = jnp.where(inside, piece, compact)

    def total(own, buffer, me, at, count, send_sem, recv_sem, meanwhile=None):
        buffer[me] = own
        copies = [
            pltpu.make_async_remote_copy(
                src_ref=buffer.at[me],
                dst_ref=buffer.at[me],
                send_sem=send_sem.at[step - 1],
                recv_sem=recv_sem.at[step - 1],
                device_id=at(step),
                device_id_type=MESH,
            )
            for step in range(1, count)
        ]
        for copy in copies:
            copy.start()
        if meanwhile is not None:
            meanwhile()
        for copy in copies:
            copy.wait()
        terms = [buffer[i] for i in range(count)]
        while len(terms) > 1:
            terms = [
                terms[i] + terms[i + 1] if i + 1 < len(terms) else terms[i]
                for i in range(0, len(terms), 2)
            ]
        return terms[0]

    compact = total(
        compact, narrow_gram, me_n, narrow_at, narrow_count, narrow_send_sem, narrow_recv_sem
    )

    def whole_rows():
        for i in range(2):
            values = []
            for b in range(fields):
                p, two = b % pairs, b >= pairs
                low, high = ends[p][i].astype(F32), ends[pairs + p][i].astype(F32)
                if two:
                    low = pltpu.roll(low, 64, 1)
                else:
                    high = pltpu.roll(high, 64, 1)
                values.append(jnp.where(left, low, high))
            rows = dot(jnp.concatenate(values, axis=0).astype(BF16), spread_ref[0, 0:128, :])
            for b in range(fields):
                at = (pl.ds(i * snaps, snaps), pl.ds(b * nodes, nodes))
                kept = z_ref[at].astype(F32)
                z_ref[at] = (kept + rows[b * snaps : (b + 1) * snaps]).astype(BF16)
        copy = pltpu.make_async_copy(z_ref, z_out, z_sem)
        copy.start()
        return copy

    copy = []
    total_ref[...] = total(
        compact,
        wide_gram,
        me_w,
        wide_at,
        wide_count,
        wide_send_sem,
        wide_recv_sem,
        lambda: copy.append(whole_rows()),
    )
    copy[0].wait()


def basis_kernel(
    row_count, radial, total_ref, z_in, q_ref, r_ref, dmd_ref, z_ref, rows_ref, z_sem
):
    snaps, nodes = q_ref.shape[0], q_ref.shape[3]
    fields = 3 * radial
    load = pltpu.make_async_copy(z_in, z_ref, z_sem)
    load.start()
    lane = lax.broadcasted_iota(jnp.int32, (snaps, 128), 1)
    line = lax.broadcasted_iota(jnp.int32, (snaps, 128), 0)
    compact = total_ref[...]
    lines = [compact]
    for g in range(1, snaps // 8):
        lines.append(pltpu.roll(compact, 128 - g * snaps, 1))
    work = jnp.concatenate(lines, axis=0)
    unit = jnp.logical_and(lane % snaps == line, lane < 4 * snaps)
    work = jnp.where(lane < snaps, work, jnp.where(unit, 1.0, 0.0))
    for k in range(0, snaps - 1, 2):
        row_a, row_b = work[k : k + 1, :], work[k + 1 : k + 2, :]
        col_a, col_b = work[:, k : k + 1], work[:, k + 1 : k + 2]
        inv_a = 1.0 / work[k : k + 1, k : k + 1]
        cross = work[k : k + 1, k + 1 : k + 2]
        ratio = cross * inv_a
        inv_b = 1.0 / (work[k + 1 : k + 2, k + 1 : k + 2] - cross * ratio)
        row_b = row_b - ratio * row_a
        col_b = col_b - ratio * col_a
        after = work - col_a * (inv_a * row_a) - col_b * (inv_b * row_b)
        work = jnp.where(line > k + 1, after, jnp.where(line == k + 1, row_b, work))
    pivot = jnp.sum(jnp.where(lane == line, work, 0.0), axis=1, keepdims=True)
    work = work * (1.0 / jnp.sqrt(pivot))
    norm = math.sqrt(row_count)
    inverse = pltpu.roll(work, 128 - snaps, 1)
    big, small = split(inverse * norm)
    weights = jnp.where(lane < 2 * snaps, big.astype(F32), small.astype(F32))
    weights = weights[:, : 3 * snaps].astype(BF16)
    load.wait()
    basis = dot(weights, jnp.concatenate([z_ref[...], z_ref[0:snaps, :]], axis=0))
    for b in range(fields):
        for j in range(nodes // 128):
            first = b * nodes + 128 * j
            rows_ref[j, pl.ds(b, snaps, stride=fields), :] = basis[:, first : first + 128]
    for s in range(snaps):
        for c in range(3):
            value = [
                rows_ref[j, pl.ds((s * 3 + c) * radial, radial), :] for j in range(nodes // 128)
            ]
            q_ref[s, c] = jnp.concatenate(value, axis=1).astype(BF16)
    upper = jnp.where(jnp.logical_and(lane >= line, lane < snaps), work, 0.0)
    r_ref[...] = upper[:, :snaps] / norm
    moved = jnp.where(lane < snaps - 1, pltpu.roll(upper, 127, 1), 0.0)
    back = jnp.where(lane < snaps - 1, inverse, 0.0)
    operator = lax.dot_general(
        moved,
        back,
        (((1,), (1,)), ((), ())),
        precision=lax.Precision.HIGHEST,
        preferred_element_type=F32,
    )
    dmd_ref[...] = operator[:, : snaps - 1]


def shards(wide_count, narrow_count, velocity, extents):
    snaps, _, _, _, radial, nodes = velocity.shape
    fields = 3 * radial
    pairs = (fields + 2) // 2
    vmem = pl.BlockSpec(memory_space=pltpu.VMEM)
    operands = [
        velocity.reshape(snaps, 3, radial, nodes),
        extents,
        *[jnp.asarray(table) for table in tables()],
    ]
    corners = len({1, narrow_count - 1})
    edge = (-(-pairs // 4), snaps, 128)
    face = pltpu.VMEM((2, pairs, snaps, 128), F32)
    dma = pltpu.SemaphoreType.DMA
    limit = 60 * 1024 * 1024
    hbm = pl.BlockSpec(memory_space=pltpu.HBM)
    rows = jax.ShapeDtypeStruct((2 * snaps, fields * nodes), BF16)
    rows, total = pl.pallas_call(
        functools.partial(kernel, wide_count, narrow_count),
        out_shape=(rows, jax.ShapeDtypeStruct((8, 128), F32)),
        in_specs=[hbm] * len(operands),
        out_specs=(hbm, vmem),
        scratch_shapes=[
            (pltpu.SMEM if i == 1 else pltpu.VMEM)(operand.shape, operand.dtype)
            for i, operand in enumerate(operands)
        ]
        + [
            dma((len(operands),)),
            pltpu.VMEM((nodes // 128, fields * snaps, 128), F32),
            pltpu.VMEM((fields * snaps, nodes), BF16),
            pltpu.VMEM((2 * snaps, fields * nodes), BF16),
            dma(()),
            face,
            face,
            face,
            face,
            pltpu.VMEM((2,) + edge, F32),
            pltpu.VMEM((2, corners) + edge, F32),
            pltpu.VMEM((2 * snaps, 128), F32),
            pltpu.VMEM((narrow_count, 8, 128), F32),
            pltpu.VMEM((wide_count, 8, 128), F32),
            dma((4,)),
            dma((4,)),
            dma((2, corners)),
            dma((2, corners)),
            dma((narrow_count - 1,)),
            dma((narrow_count - 1,)),
            dma((wide_count - 1,)),
            dma((wide_count - 1,)),
        ],
        compiler_params=pltpu.CompilerParams(
            collective_id=0, has_side_effects=True, vmem_limit_bytes=limit
        ),
        cost_estimate=pl.CostEstimate(
            flops=400_000_000, bytes_accessed=3_000_000, transcendentals=10_000
        ),
        name="pipe",
    )(*operands)
    row_count = fields * nodes * wide_count * narrow_count
    q, r, dmd = pl.pallas_call(
        functools.partial(basis_kernel, row_count, radial),
        out_shape=(
            jax.ShapeDtypeStruct((snaps, 3, radial, nodes), BF16),
            jax.ShapeDtypeStruct((snaps, snaps), F32),
            jax.ShapeDtypeStruct((snaps, snaps - 1), F32),
        ),
        in_specs=[vmem, hbm],
        out_specs=(vmem, vmem, vmem),
        scratch_shapes=[
            pltpu.VMEM((2 * snaps, fields * nodes), BF16),
            pltpu.VMEM((nodes // 128, fields * snaps, 128), F32),
            dma(()),
        ],
        compiler_params=pltpu.CompilerParams(vmem_limit_bytes=limit),
        name="basis",
    )(total, rows)
    return q.reshape(velocity.shape), r, dmd


def solution(mesh):
    return jax.shard_map(
        functools.partial(shards, mesh.shape["wide"], mesh.shape["narrow"]),
        mesh=mesh,
        in_specs=(P(None, None, "wide", "narrow", None, None), P(None, "wide", "narrow", None)),
        out_specs=(P(None, None, "wide", "narrow", None, None), P(), P()),
        check_vma=False,
    )
```

```python
import functools
import math

import jax
import jax.numpy as jnp
import ml_dtypes
import numpy as np
from jax import lax
from jax.experimental import pallas as pl
from jax.experimental.pallas import tpu as pltpu
from jax.sharding import PartitionSpec as P

MESH = pl.DeviceIdType.MESH
F32 = jnp.float32
BF16 = jnp.bfloat16


def gll_tables():
    degree = 7
    node_count = 8
    gll_nodes = np.cos(np.pi * np.arange(node_count) / degree)
    legendre = np.zeros((node_count, node_count))
    for sweep_index in range(60):
        previous = gll_nodes.copy()
        legendre[:, 0] = 1.0
        legendre[:, 1] = previous
        for power in range(2, node_count):
            legendre[:, power] = (
                (2 * power - 1) * previous * legendre[:, power - 1]
                - (power - 1) * legendre[:, power - 2]
            ) / power
        gll_nodes = previous - (previous * legendre[:, degree] - legendre[:, degree - 1]) / (
            node_count * legendre[:, degree]
        )
    legendre[:, 0] = 1.0
    legendre[:, 1] = gll_nodes
    for power in range(2, node_count):
        legendre[:, power] = (
            (2 * power - 1) * gll_nodes * legendre[:, power - 1]
            - (power - 1) * legendre[:, power - 2]
        ) / power
    top_poly = legendre[:, degree][::-1]
    weights = (2.0 / (degree * node_count * legendre[:, degree] ** 2))[::-1]
    ordered = gll_nodes[::-1]
    unit_diag = np.eye(node_count)
    spacing = ordered[:, None] - ordered[None, :] + unit_diag
    derivative = top_poly[:, None] / top_poly[None, :] / spacing
    derivative = derivative * (1.0 - unit_diag)
    derivative[0, 0] = -degree * node_count / 4.0
    derivative[-1, -1] = degree * node_count / 4.0
    return (derivative, weights)


def tables():
    derivative, weights = gll_tables()
    d8 = derivative.astype(np.float32).astype(ml_dtypes.bfloat16).astype(np.float32)
    i8, i64 = np.eye(8, dtype=np.float32), np.eye(64, dtype=np.float32)
    full = [
        np.kron(d8, i64).T,
        np.kron(i8, np.kron(d8, i8)).T,
        np.kron(i64, d8).T,
    ]
    node = np.arange(512)
    i2, i3 = (node // 8) % 8, node % 8
    picks = np.concatenate([node[i3 == 0], node[i3 == 7], node[i2 == 0], node[i2 == 7]])
    faces = np.concatenate([table[:, picks] for table in full], axis=0)
    spread = np.zeros((2, 128, 512), np.float32)
    for which in range(2):
        spread[which, np.arange(128), picks[128 * which : 128 * which + 128]] = 1.0
    spread = np.concatenate([spread, spread], axis=1)
    cube = weights[:, None, None] * weights[None, :, None] * weights[None, None, :] * 64.0
    root = np.sqrt(cube).reshape(1, 512).astype(np.float32)
    half = lambda table: table.astype(ml_dtypes.bfloat16)
    return (
        half(full[0]),
        half(np.stack([full[1][:256, :256], full[2][:256, :256]])),
        half(faces),
        half(spread),
        root,
        np.concatenate([root[:, picks[:64]]] * 2, axis=1),
    )


def dot(left, right):
    return jnp.dot(left, right, preferred_element_type=F32)


def split(value):
    high = value.astype(BF16)
    low = (value - high.astype(F32)).astype(BF16)
    return high, low


def kernel(
    wide_count,
    narrow_count,
    vel_in,
    ext_in,
    first_in,
    near_in,
    face_in,
    spread_in,
    root_in,
    edge_root_in,
    z_out,
    total_ref,
    vel_ref,
    ext_ref,
    first_ref,
    near_ref,
    face_ref,
    spread_ref,
    root_ref,
    edge_root_ref,
    load_sem,
    rows_ref,
    vb_ref,
    z_ref,
    z_sem,
    send_narrow,
    recv_narrow,
    send_wide,
    recv_wide,
    send_edge,
    recv_edge,
    gram_ref,
    sums_ref,
    face_send_sem,
    face_recv_sem,
    edge_send_sem,
    edge_recv_sem,
    sum_send_sem,
    sum_recv_sem,
):
    snaps, _, radial, nodes = vel_ref.shape
    fields = 3 * radial
    blocks = fields + 2 - fields % 2
    pairs = blocks // 2
    me_w, me_n = lax.axis_index("wide"), lax.axis_index("narrow")
    wide_at = lambda step: (lax.rem(me_w + step, wide_count), me_n)
    narrow_at = lambda step: (me_w, lax.rem(me_n + step, narrow_count))

    loads = [
        pltpu.make_async_copy(source, target, load_sem.at[i])
        for i, (source, target) in enumerate(
            [
                (vel_in, vel_ref),
                (ext_in, ext_ref),
                (face_in, face_ref),
                (first_in, first_ref),
                (near_in, near_ref),
                (spread_in, spread_ref),
                (root_in, root_ref),
                (edge_root_in, edge_root_ref),
            ]
        )
    ]
    for load in loads[:3]:
        load.start()

    barrier = pltpu.get_barrier_semaphore()
    count = wide_count * narrow_count
    me = me_w * narrow_count + me_n

    def device(step):
        peer = lax.rem(me + step, count)
        return (peer // narrow_count, lax.rem(peer, narrow_count))

    def each_peer(action):
        if count <= 64:
            for step in range(1, count):
                action(step)
        else:
            lax.fori_loop(1, count, lambda step, carry: (action(step), carry)[1], 0)

    each_peer(
        lambda step: pl.semaphore_signal(
            barrier, inc=1, device_id=device(step), device_id_type=MESH
        )
    )
    turns = sorted({1, narrow_count - 1})
    corner_at = lambda step, turn: (
        lax.rem(me_w + step, wide_count),
        lax.rem(me_n + turn, narrow_count),
    )
    ways = (1, wide_count - 1)
    loads[0].wait()
    for s in range(snaps):
        for c in range(3):
            value = vel_ref[s, c].astype(F32)
            for j in range(nodes // 128):
                rows_ref[j, pl.ds((s * 3 + c) * radial, radial), :] = value[
                    :, 128 * j : 128 * j + 128
                ]
    for b in range(fields):
        for j in range(nodes // 128):
            vb_ref[pl.ds(b * snaps, snaps), pl.ds(128 * j, 128)] = rows_ref[
                j, pl.ds(b, snaps, stride=fields), :
            ].astype(BF16)
    gram_ref[...] = jnp.zeros_like(gram_ref)
    part = radial * snaps
    comp = lambda c: vb_ref[pl.ds(c * part, part), :]
    pair = [
        jnp.concatenate([comp((k + 1) % 3), comp((k + 2) % 3)], axis=0) for k in range(3)
    ]

    loads[1].wait()
    extent = [[ext_ref[k, 0, 0, e] for e in range(radial)] for k in range(3)]
    volume = [extent[0][e] * extent[1][e] * extent[2][e] for e in range(radial)]

    def curl(grads):
        out = []
        for a in range(3):
            b, c = (a + 1) % 3, (a + 2) % 3
            for e in range(radial):
                one = grads[b][e * snaps : (e + 1) * snaps]
                two = grads[c][part + e * snaps : part + (e + 1) * snaps]
                lead = 2.0 * extent[a][e]
                out.append((lead * extent[c][e]) * one - (lead * extent[b][e]) * two)
        return out

    loads[2].wait()
    for load in loads[3:]:
        load.start()
    grads = [dot(pair[k], face_ref[pl.ds(k * nodes, nodes), :]) for k in range(3)]
    raw = curl(grads)
    lane = lax.broadcasted_iota(jnp.int32, (snaps, 128), 1)
    place = lane % 64
    at_low, at_high = place < 8, place >= 56
    faces = [[], []]
    for which in range(2):
        cut = [block[:, 128 * which : 128 * which + 128] for block in raw]
        for a in range(3):
            for e in range(radial):
                value = cut[a * radial + e]
                if e > 0:
                    value += jnp.where(at_low, pltpu.roll(cut[a * radial + e - 1], 72, 1), 0.0)
                if e < radial - 1:
                    value += jnp.where(at_high, pltpu.roll(cut[a * radial + e + 1], 56, 1), 0.0)
                faces[which].append(value)
    line = lax.broadcasted_iota(jnp.int32, (snaps, 128), 0)
    mass = jnp.zeros((snaps, 128), F32)
    for e in range(radial):
        row = jnp.full((snaps, 128), volume[e], F32)
        if e > 0:
            row += jnp.where(at_low, volume[e - 1], 0.0)
        if e < radial - 1:
            row += jnp.where(at_high, volume[e + 1], 0.0)
        mass = jnp.where(line == e, row, mass)
    blank = jnp.zeros((snaps, 128), F32)
    for which in range(2):
        faces[which].append(mass)
        while len(faces[which]) < blocks:
            faces[which].append(blank)
    left = lane < 64

    def packed(which, p):
        one, two = faces[which][p], faces[which][p + pairs]
        low = jnp.where(left, one, pltpu.roll(two, 64, 1))
        high = jnp.where(left, pltpu.roll(one, 64, 1), two)
        return low, high

    groups_of = -(-pairs // 4)
    residue = lane % 8
    edge_of = [
        jnp.logical_or(residue == 2 * r, residue == (2 * r + 7) % 8) for r in range(4)
    ]
    for g in range(groups_of):
        edges = [blank, blank]
        for r in range(4):
            p = 4 * g + r
            if p >= pairs:
                continue
            low, high = packed(0, p)
            send_wide[0, p] = high
            send_wide[1, p] = low
            for way, value in enumerate((high, low)):
                if r:
                    value = pltpu.roll(value, 2 * r, 1)
                edges[way] = jnp.where(edge_of[r], value, edges[way])
        for way in range(2):
            send_edge[way, g] = edges[way]

    pl.semaphore_wait(barrier, count - 1)

    def face_copies(source, target, at, count, first):
        return [
            pltpu.make_async_remote_copy(
                src_ref=source.at[way],
                dst_ref=target.at[way],
                send_sem=face_send_sem.at[first + way],
                recv_sem=face_recv_sem.at[first + way],
                device_id=at(1 if way == 0 else count - 1),
                device_id_type=MESH,
            )
            for way in range(2)
        ]

    wide_copies = face_copies(send_wide, recv_wide, wide_at, wide_count, 2)
    edge_copies = [
        pltpu.make_async_remote_copy(
            src_ref=send_edge.at[way],
            dst_ref=recv_edge.at[way, i],
            send_sem=edge_send_sem.at[way, i],
            recv_sem=edge_recv_sem.at[way, i],
            device_id=corner_at(ways[way], turn),
            device_id_type=MESH,
        )
        for way in range(2)
        for i, turn in enumerate(turns)
    ]
    for copy in wide_copies + edge_copies:
        copy.start()
    for p in range(pairs):
        low, high = packed(1, p)
        send_narrow[0, p] = high
        send_narrow[1, p] = low
    narrow_copies = face_copies(send_narrow, recv_narrow, narrow_at, narrow_count, 0)
    for copy in narrow_copies:
        copy.start()

    for load in loads[3:]:
        load.wait()
    near = [near_ref[0], near_ref[1]]
    whole = [dot(pair[0], first_ref[...])]
    for k in range(2):
        whole.append(
            jnp.concatenate(
                [dot(pair[k + 1][:, :256], near[k]), dot(pair[k + 1][:, 256:], near[k])], axis=1
            )
        )
    raw = curl(whole)
    right = jnp.logical_not(left)
    field = []
    for a in range(3):
        for e in range(radial):
            value = raw[a * radial + e]
            head, tail = value[:, :128], value[:, nodes - 128 :]
            if e > 0:
                last = raw[a * radial + e - 1][:, nodes - 128 :]
                head = head + jnp.where(left, pltpu.roll(last, 64, 1), 0.0)
            if e < radial - 1:
                first = raw[a * radial + e + 1][:, :128]
                tail = tail + jnp.where(right, pltpu.roll(first, 64, 1), 0.0)
            field.append(jnp.concatenate([head, value[:, 128 : nodes - 128], tail], axis=1))
    long_lane = lax.broadcasted_iota(jnp.int32, (snaps, nodes), 1)
    long_line = lax.broadcasted_iota(jnp.int32, (snaps, nodes), 0)
    mass = jnp.ones((snaps, nodes), F32)
    root = jnp.zeros((snaps, nodes), F32)
    for e in range(radial):
        row = jnp.full((snaps, nodes), volume[e], F32)
        size = row
        if e > 0:
            row += jnp.where(long_lane < 64, volume[e - 1], 0.0)
        if e < radial - 1:
            row += jnp.where(long_lane >= nodes - 64, volume[e + 1], 0.0)
        mass = jnp.where(long_line == e, row, mass)
        root = jnp.where(long_line == e, size, root)
    root = jnp.sqrt(root) * root_ref[...]
    field.append(mass)

    edge_low, edge_high = residue == 0, residue == 7

    for copy in narrow_copies:
        copy.wait()
    highs, lows = [], []
    for part_of in range(2):
        for p in range(pairs):
            below, above = recv_narrow[0, p], recv_narrow[1, p]
            if part_of == 0:
                both = jnp.where(left, below, pltpu.roll(above, 64, 1))
            else:
                both = jnp.where(left, pltpu.roll(below, 64, 1), above)
            high, low = split(both)
            highs.append(high)
            lows.append(low)
    stacked = jnp.concatenate(
        [jnp.concatenate(highs, axis=0), jnp.concatenate(lows, axis=0)], axis=1
    )
    extra = dot(stacked, spread_ref[1])
    field = [value + extra[b * snaps : (b + 1) * snaps] for b, value in enumerate(field)]
    inner = jnp.logical_and(long_lane % 8 != 0, long_lane % 8 != 7)
    scale = jnp.where(inner, root / field[fields], 0.0)
    for b in range(fields):
        e = b % radial
        high, low = split(field[b] * scale[e : e + 1, :])
        z_ref[0:snaps, pl.ds(b * nodes, nodes)] = high
        z_ref[snaps : 2 * snaps, pl.ds(b * nodes, nodes)] = low

    def products(both):
        return lax.dot_general(
            both, both, (((1,), (1,)), ((), ())), preferred_element_type=F32
        )

    inside = products(z_ref[...])
    own = [[], []]
    for p in range(pairs):
        below, above = recv_narrow[0, p], recv_narrow[1, p]
        own[0].append(
            send_wide[1, p]
            + jnp.where(edge_low, below, 0.0)
            + jnp.where(edge_high, pltpu.roll(above, 7, 1), 0.0)
        )
        own[1].append(
            send_wide[0, p]
            + jnp.where(edge_high, above, 0.0)
            + jnp.where(edge_low, pltpu.roll(below, 121, 1), 0.0)
        )
    edge_size = jnp.zeros((snaps, 128), F32)
    for e in range(radial):
        edge_size = jnp.where(line == e, jnp.full((snaps, 128), volume[e], F32), edge_size)
    edge_root = jnp.sqrt(edge_size) * edge_root_ref[...]

    for copy in edge_copies + wide_copies:
        copy.wait()

    def arrived(way, p):
        g, r = p // 4, p % 4
        pieces = []
        for slot, places, shift in ((0, edge_low, 121), (len(turns) - 1, edge_high, 7)):
            piece = pltpu.roll(recv_edge[way, slot, g], (shift - 2 * r) % 128, 1)
            pieces.append(jnp.where(places, piece, 0.0))
        return own[way][p] + (recv_wide[way, p] + (pieces[0] + pieces[1]))

    mass_pair, mass_left = fields % pairs, fields < pairs
    ends = [[], []]
    for way in range(2):
        values = [arrived(way, p) for p in range(pairs)]
        mass = values[mass_pair]
        turned = pltpu.roll(mass, 64, 1)
        mass = jnp.where(left, mass, turned) if mass_left else jnp.where(left, turned, mass)
        scale = edge_root / mass
        for p in range(pairs):
            one, two = p % radial, (p + pairs) % radial
            factor = jnp.where(left, scale[one : one + 1, :], scale[two : two + 1, :])
            if p >= fields:
                factor = jnp.zeros_like(factor)
            elif p + pairs >= fields:
                factor = jnp.where(left, factor, 0.0)
            ends[way].append(split(values[p] * factor))
    ends = ends[0] + ends[1]
    both = jnp.concatenate(
        [jnp.concatenate([end[i] for end in ends], axis=1) for i in range(2)], axis=0
    )
    gram_ref[:, : 2 * snaps] = inside + products(both)
    product = gram_ref[...]
    top = product[:snaps]
    gram = top + pltpu.roll(top, 128 - snaps, 1) + product[snaps:]
    gram = jnp.where(lane < snaps, gram, 0.0)
    groups = snaps // 8
    for g in range(groups):
        piece = pltpu.roll(gram[8 * g : 8 * g + 8], 0, 1, stride=snaps, stride_axis=0)
        sums_ref[me, g : g + 1, :] = jnp.sum(piece, axis=0, keepdims=True)

    def sum_copy(step):
        return pltpu.make_async_remote_copy(
            src_ref=sums_ref.at[me],
            dst_ref=sums_ref.at[me],
            send_sem=sum_send_sem,
            recv_sem=sum_recv_sem,
            device_id=device(step),
            device_id_type=MESH,
        )

    each_peer(lambda step: sum_copy(step).start())

    def whole_rows():
        for i in range(2):
            values = []
            for b in range(fields):
                p, two = b % pairs, b >= pairs
                low, high = ends[p][i].astype(F32), ends[pairs + p][i].astype(F32)
                if two:
                    low = pltpu.roll(low, 64, 1)
                else:
                    high = pltpu.roll(high, 64, 1)
                values.append(jnp.where(left, low, high))
            rows = dot(jnp.concatenate(values, axis=0).astype(BF16), spread_ref[0, 0:128, :])
            for b in range(fields):
                at = (pl.ds(i * snaps, snaps), pl.ds(b * nodes, nodes))
                kept = z_ref[at].astype(F32)
                z_ref[at] = (kept + rows[b * snaps : (b + 1) * snaps]).astype(BF16)
        copy = pltpu.make_async_copy(z_ref, z_out, z_sem)
        copy.start()
        return copy

    copy = whole_rows()
    others = sums_ref.at[pl.ds(0, count - 1)]
    pltpu.make_async_copy(others, others, sum_recv_sem).wait()
    pltpu.make_async_copy(others, others, sum_send_sem).wait()
    terms = [sums_ref[i] for i in range(count)]
    while len(terms) > 1:
        terms = [
            terms[i] + terms[i + 1] if i + 1 < len(terms) else terms[i]
            for i in range(0, len(terms), 2)
        ]
    total_ref[...] = terms[0]
    copy.wait()


def basis_kernel(
    row_count, radial, total_ref, z_in, q_ref, r_ref, dmd_ref, z_ref, rows_ref, z_sem
):
    snaps, nodes = q_ref.shape[0], q_ref.shape[3]
    fields = 3 * radial
    load = pltpu.make_async_copy(z_in, z_ref, z_sem)
    load.start()
    lane = lax.broadcasted_iota(jnp.int32, (snaps, 128), 1)
    line = lax.broadcasted_iota(jnp.int32, (snaps, 128), 0)
    lines = []
    for g in range(snaps // 8):
        whole = jnp.broadcast_to(total_ref[g : g + 1, :], (8, 128))
        piece = whole
        for i in range(1, 8):
            piece = jnp.where(line[:8] == i, pltpu.roll(whole, 128 - snaps * i, 1), piece)
        lines.append(piece)
    work = jnp.concatenate(lines, axis=0)
    unit = jnp.logical_and(lane % snaps == line, lane < 4 * snaps)
    work = jnp.where(lane < snaps, work, jnp.where(unit, 1.0, 0.0))
    for k in range(0, snaps - 1, 2):
        row_a, row_b = work[k : k + 1, :], work[k + 1 : k + 2, :]
        col_a, col_b = work[:, k : k + 1], work[:, k + 1 : k + 2]
        inv_a = 1.0 / work[k : k + 1, k : k + 1]
        cross = work[k : k + 1, k + 1 : k + 2]
        ratio = cross * inv_a
        inv_b = 1.0 / (work[k + 1 : k + 2, k + 1 : k + 2] - cross * ratio)
        row_b = row_b - ratio * row_a
        col_b = col_b - ratio * col_a
        after = work - col_a * (inv_a * row_a) - col_b * (inv_b * row_b)
        work = jnp.where(line > k + 1, after, jnp.where(line == k + 1, row_b, work))
    pivot = jnp.sum(jnp.where(lane == line, work, 0.0), axis=1, keepdims=True)
    work = work * (1.0 / jnp.sqrt(pivot))
    norm = math.sqrt(row_count)
    inverse = pltpu.roll(work, 128 - snaps, 1)
    big, small = split(inverse * norm)
    weights = jnp.where(lane < 2 * snaps, big.astype(F32), small.astype(F32))
    weights = weights[:, : 3 * snaps].astype(BF16)
    load.wait()
    basis = dot(weights, jnp.concatenate([z_ref[...], z_ref[0:snaps, :]], axis=0))
    for b in range(fields):
        for j in range(nodes // 128):
            first = b * nodes + 128 * j
            rows_ref[j, pl.ds(b, snaps, stride=fields), :] = basis[:, first : first + 128]
    for s in range(snaps):
        for c in range(3):
            value = [
                rows_ref[j, pl.ds((s * 3 + c) * radial, radial), :] for j in range(nodes // 128)
            ]
            q_ref[s, c] = jnp.concatenate(value, axis=1).astype(BF16)
    upper = jnp.where(jnp.logical_and(lane >= line, lane < snaps), work, 0.0)
    r_ref[...] = upper[:, :snaps] / norm
    moved = jnp.where(lane < snaps - 1, pltpu.roll(upper, 127, 1), 0.0)
    back = jnp.where(lane < snaps - 1, inverse, 0.0)
    operator = lax.dot_general(
        moved,
        back,
        (((1,), (1,)), ((), ())),
        precision=lax.Precision.HIGHEST,
        preferred_element_type=F32,
    )
    dmd_ref[...] = operator[:, : snaps - 1]


def shards(wide_count, narrow_count, velocity, extents):
    snaps, _, _, _, radial, nodes = velocity.shape
    fields = 3 * radial
    pairs = (fields + 2) // 2
    vmem = pl.BlockSpec(memory_space=pltpu.VMEM)
    operands = [
        velocity.reshape(snaps, 3, radial, nodes),
        extents,
        *[jnp.asarray(table) for table in tables()],
    ]
    corners = len({1, narrow_count - 1})
    edge = (-(-pairs // 4), snaps, 128)
    face = pltpu.VMEM((2, pairs, snaps, 128), F32)
    dma = pltpu.SemaphoreType.DMA
    limit = 60 * 1024 * 1024
    hbm = pl.BlockSpec(memory_space=pltpu.HBM)
    rows = jax.ShapeDtypeStruct((2 * snaps, fields * nodes), BF16)
    rows, total = pl.pallas_call(
        functools.partial(kernel, wide_count, narrow_count),
        out_shape=(rows, jax.ShapeDtypeStruct((snaps // 8, 128), F32)),
        in_specs=[hbm] * len(operands),
        out_specs=(hbm, vmem),
        scratch_shapes=[
            (pltpu.SMEM if i == 1 else pltpu.VMEM)(operand.shape, operand.dtype)
            for i, operand in enumerate(operands)
        ]
        + [
            dma((len(operands),)),
            pltpu.VMEM((nodes // 128, fields * snaps, 128), F32),
            pltpu.VMEM((fields * snaps, nodes), BF16),
            pltpu.VMEM((2 * snaps, fields * nodes), BF16),
            dma(()),
            face,
            face,
            face,
            face,
            pltpu.VMEM((2,) + edge, F32),
            pltpu.VMEM((2, corners) + edge, F32),
            pltpu.VMEM((2 * snaps, 128), F32),
            pltpu.VMEM((wide_count * narrow_count, snaps // 8, 128), F32),
            dma((4,)),
            dma((4,)),
            dma((2, corners)),
            dma((2, corners)),
            dma(()),
            dma(()),
        ],
        compiler_params=pltpu.CompilerParams(
            collective_id=0, has_side_effects=True, vmem_limit_bytes=limit
        ),
        cost_estimate=pl.CostEstimate(
            flops=400_000_000, bytes_accessed=3_000_000, transcendentals=10_000
        ),
        name="pipe",
    )(*operands)
    row_count = fields * nodes * wide_count * narrow_count
    q, r, dmd = pl.pallas_call(
        functools.partial(basis_kernel, row_count, radial),
        out_shape=(
            jax.ShapeDtypeStruct((snaps, 3, radial, nodes), BF16),
            jax.ShapeDtypeStruct((snaps, snaps), F32),
            jax.ShapeDtypeStruct((snaps, snaps - 1), F32),
        ),
        in_specs=[vmem, hbm],
        out_specs=(vmem, vmem, vmem),
        scratch_shapes=[
            pltpu.VMEM((2 * snaps, fields * nodes), BF16),
            pltpu.VMEM((nodes // 128, fields * snaps, 128), F32),
            dma(()),
        ],
        compiler_params=pltpu.CompilerParams(vmem_limit_bytes=limit),
        name="basis",
    )(total, rows)
    return q.reshape(velocity.shape), r, dmd


def solution(mesh):
    return jax.shard_map(
        functools.partial(shards, mesh.shape["wide"], mesh.shape["narrow"]),
        mesh=mesh,
        in_specs=(P(None, None, "wide", "narrow", None, None), P(None, "wide", "narrow", None)),
        out_specs=(P(None, None, "wide", "narrow", None, None), P(), P()),
        check_vma=False,
    )
```

```python
import functools
import math

import jax
import jax.numpy as jnp
import ml_dtypes
import numpy as np
from jax import lax
from jax.experimental import pallas as pl
from jax.experimental.pallas import tpu as pltpu
from jax.sharding import PartitionSpec as P

MESH = pl.DeviceIdType.MESH
F32 = jnp.float32
BF16 = jnp.bfloat16


def gll_tables():
    degree = 7
    node_count = 8
    gll_nodes = np.cos(np.pi * np.arange(node_count) / degree)
    legendre = np.zeros((node_count, node_count))
    for sweep_index in range(60):
        previous = gll_nodes.copy()
        legendre[:, 0] = 1.0
        legendre[:, 1] = previous
        for power in range(2, node_count):
            legendre[:, power] = (
                (2 * power - 1) * previous * legendre[:, power - 1]
                - (power - 1) * legendre[:, power - 2]
            ) / power
        gll_nodes = previous - (previous * legendre[:, degree] - legendre[:, degree - 1]) / (
            node_count * legendre[:, degree]
        )
    legendre[:, 0] = 1.0
    legendre[:, 1] = gll_nodes
    for power in range(2, node_count):
        legendre[:, power] = (
            (2 * power - 1) * gll_nodes * legendre[:, power - 1]
            - (power - 1) * legendre[:, power - 2]
        ) / power
    top_poly = legendre[:, degree][::-1]
    weights = (2.0 / (degree * node_count * legendre[:, degree] ** 2))[::-1]
    ordered = gll_nodes[::-1]
    unit_diag = np.eye(node_count)
    spacing = ordered[:, None] - ordered[None, :] + unit_diag
    derivative = top_poly[:, None] / top_poly[None, :] / spacing
    derivative = derivative * (1.0 - unit_diag)
    derivative[0, 0] = -degree * node_count / 4.0
    derivative[-1, -1] = degree * node_count / 4.0
    return (derivative, weights)


def tables():
    derivative, weights = gll_tables()
    d8 = derivative.astype(np.float32).astype(ml_dtypes.bfloat16).astype(np.float32)
    i8, i64 = np.eye(8, dtype=np.float32), np.eye(64, dtype=np.float32)
    full = [
        np.kron(d8, i64).T,
        np.kron(i8, np.kron(d8, i8)).T,
        np.kron(i64, d8).T,
    ]
    node = np.arange(512)
    i2, i3 = (node // 8) % 8, node % 8
    picks = np.concatenate([node[i3 == 0], node[i3 == 7], node[i2 == 0], node[i2 == 7]])
    faces = np.concatenate([table[:, picks] for table in full], axis=0)
    spread = np.zeros((2, 128, 512), np.float32)
    for which in range(2):
        spread[which, np.arange(128), picks[128 * which : 128 * which + 128]] = 1.0
    spread = np.concatenate([spread, spread], axis=1)
    cube = weights[:, None, None] * weights[None, :, None] * weights[None, None, :] * 64.0
    root = np.sqrt(cube).reshape(1, 512).astype(np.float32)
    half = lambda table: table.astype(ml_dtypes.bfloat16)
    return (
        half(full[0]),
        half(np.stack([full[1][:256, :256], full[2][:256, :256]])),
        half(faces),
        half(spread),
        root,
        np.concatenate([root[:, picks[:64]]] * 2, axis=1),
    )


def dot(left, right):
    return jnp.dot(left, right, preferred_element_type=F32)


def split(value):
    high = value.astype(BF16)
    low = (value - high.astype(F32)).astype(BF16)
    return high, low


def kernel(
    wide_count,
    narrow_count,
    vel_in,
    ext_in,
    first_in,
    near_in,
    face_in,
    spread_in,
    root_in,
    edge_root_in,
    z_out,
    total_ref,
    vel_ref,
    ext_ref,
    first_ref,
    near_ref,
    face_ref,
    spread_ref,
    root_ref,
    edge_root_ref,
    load_sem,
    rows_ref,
    vb_ref,
    z_ref,
    z_sem,
    send_narrow,
    recv_narrow,
    send_wide,
    recv_wide,
    send_edge,
    recv_edge,
    gram_ref,
    sums_ref,
    face_send_sem,
    face_recv_sem,
    edge_send_sem,
    edge_recv_sem,
    sum_send_sem,
    sum_recv_sem,
):
    snaps, _, radial, nodes = vel_ref.shape
    fields = 3 * radial
    blocks = fields + 2 - fields % 2
    pairs = blocks // 2
    me_w, me_n = lax.axis_index("wide"), lax.axis_index("narrow")
    wrapped = lambda place, size: jnp.where(place >= size, place - size, place)
    wide_at = lambda step: (wrapped(me_w + step, wide_count), me_n)
    narrow_at = lambda step: (me_w, wrapped(me_n + step, narrow_count))
    turns = sorted({1, narrow_count - 1})
    corner_at = lambda step, turn: (
        wrapped(me_w + step, wide_count),
        wrapped(me_n + turn, narrow_count),
    )
    ways = (1, wide_count - 1)

    loads = [
        pltpu.make_async_copy(source, target, load_sem.at[i])
        for i, (source, target) in enumerate(
            [
                (vel_in, vel_ref),
                (ext_in, ext_ref),
                (face_in, face_ref),
                (first_in, first_ref),
                (near_in, near_ref),
                (spread_in, spread_ref),
                (root_in, root_ref),
                (edge_root_in, edge_root_ref),
            ]
        )
    ]
    for load in loads[:3]:
        load.start()

    barrier = pltpu.get_barrier_semaphore()
    count = wide_count * narrow_count
    me = me_w * narrow_count + me_n

    def each_peer(action):
        steps = sorted(range(wide_count), key=lambda step: abs(2 * step - wide_count))
        if count <= 64:
            for step in steps:
                for turn in range(narrow_count):
                    if step or turn:
                        action(corner_at(step, turn))
        else:

            def one_step(step, carry):
                for turn in range(narrow_count):
                    action(corner_at(step, turn))
                return carry

            lax.fori_loop(1, wide_count, one_step, 0)
            for turn in range(1, narrow_count):
                action(narrow_at(turn))

    each_peer(
        lambda peer: pl.semaphore_signal(barrier, inc=1, device_id=peer, device_id_type=MESH)
    )
    loads[0].wait()
    for s in range(snaps):
        for c in range(3):
            value = vel_ref[s, c].astype(F32)
            for j in range(nodes // 128):
                rows_ref[j, pl.ds((s * 3 + c) * radial, radial), :] = value[
                    :, 128 * j : 128 * j + 128
                ]
    for b in range(fields):
        for j in range(nodes // 128):
            vb_ref[pl.ds(b * snaps, snaps), pl.ds(128 * j, 128)] = rows_ref[
                j, pl.ds(b, snaps, stride=fields), :
            ].astype(BF16)
    gram_ref[...] = jnp.zeros_like(gram_ref)
    part = radial * snaps
    comp = lambda c: vb_ref[pl.ds(c * part, part), :]
    pair = [
        jnp.concatenate([comp((k + 1) % 3), comp((k + 2) % 3)], axis=0) for k in range(3)
    ]

    loads[1].wait()
    extent = [[ext_ref[k, 0, 0, e] for e in range(radial)] for k in range(3)]
    volume = [extent[0][e] * extent[1][e] * extent[2][e] for e in range(radial)]

    def curl(grads):
        out = []
        for a in range(3):
            b, c = (a + 1) % 3, (a + 2) % 3
            for e in range(radial):
                one = grads[b][e * snaps : (e + 1) * snaps]
                two = grads[c][part + e * snaps : part + (e + 1) * snaps]
                lead = 2.0 * extent[a][e]
                out.append((lead * extent[c][e]) * one - (lead * extent[b][e]) * two)
        return out

    loads[2].wait()
    for load in loads[3:]:
        load.start()
    grads = [dot(pair[k], face_ref[pl.ds(k * nodes, nodes), :]) for k in range(3)]
    raw = curl(grads)
    lane = lax.broadcasted_iota(jnp.int32, (snaps, 128), 1)
    place = lane % 64
    at_low, at_high = place < 8, place >= 56
    faces = [[], []]
    for which in range(2):
        cut = [block[:, 128 * which : 128 * which + 128] for block in raw]
        for a in range(3):
            for e in range(radial):
                value = cut[a * radial + e]
                if e > 0:
                    value += jnp.where(at_low, pltpu.roll(cut[a * radial + e - 1], 72, 1), 0.0)
                if e < radial - 1:
                    value += jnp.where(at_high, pltpu.roll(cut[a * radial + e + 1], 56, 1), 0.0)
                faces[which].append(value)
    line = lax.broadcasted_iota(jnp.int32, (snaps, 128), 0)
    mass = jnp.zeros((snaps, 128), F32)
    for e in range(radial):
        row = jnp.full((snaps, 128), volume[e], F32)
        if e > 0:
            row += jnp.where(at_low, volume[e - 1], 0.0)
        if e < radial - 1:
            row += jnp.where(at_high, volume[e + 1], 0.0)
        mass = jnp.where(line == e, row, mass)
    blank = jnp.zeros((snaps, 128), F32)
    for which in range(2):
        faces[which].append(mass)
        while len(faces[which]) < blocks:
            faces[which].append(blank)
    left = lane < 64

    def packed(which, p):
        one, two = faces[which][p], faces[which][p + pairs]
        low = jnp.where(left, one, pltpu.roll(two, 64, 1))
        high = jnp.where(left, pltpu.roll(one, 64, 1), two)
        return low, high

    groups_of = -(-pairs // 4)
    residue = lane % 8
    edge_of = [
        jnp.logical_or(residue == 2 * r, residue == (2 * r + 7) % 8) for r in range(4)
    ]
    for g in range(groups_of):
        edges = [blank, blank]
        for r in range(4):
            p = 4 * g + r
            if p >= pairs:
                continue
            low, high = packed(0, p)
            send_wide[0, p] = high
            send_wide[1, p] = low
            for way, value in enumerate((high, low)):
                if r:
                    value = pltpu.roll(value, 2 * r, 1)
                edges[way] = jnp.where(edge_of[r], value, edges[way])
        for way in range(2):
            send_edge[way, g] = edges[way]

    pl.semaphore_wait(barrier, count - 1)

    def face_copies(source, target, at, count, first):
        return [
            pltpu.make_async_remote_copy(
                src_ref=source.at[way],
                dst_ref=target.at[way],
                send_sem=face_send_sem.at[first + way],
                recv_sem=face_recv_sem.at[first + way],
                device_id=at(1 if way == 0 else count - 1),
                device_id_type=MESH,
            )
            for way in range(2)
        ]

    wide_copies = face_copies(send_wide, recv_wide, wide_at, wide_count, 2)
    edge_copies = [
        pltpu.make_async_remote_copy(
            src_ref=send_edge.at[way],
            dst_ref=recv_edge.at[way, i],
            send_sem=edge_send_sem.at[way, i],
            recv_sem=edge_recv_sem.at[way, i],
            device_id=corner_at(ways[way], turn),
            device_id_type=MESH,
        )
        for way in range(2)
        for i, turn in enumerate(turns)
    ]
    for copy in wide_copies + edge_copies:
        copy.start()
    for p in range(pairs):
        low, high = packed(1, p)
        send_narrow[0, p] = high
        send_narrow[1, p] = low
    narrow_copies = face_copies(send_narrow, recv_narrow, narrow_at, narrow_count, 0)
    for copy in narrow_copies:
        copy.start()

    for load in loads[3:]:
        load.wait()
    near = [near_ref[0], near_ref[1]]
    whole = [dot(pair[0], first_ref[...])]
    for k in range(2):
        whole.append(
            jnp.concatenate(
                [dot(pair[k + 1][:, :256], near[k]), dot(pair[k + 1][:, 256:], near[k])], axis=1
            )
        )
    raw = curl(whole)
    right = jnp.logical_not(left)
    field = []
    for a in range(3):
        for e in range(radial):
            value = raw[a * radial + e]
            head, tail = value[:, :128], value[:, nodes - 128 :]
            if e > 0:
                last = raw[a * radial + e - 1][:, nodes - 128 :]
                head = head + jnp.where(left, pltpu.roll(last, 64, 1), 0.0)
            if e < radial - 1:
                first = raw[a * radial + e + 1][:, :128]
                tail = tail + jnp.where(right, pltpu.roll(first, 64, 1), 0.0)
            field.append(jnp.concatenate([head, value[:, 128 : nodes - 128], tail], axis=1))
    long_lane = lax.broadcasted_iota(jnp.int32, (snaps, nodes), 1)
    long_line = lax.broadcasted_iota(jnp.int32, (snaps, nodes), 0)
    mass = jnp.ones((snaps, nodes), F32)
    root = jnp.zeros((snaps, nodes), F32)
    for e in range(radial):
        row = jnp.full((snaps, nodes), volume[e], F32)
        size = row
        if e > 0:
            row += jnp.where(long_lane < 64, volume[e - 1], 0.0)
        if e < radial - 1:
            row += jnp.where(long_lane >= nodes - 64, volume[e + 1], 0.0)
        mass = jnp.where(long_line == e, row, mass)
        root = jnp.where(long_line == e, size, root)
    root = jnp.sqrt(root) * root_ref[...]
    field.append(mass)

    edge_low, edge_high = residue == 0, residue == 7

    for copy in narrow_copies:
        copy.wait()
    highs, lows = [], []
    for part_of in range(2):
        for p in range(pairs):
            below, above = recv_narrow[0, p], recv_narrow[1, p]
            if part_of == 0:
                both = jnp.where(left, below, pltpu.roll(above, 64, 1))
            else:
                both = jnp.where(left, pltpu.roll(below, 64, 1), above)
            high, low = split(both)
            highs.append(high)
            lows.append(low)
    stacked = jnp.concatenate(
        [jnp.concatenate(highs, axis=0), jnp.concatenate(lows, axis=0)], axis=1
    )
    extra = dot(stacked, spread_ref[1])
    field = [value + extra[b * snaps : (b + 1) * snaps] for b, value in enumerate(field)]
    inner = jnp.logical_and(long_lane % 8 != 0, long_lane % 8 != 7)
    scale = jnp.where(inner, root / field[fields], 0.0)
    for b in range(fields):
        e = b % radial
        high, low = split(field[b] * scale[e : e + 1, :])
        z_ref[0:snaps, pl.ds(b * nodes, nodes)] = high
        z_ref[snaps : 2 * snaps, pl.ds(b * nodes, nodes)] = low

    def products(both):
        return lax.dot_general(
            both, both, (((1,), (1,)), ((), ())), preferred_element_type=F32
        )

    inside = products(z_ref[...])
    own = [[], []]
    for p in range(pairs):
        below, above = recv_narrow[0, p], recv_narrow[1, p]
        own[0].append(
            send_wide[1, p]
            + jnp.where(edge_low, below, 0.0)
            + jnp.where(edge_high, pltpu.roll(above, 7, 1), 0.0)
        )
        own[1].append(
            send_wide[0, p]
            + jnp.where(edge_high, above, 0.0)
            + jnp.where(edge_low, pltpu.roll(below, 121, 1), 0.0)
        )
    edge_size = jnp.zeros((snaps, 128), F32)
    for e in range(radial):
        edge_size = jnp.where(line == e, jnp.full((snaps, 128), volume[e], F32), edge_size)
    edge_root = jnp.sqrt(edge_size) * edge_root_ref[...]

    for copy in edge_copies + wide_copies:
        copy.wait()

    def arrived(way, p):
        g, r = p // 4, p % 4
        pieces = []
        for slot, places, shift in ((0, edge_low, 121), (len(turns) - 1, edge_high, 7)):
            piece = pltpu.roll(recv_edge[way, slot, g], (shift - 2 * r) % 128, 1)
            pieces.append(jnp.where(places, piece, 0.0))
        return own[way][p] + (recv_wide[way, p] + (pieces[0] + pieces[1]))

    mass_pair, mass_left = fields % pairs, fields < pairs
    ends = [[], []]
    for way in range(2):
        values = [arrived(way, p) for p in range(pairs)]
        mass = values[mass_pair]
        turned = pltpu.roll(mass, 64, 1)
        mass = jnp.where(left, mass, turned) if mass_left else jnp.where(left, turned, mass)
        scale = edge_root / mass
        for p in range(pairs):
            one, two = p % radial, (p + pairs) % radial
            factor = jnp.where(left, scale[one : one + 1, :], scale[two : two + 1, :])
            if p >= fields:
                factor = jnp.zeros_like(factor)
            elif p + pairs >= fields:
                factor = jnp.where(left, factor, 0.0)
            ends[way].append(split(values[p] * factor))
    ends = ends[0] + ends[1]
    both = jnp.concatenate(
        [jnp.concatenate([end[i] for end in ends], axis=1) for i in range(2)], axis=0
    )
    gram_ref[:, : 2 * snaps] = inside + products(both)
    product = gram_ref[...]
    top = product[:snaps]
    gram = top + pltpu.roll(top, 128 - snaps, 1) + product[snaps:]
    gram = jnp.where(lane < snaps, gram, 0.0)
    groups = snaps // 8
    for g in range(groups):
        piece = pltpu.roll(gram[8 * g : 8 * g + 8], 0, 1, stride=snaps, stride_axis=0)
        sums_ref[me, g : g + 1, :] = jnp.sum(piece, axis=0, keepdims=True)

    def sum_copy(peer):
        return pltpu.make_async_remote_copy(
            src_ref=sums_ref.at[me],
            dst_ref=sums_ref.at[me],
            send_sem=sum_send_sem,
            recv_sem=sum_recv_sem,
            device_id=peer,
            device_id_type=MESH,
        )

    each_peer(lambda peer: sum_copy(peer).start())

    def whole_rows():
        for i in range(2):
            values = []
            for b in range(fields):
                p, two = b % pairs, b >= pairs
                low, high = ends[p][i].astype(F32), ends[pairs + p][i].astype(F32)
                if two:
                    low = pltpu.roll(low, 64, 1)
                else:
                    high = pltpu.roll(high, 64, 1)
                values.append(jnp.where(left, low, high))
            rows = dot(jnp.concatenate(values, axis=0).astype(BF16), spread_ref[0, 0:128, :])
            for b in range(fields):
                at = (pl.ds(i * snaps, snaps), pl.ds(b * nodes, nodes))
                kept = z_ref[at].astype(F32)
                z_ref[at] = (kept + rows[b * snaps : (b + 1) * snaps]).astype(BF16)
        copy = pltpu.make_async_copy(z_ref, z_out, z_sem)
        copy.start()
        return copy

    copy = whole_rows()
    others = sums_ref.at[pl.ds(0, count - 1)]
    pltpu.make_async_copy(others, others, sum_recv_sem).wait()
    pltpu.make_async_copy(others, others, sum_send_sem).wait()
    terms = [sums_ref[i] for i in range(count)]
    while len(terms) > 1:
        terms = [
            terms[i] + terms[i + 1] if i + 1 < len(terms) else terms[i]
            for i in range(0, len(terms), 2)
        ]
    total_ref[...] = terms[0]
    copy.wait()


def basis_kernel(
    row_count, radial, total_ref, z_in, q_ref, r_ref, dmd_ref, z_ref, rows_ref, z_sem
):
    snaps, nodes = q_ref.shape[0], q_ref.shape[3]
    fields = 3 * radial
    load = pltpu.make_async_copy(z_in, z_ref, z_sem)
    load.start()
    lane = lax.broadcasted_iota(jnp.int32, (snaps, 128), 1)
    line = lax.broadcasted_iota(jnp.int32, (snaps, 128), 0)
    lines = []
    for g in range(snaps // 8):
        whole = jnp.broadcast_to(total_ref[g : g + 1, :], (8, 128))
        piece = whole
        for i in range(1, 8):
            piece = jnp.where(line[:8] == i, pltpu.roll(whole, 128 - snaps * i, 1), piece)
        lines.append(piece)
    work = jnp.concatenate(lines, axis=0)
    unit = jnp.logical_and(lane % snaps == line, lane < 4 * snaps)
    work = jnp.where(lane < snaps, work, jnp.where(unit, 1.0, 0.0))
    for k in range(0, snaps - 1, 2):
        row_a, row_b = work[k : k + 1, :], work[k + 1 : k + 2, :]
        col_a, col_b = work[:, k : k + 1], work[:, k + 1 : k + 2]
        inv_a = 1.0 / work[k : k + 1, k : k + 1]
        cross = work[k : k + 1, k + 1 : k + 2]
        ratio = cross * inv_a
        inv_b = 1.0 / (work[k + 1 : k + 2, k + 1 : k + 2] - cross * ratio)
        row_b = row_b - ratio * row_a
        col_b = col_b - ratio * col_a
        after = work - col_a * (inv_a * row_a) - col_b * (inv_b * row_b)
        work = jnp.where(line > k + 1, after, jnp.where(line == k + 1, row_b, work))
    pivot = jnp.sum(jnp.where(lane == line, work, 0.0), axis=1, keepdims=True)
    work = work * (1.0 / jnp.sqrt(pivot))
    norm = math.sqrt(row_count)
    inverse = pltpu.roll(work, 128 - snaps, 1)
    big, small = split(inverse * norm)
    weights = jnp.where(lane < 2 * snaps, big.astype(F32), small.astype(F32))
    weights = weights[:, : 3 * snaps].astype(BF16)
    load.wait()
    basis = dot(weights, jnp.concatenate([z_ref[...], z_ref[0:snaps, :]], axis=0))
    for b in range(fields):
        for j in range(nodes // 128):
            first = b * nodes + 128 * j
            rows_ref[j, pl.ds(b, snaps, stride=fields), :] = basis[:, first : first + 128]
    for s in range(snaps):
        for c in range(3):
            value = [
                rows_ref[j, pl.ds((s * 3 + c) * radial, radial), :] for j in range(nodes // 128)
            ]
            q_ref[s, c] = jnp.concatenate(value, axis=1).astype(BF16)
    upper = jnp.where(jnp.logical_and(lane >= line, lane < snaps), work, 0.0)
    r_ref[...] = upper[:, :snaps] / norm
    moved = jnp.where(lane < snaps - 1, pltpu.roll(upper, 127, 1), 0.0)
    back = jnp.where(lane < snaps - 1, inverse, 0.0)
    operator = lax.dot_general(
        moved,
        back,
        (((1,), (1,)), ((), ())),
        precision=lax.Precision.HIGHEST,
        preferred_element_type=F32,
    )
    dmd_ref[...] = operator[:, : snaps - 1]


def shards(wide_count, narrow_count, velocity, extents):
    snaps, _, _, _, radial, nodes = velocity.shape
    fields = 3 * radial
    pairs = (fields + 2) // 2
    vmem = pl.BlockSpec(memory_space=pltpu.VMEM)
    operands = [
        velocity.reshape(snaps, 3, radial, nodes),
        extents,
        *[jnp.asarray(table) for table in tables()],
    ]
    corners = len({1, narrow_count - 1})
    edge = (-(-pairs // 4), snaps, 128)
    face = pltpu.VMEM((2, pairs, snaps, 128), F32)
    dma = pltpu.SemaphoreType.DMA
    limit = 60 * 1024 * 1024
    hbm = pl.BlockSpec(memory_space=pltpu.HBM)
    rows = jax.ShapeDtypeStruct((2 * snaps, fields * nodes), BF16)
    rows, total = pl.pallas_call(
        functools.partial(kernel, wide_count, narrow_count),
        out_shape=(rows, jax.ShapeDtypeStruct((snaps // 8, 128), F32)),
        in_specs=[hbm] * len(operands),
        out_specs=(hbm, vmem),
        scratch_shapes=[
            (pltpu.SMEM if i == 1 else pltpu.VMEM)(operand.shape, operand.dtype)
            for i, operand in enumerate(operands)
        ]
        + [
            dma((len(operands),)),
            pltpu.VMEM((nodes // 128, fields * snaps, 128), F32),
            pltpu.VMEM((fields * snaps, nodes), BF16),
            pltpu.VMEM((2 * snaps, fields * nodes), BF16),
            dma(()),
            face,
            face,
            face,
            face,
            pltpu.VMEM((2,) + edge, F32),
            pltpu.VMEM((2, corners) + edge, F32),
            pltpu.VMEM((2 * snaps, 128), F32),
            pltpu.VMEM((wide_count * narrow_count, snaps // 8, 128), F32),
            dma((4,)),
            dma((4,)),
            dma((2, corners)),
            dma((2, corners)),
            dma(()),
            dma(()),
        ],
        compiler_params=pltpu.CompilerParams(
            collective_id=0, has_side_effects=True, vmem_limit_bytes=limit
        ),
        cost_estimate=pl.CostEstimate(
            flops=400_000_000, bytes_accessed=3_000_000, transcendentals=10_000
        ),
        name="pipe",
    )(*operands)
    row_count = fields * nodes * wide_count * narrow_count
    q, r, dmd = pl.pallas_call(
        functools.partial(basis_kernel, row_count, radial),
        out_shape=(
            jax.ShapeDtypeStruct((snaps, 3, radial, nodes), BF16),
            jax.ShapeDtypeStruct((snaps, snaps), F32),
            jax.ShapeDtypeStruct((snaps, snaps - 1), F32),
        ),
        in_specs=[vmem, hbm],
        out_specs=(vmem, vmem, vmem),
        scratch_shapes=[
            pltpu.VMEM((2 * snaps, fields * nodes), BF16),
            pltpu.VMEM((nodes // 128, fields * snaps, 128), F32),
            dma(()),
        ],
        compiler_params=pltpu.CompilerParams(vmem_limit_bytes=limit),
        name="basis",
    )(total, rows)
    return q.reshape(velocity.shape), r, dmd


def solution(mesh):
    return jax.shard_map(
        functools.partial(shards, mesh.shape["wide"], mesh.shape["narrow"]),
        mesh=mesh,
        in_specs=(P(None, None, "wide", "narrow", None, None), P(None, "wide", "narrow", None)),
        out_specs=(P(None, None, "wide", "narrow", None, None), P(), P()),
        check_vma=False,
    )
```

```python
import functools
import math

import jax
import jax.numpy as jnp
import ml_dtypes
import numpy as np
from jax import lax
from jax.experimental import pallas as pl
from jax.experimental.pallas import tpu as pltpu
from jax.sharding import PartitionSpec as P

MESH = pl.DeviceIdType.MESH
F32 = jnp.float32
BF16 = jnp.bfloat16


def gll_tables():
    degree = 7
    node_count = 8
    gll_nodes = np.cos(np.pi * np.arange(node_count) / degree)
    legendre = np.zeros((node_count, node_count))
    for sweep_index in range(60):
        previous = gll_nodes.copy()
        legendre[:, 0] = 1.0
        legendre[:, 1] = previous
        for power in range(2, node_count):
            legendre[:, power] = (
                (2 * power - 1) * previous * legendre[:, power - 1]
                - (power - 1) * legendre[:, power - 2]
            ) / power
        gll_nodes = previous - (previous * legendre[:, degree] - legendre[:, degree - 1]) / (
            node_count * legendre[:, degree]
        )
    legendre[:, 0] = 1.0
    legendre[:, 1] = gll_nodes
    for power in range(2, node_count):
        legendre[:, power] = (
            (2 * power - 1) * gll_nodes * legendre[:, power - 1]
            - (power - 1) * legendre[:, power - 2]
        ) / power
    top_poly = legendre[:, degree][::-1]
    weights = (2.0 / (degree * node_count * legendre[:, degree] ** 2))[::-1]
    ordered = gll_nodes[::-1]
    unit_diag = np.eye(node_count)
    spacing = ordered[:, None] - ordered[None, :] + unit_diag
    derivative = top_poly[:, None] / top_poly[None, :] / spacing
    derivative = derivative * (1.0 - unit_diag)
    derivative[0, 0] = -degree * node_count / 4.0
    derivative[-1, -1] = degree * node_count / 4.0
    return (derivative, weights)


def tables():
    derivative, weights = gll_tables()
    d8 = derivative.astype(np.float32).astype(ml_dtypes.bfloat16).astype(np.float32)
    i8, i64 = np.eye(8, dtype=np.float32), np.eye(64, dtype=np.float32)
    full = [
        np.kron(d8, i64).T,
        np.kron(i8, np.kron(d8, i8)).T,
        np.kron(i64, d8).T,
    ]
    node = np.arange(512)
    i2, i3 = (node // 8) % 8, node % 8
    picks = np.concatenate([node[i3 == 0], node[i3 == 7], node[i2 == 0], node[i2 == 7]])
    faces = np.concatenate([table[:, picks] for table in full], axis=0)
    spread = np.zeros((2, 128, 512), np.float32)
    for which in range(2):
        spread[which, np.arange(128), picks[128 * which : 128 * which + 128]] = 1.0
    spread = np.concatenate([spread, spread], axis=1)
    cube = weights[:, None, None] * weights[None, :, None] * weights[None, None, :] * 64.0
    root = np.sqrt(cube).reshape(1, 512).astype(np.float32)
    half = lambda table: table.astype(ml_dtypes.bfloat16)
    return (
        half(full[0]),
        half(np.stack([full[1][:256, :256], full[2][:256, :256]])),
        half(faces),
        half(spread),
        root,
        np.concatenate([root[:, picks[:64]]] * 2, axis=1),
    )


def dot(left, right):
    return jnp.dot(left, right, preferred_element_type=F32)


def split(value):
    high = value.astype(BF16)
    low = (value - high.astype(F32)).astype(BF16)
    return high, low


def kernel(
    wide_count,
    narrow_count,
    vel_in,
    ext_in,
    first_in,
    near_in,
    face_in,
    spread_in,
    root_in,
    edge_root_in,
    z_out,
    total_ref,
    vel_ref,
    ext_ref,
    first_ref,
    near_ref,
    face_ref,
    spread_ref,
    root_ref,
    edge_root_ref,
    load_sem,
    rows_ref,
    vb_ref,
    z_ref,
    z_sem,
    send_narrow,
    recv_narrow,
    send_wide,
    recv_wide,
    send_edge,
    recv_edge,
    sums_ref,
    face_send_sem,
    face_recv_sem,
    edge_send_sem,
    edge_recv_sem,
    sum_send_sem,
    sum_recv_sem,
):
    snaps, _, radial, nodes = vel_ref.shape
    fields = 3 * radial
    blocks = fields + 2 - fields % 2
    pairs = blocks // 2
    me_w, me_n = lax.axis_index("wide"), lax.axis_index("narrow")
    wrapped = lambda place, size: jnp.where(place >= size, place - size, place)
    wide_at = lambda step: (wrapped(me_w + step, wide_count), me_n)
    narrow_at = lambda step: (me_w, wrapped(me_n + step, narrow_count))
    turns = sorted({1, narrow_count - 1})
    corner_at = lambda step, turn: (
        wrapped(me_w + step, wide_count),
        wrapped(me_n + turn, narrow_count),
    )
    ways = (1, wide_count - 1)

    loads = [
        pltpu.make_async_copy(source, target, load_sem.at[i])
        for i, (source, target) in enumerate(
            [
                (vel_in, vel_ref),
                (ext_in, ext_ref),
                (face_in, face_ref),
                (first_in, first_ref),
                (near_in, near_ref),
                (spread_in, spread_ref),
                (root_in, root_ref),
                (edge_root_in, edge_root_ref),
            ]
        )
    ]
    for load in loads[:3]:
        load.start()

    barrier = pltpu.get_barrier_semaphore()
    count = wide_count * narrow_count
    me = me_w * narrow_count + me_n

    def each_peer(action):
        steps = sorted(range(wide_count), key=lambda step: abs(2 * step - wide_count))
        if count <= 64:
            for step in steps:
                for turn in range(narrow_count):
                    if step or turn:
                        action(corner_at(step, turn))
        else:

            def one_step(step, carry):
                for turn in range(narrow_count):
                    action(corner_at(step, turn))
                return carry

            lax.fori_loop(1, wide_count, one_step, 0)
            for turn in range(1, narrow_count):
                action(narrow_at(turn))

    each_peer(
        lambda peer: pl.semaphore_signal(barrier, inc=1, device_id=peer, device_id_type=MESH)
    )
    loads[0].wait()
    for s in range(snaps):
        for c in range(3):
            value = vel_ref[s, c].astype(F32)
            for j in range(nodes // 128):
                rows_ref[j, pl.ds((s * 3 + c) * radial, radial), :] = value[
                    :, 128 * j : 128 * j + 128
                ]
    for b in range(fields):
        for j in range(nodes // 128):
            vb_ref[pl.ds(b * snaps, snaps), pl.ds(128 * j, 128)] = rows_ref[
                j, pl.ds(b, snaps, stride=fields), :
            ].astype(BF16)
    part = radial * snaps
    comp = lambda c: vb_ref[pl.ds(c * part, part), :]
    pair = [
        jnp.concatenate([comp((k + 1) % 3), comp((k + 2) % 3)], axis=0) for k in range(3)
    ]

    loads[1].wait()
    extent = [[ext_ref[k, 0, 0, e] for e in range(radial)] for k in range(3)]
    volume = [extent[0][e] * extent[1][e] * extent[2][e] for e in range(radial)]

    def curl(grads):
        out = []
        for a in range(3):
            b, c = (a + 1) % 3, (a + 2) % 3
            for e in range(radial):
                one = grads[b][e * snaps : (e + 1) * snaps]
                two = grads[c][part + e * snaps : part + (e + 1) * snaps]
                lead = 2.0 * extent[a][e]
                out.append((lead * extent[c][e]) * one - (lead * extent[b][e]) * two)
        return out

    loads[2].wait()
    for load in loads[3:]:
        load.start()
    grads = [dot(pair[k], face_ref[pl.ds(k * nodes, nodes), :]) for k in range(3)]
    raw = curl(grads)
    lane = lax.broadcasted_iota(jnp.int32, (snaps, 128), 1)
    place = lane % 64
    at_low, at_high = place < 8, place >= 56
    faces = [[], []]
    for which in range(2):
        cut = [block[:, 128 * which : 128 * which + 128] for block in raw]
        for a in range(3):
            for e in range(radial):
                value = cut[a * radial + e]
                if e > 0:
                    value += jnp.where(at_low, pltpu.roll(cut[a * radial + e - 1], 72, 1), 0.0)
                if e < radial - 1:
                    value += jnp.where(at_high, pltpu.roll(cut[a * radial + e + 1], 56, 1), 0.0)
                faces[which].append(value)
    line = lax.broadcasted_iota(jnp.int32, (snaps, 128), 0)
    mass = jnp.zeros((snaps, 128), F32)
    for e in range(radial):
        row = jnp.full((snaps, 128), volume[e], F32)
        if e > 0:
            row += jnp.where(at_low, volume[e - 1], 0.0)
        if e < radial - 1:
            row += jnp.where(at_high, volume[e + 1], 0.0)
        mass = jnp.where(line == e, row, mass)
    blank = jnp.zeros((snaps, 128), F32)
    for which in range(2):
        faces[which].append(mass)
        while len(faces[which]) < blocks:
            faces[which].append(blank)
    left = lane < 64

    def packed(which, p):
        one, two = faces[which][p], faces[which][p + pairs]
        low = jnp.where(left, one, pltpu.roll(two, 64, 1))
        high = jnp.where(left, pltpu.roll(one, 64, 1), two)
        return low, high

    groups_of = -(-pairs // 4)
    residue = lane % 8
    edge_of = [
        jnp.logical_or(residue == 2 * r, residue == (2 * r + 7) % 8) for r in range(4)
    ]
    for g in range(groups_of):
        edges = [blank, blank]
        for r in range(4):
            p = 4 * g + r
            if p >= pairs:
                continue
            low, high = packed(0, p)
            send_wide[0, p] = high
            send_wide[1, p] = low
            for way, value in enumerate((high, low)):
                if r:
                    value = pltpu.roll(value, 2 * r, 1)
                edges[way] = jnp.where(edge_of[r], value, edges[way])
        for way in range(2):
            send_edge[way, g] = edges[way]

    pl.semaphore_wait(barrier, count - 1)

    def face_copies(source, target, at, count, first):
        return [
            pltpu.make_async_remote_copy(
                src_ref=source.at[way],
                dst_ref=target.at[way],
                send_sem=face_send_sem.at[first + way],
                recv_sem=face_recv_sem.at[first + way],
                device_id=at(1 if way == 0 else count - 1),
                device_id_type=MESH,
            )
            for way in range(2)
        ]

    wide_copies = face_copies(send_wide, recv_wide, wide_at, wide_count, 2)
    edge_copies = [
        pltpu.make_async_remote_copy(
            src_ref=send_edge.at[way],
            dst_ref=recv_edge.at[way, i],
            send_sem=edge_send_sem.at[way, i],
            recv_sem=edge_recv_sem.at[way, i],
            device_id=corner_at(ways[way], turn),
            device_id_type=MESH,
        )
        for way in range(2)
        for i, turn in enumerate(turns)
    ]
    for copy in wide_copies + edge_copies:
        copy.start()
    for p in range(pairs):
        low, high = packed(1, p)
        send_narrow[0, p] = high
        send_narrow[1, p] = low
    narrow_copies = face_copies(send_narrow, recv_narrow, narrow_at, narrow_count, 0)
    for copy in narrow_copies:
        copy.start()

    for load in loads[3:]:
        load.wait()
    near = [near_ref[0], near_ref[1]]
    whole = [dot(pair[0], first_ref[...])]
    for k in range(2):
        whole.append(
            jnp.concatenate(
                [dot(pair[k + 1][:, :256], near[k]), dot(pair[k + 1][:, 256:], near[k])], axis=1
            )
        )
    raw = curl(whole)
    right = jnp.logical_not(left)
    field = []
    for a in range(3):
        for e in range(radial):
            value = raw[a * radial + e]
            head, tail = value[:, :128], value[:, nodes - 128 :]
            if e > 0:
                last = raw[a * radial + e - 1][:, nodes - 128 :]
                head = head + jnp.where(left, pltpu.roll(last, 64, 1), 0.0)
            if e < radial - 1:
                first = raw[a * radial + e + 1][:, :128]
                tail = tail + jnp.where(right, pltpu.roll(first, 64, 1), 0.0)
            field.append(jnp.concatenate([head, value[:, 128 : nodes - 128], tail], axis=1))
    long_lane = lax.broadcasted_iota(jnp.int32, (snaps, nodes), 1)
    long_line = lax.broadcasted_iota(jnp.int32, (snaps, nodes), 0)
    mass = jnp.ones((snaps, nodes), F32)
    root = jnp.zeros((snaps, nodes), F32)
    for e in range(radial):
        row = jnp.full((snaps, nodes), volume[e], F32)
        size = row
        if e > 0:
            row += jnp.where(long_lane < 64, volume[e - 1], 0.0)
        if e < radial - 1:
            row += jnp.where(long_lane >= nodes - 64, volume[e + 1], 0.0)
        mass = jnp.where(long_line == e, row, mass)
        root = jnp.where(long_line == e, size, root)
    root = jnp.sqrt(root) * root_ref[...]
    field.append(mass)

    edge_low, edge_high = residue == 0, residue == 7

    for copy in narrow_copies:
        copy.wait()
    highs, lows = [], []
    for part_of in range(2):
        for p in range(pairs):
            below, above = recv_narrow[0, p], recv_narrow[1, p]
            if part_of == 0:
                both = jnp.where(left, below, pltpu.roll(above, 64, 1))
            else:
                both = jnp.where(left, pltpu.roll(below, 64, 1), above)
            high, low = split(both)
            highs.append(high)
            lows.append(low)
    stacked = jnp.concatenate(
        [jnp.concatenate(highs, axis=0), jnp.concatenate(lows, axis=0)], axis=1
    )
    extra = dot(stacked, spread_ref[1])
    field = [value + extra[b * snaps : (b + 1) * snaps] for b, value in enumerate(field)]
    inner = jnp.logical_and(long_lane % 8 != 0, long_lane % 8 != 7)
    scale = jnp.where(inner, root / field[fields], 0.0)
    for b in range(fields):
        e = b % radial
        high, low = split(field[b] * scale[e : e + 1, :])
        z_ref[b, 0:snaps, :] = high
        z_ref[b, snaps : 2 * snaps, :] = low

    def products(chunks):
        size = 2 * snaps
        stack = jnp.concatenate(chunks, axis=0)
        grid = lax.dot_general(
            stack, stack, (((1,), (1,)), ((), ())), preferred_element_type=F32
        )
        out = None
        for i in range(len(chunks)):
            first = i * size // 128 * 128
            block = grid[i * size : (i + 1) * size, first : min(first + 128, grid.shape[1])]
            if block.shape[1] < 128:
                rest = jnp.zeros((size, 128 - block.shape[1]), F32)
                block = jnp.concatenate([block, rest], axis=1)
            if i * size > first:
                block = pltpu.roll(block, 128 - (i * size - first), 1)
            out = block if out is None else out + block
        return out

    at_once = max(1, 8 * fields // 48)
    while fields % at_once:
        at_once -= 1
    inside = products(
        [
            jnp.concatenate([z_ref[b] for b in range(first, first + at_once)], axis=1)
            for first in range(0, fields, at_once)
        ]
    )
    own = [[], []]
    for p in range(pairs):
        below, above = recv_narrow[0, p], recv_narrow[1, p]
        own[0].append(
            send_wide[1, p]
            + jnp.where(edge_low, below, 0.0)
            + jnp.where(edge_high, pltpu.roll(above, 7, 1), 0.0)
        )
        own[1].append(
            send_wide[0, p]
            + jnp.where(edge_high, above, 0.0)
            + jnp.where(edge_low, pltpu.roll(below, 121, 1), 0.0)
        )
    edge_size = jnp.zeros((snaps, 128), F32)
    for e in range(radial):
        edge_size = jnp.where(line == e, jnp.full((snaps, 128), volume[e], F32), edge_size)
    edge_root = jnp.sqrt(edge_size) * edge_root_ref[...]

    for copy in edge_copies + wide_copies:
        copy.wait()

    def arrived(way, p):
        g, r = p // 4, p % 4
        pieces = []
        for slot, places, shift in ((0, edge_low, 121), (len(turns) - 1, edge_high, 7)):
            piece = pltpu.roll(recv_edge[way, slot, g], (shift - 2 * r) % 128, 1)
            pieces.append(jnp.where(places, piece, 0.0))
        return own[way][p] + (recv_wide[way, p] + (pieces[0] + pieces[1]))

    mass_pair, mass_left = fields % pairs, fields < pairs
    ends = [[], []]
    for way in range(2):
        values = [arrived(way, p) for p in range(pairs)]
        mass = values[mass_pair]
        turned = pltpu.roll(mass, 64, 1)
        mass = jnp.where(left, mass, turned) if mass_left else jnp.where(left, turned, mass)
        scale = edge_root / mass
        for p in range(pairs):
            one, two = p % radial, (p + pairs) % radial
            factor = jnp.where(left, scale[one : one + 1, :], scale[two : two + 1, :])
            if p >= fields:
                factor = jnp.zeros_like(factor)
            elif p + pairs >= fields:
                factor = jnp.where(left, factor, 0.0)
            ends[way].append(split(values[p] * factor))
    ends = ends[0] + ends[1]
    stacks = [jnp.concatenate(end, axis=0) for end in ends]
    product = inside + products(
        [
            jnp.concatenate(stacks[first : first + 2], axis=1)
            for first in range(0, len(stacks), 2)
        ]
    )
    top = product[:snaps]
    gram = top + pltpu.roll(top, 128 - snaps, 1) + product[snaps:]
    gram = jnp.where(lane < snaps, gram, 0.0)
    groups = snaps // 8
    for g in range(groups):
        piece = pltpu.roll(gram[8 * g : 8 * g + 8], 0, 1, stride=snaps, stride_axis=0)
        sums_ref[me, g : g + 1, :] = jnp.sum(piece, axis=0, keepdims=True)

    def sum_copy(peer):
        return pltpu.make_async_remote_copy(
            src_ref=sums_ref.at[me],
            dst_ref=sums_ref.at[me],
            send_sem=sum_send_sem,
            recv_sem=sum_recv_sem,
            device_id=peer,
            device_id_type=MESH,
        )

    each_peer(lambda peer: sum_copy(peer).start())

    def whole_rows():
        for i in range(2):
            values = []
            for b in range(fields):
                p, two = b % pairs, b >= pairs
                low, high = ends[p][i].astype(F32), ends[pairs + p][i].astype(F32)
                if two:
                    low = pltpu.roll(low, 64, 1)
                else:
                    high = pltpu.roll(high, 64, 1)
                values.append(jnp.where(left, low, high))
            rows = dot(jnp.concatenate(values, axis=0).astype(BF16), spread_ref[0, 0:128, :])
            for b in range(fields):
                at = (b, pl.ds(i * snaps, snaps), slice(None))
                kept = z_ref[at].astype(F32)
                z_ref[at] = (kept + rows[b * snaps : (b + 1) * snaps]).astype(BF16)
        copy = pltpu.make_async_copy(z_ref, z_out, z_sem)
        copy.start()
        return copy

    copy = whole_rows()
    others = sums_ref.at[pl.ds(0, count - 1)]
    pltpu.make_async_copy(others, others, sum_recv_sem).wait()
    pltpu.make_async_copy(others, others, sum_send_sem).wait()
    terms = [sums_ref[i] for i in range(count)]
    while len(terms) > 1:
        terms = [
            terms[i] + terms[i + 1] if i + 1 < len(terms) else terms[i]
            for i in range(0, len(terms), 2)
        ]
    total_ref[...] = terms[0]
    copy.wait()


def basis_kernel(
    row_count, radial, total_ref, z_in, q_ref, r_ref, dmd_ref, z_ref, rows_ref, z_sem
):
    snaps, nodes = q_ref.shape[0], q_ref.shape[3]
    fields = 3 * radial
    load = pltpu.make_async_copy(z_in, z_ref, z_sem)
    load.start()
    lane = lax.broadcasted_iota(jnp.int32, (snaps, 128), 1)
    line = lax.broadcasted_iota(jnp.int32, (snaps, 128), 0)
    lines = []
    for g in range(snaps // 8):
        whole = jnp.broadcast_to(total_ref[g : g + 1, :], (8, 128))
        piece = whole
        for i in range(1, 8):
            piece = jnp.where(line[:8] == i, pltpu.roll(whole, 128 - snaps * i, 1), piece)
        lines.append(piece)
    work = jnp.concatenate(lines, axis=0)
    unit = jnp.logical_and(lane % snaps == line, lane < 4 * snaps)
    work = jnp.where(lane < snaps, work, jnp.where(unit, 1.0, 0.0))
    for k in range(0, snaps - 1, 2):
        row_a, row_b = work[k : k + 1, :], work[k + 1 : k + 2, :]
        col_a, col_b = work[:, k : k + 1], work[:, k + 1 : k + 2]
        inv_a = 1.0 / work[k : k + 1, k : k + 1]
        cross = work[k : k + 1, k + 1 : k + 2]
        ratio = cross * inv_a
        inv_b = 1.0 / (work[k + 1 : k + 2, k + 1 : k + 2] - cross * ratio)
        row_b = row_b - ratio * row_a
        col_b = col_b - ratio * col_a
        after = work - col_a * (inv_a * row_a) - col_b * (inv_b * row_b)
        work = jnp.where(line > k + 1, after, jnp.where(line == k + 1, row_b, work))
    pivot = jnp.sum(jnp.where(lane == line, work, 0.0), axis=1, keepdims=True)
    work = work * (1.0 / jnp.sqrt(pivot))
    norm = math.sqrt(row_count)
    inverse = pltpu.roll(work, 128 - snaps, 1)
    big, small = split(inverse * norm)
    weights = jnp.where(lane < 2 * snaps, big.astype(F32), small.astype(F32))
    weights = weights[:, : 3 * snaps].astype(BF16)
    load.wait()
    for b in range(fields):
        basis = dot(weights, jnp.concatenate([z_ref[b], z_ref[b, 0:snaps, :]], axis=0))
        for j in range(nodes // 128):
            rows_ref[j, pl.ds(b, snaps, stride=fields), :] = basis[:, 128 * j : 128 * j + 128]
    for s in range(snaps):
        for c in range(3):
            value = [
                rows_ref[j, pl.ds((s * 3 + c) * radial, radial), :] for j in range(nodes // 128)
            ]
            q_ref[s, c] = jnp.concatenate(value, axis=1).astype(BF16)
    upper = jnp.where(jnp.logical_and(lane >= line, lane < snaps), work, 0.0)
    r_ref[...] = upper[:, :snaps] / norm
    moved = jnp.where(lane < snaps - 1, pltpu.roll(upper, 127, 1), 0.0)
    back = jnp.where(lane < snaps - 1, inverse, 0.0)
    operator = lax.dot_general(
        moved,
        back,
        (((1,), (1,)), ((), ())),
        precision=lax.Precision.HIGHEST,
        preferred_element_type=F32,
    )
    dmd_ref[...] = operator[:, : snaps - 1]


def shards(wide_count, narrow_count, velocity, extents):
    snaps, _, _, _, radial, nodes = velocity.shape
    fields = 3 * radial
    pairs = (fields + 2) // 2
    vmem = pl.BlockSpec(memory_space=pltpu.VMEM)
    operands = [
        velocity.reshape(snaps, 3, radial, nodes),
        extents,
        *[jnp.asarray(table) for table in tables()],
    ]
    corners = len({1, narrow_count - 1})
    edge = (-(-pairs // 4), snaps, 128)
    face = pltpu.VMEM((2, pairs, snaps, 128), F32)
    dma = pltpu.SemaphoreType.DMA
    limit = 60 * 1024 * 1024
    hbm = pl.BlockSpec(memory_space=pltpu.HBM)
    rows = jax.ShapeDtypeStruct((fields, 2 * snaps, nodes), BF16)
    rows, total = pl.pallas_call(
        functools.partial(kernel, wide_count, narrow_count),
        out_shape=(rows, jax.ShapeDtypeStruct((snaps // 8, 128), F32)),
        in_specs=[hbm] * len(operands),
        out_specs=(hbm, vmem),
        scratch_shapes=[
            (pltpu.SMEM if i == 1 else pltpu.VMEM)(operand.shape, operand.dtype)
            for i, operand in enumerate(operands)
        ]
        + [
            dma((len(operands),)),
            pltpu.VMEM((nodes // 128, fields * snaps, 128), F32),
            pltpu.VMEM((fields * snaps, nodes), BF16),
            pltpu.VMEM((fields, 2 * snaps, nodes), BF16),
            dma(()),
            face,
            face,
            face,
            face,
            pltpu.VMEM((2,) + edge, F32),
            pltpu.VMEM((2, corners) + edge, F32),
            pltpu.VMEM((wide_count * narrow_count, snaps // 8, 128), F32),
            dma((4,)),
            dma((4,)),
            dma((2, corners)),
            dma((2, corners)),
            dma(()),
            dma(()),
        ],
        compiler_params=pltpu.CompilerParams(
            collective_id=0, has_side_effects=True, vmem_limit_bytes=limit
        ),
        cost_estimate=pl.CostEstimate(
            flops=400_000_000, bytes_accessed=3_000_000, transcendentals=10_000
        ),
        name="pipe",
    )(*operands)
    row_count = fields * nodes * wide_count * narrow_count
    q, r, dmd = pl.pallas_call(
        functools.partial(basis_kernel, row_count, radial),
        out_shape=(
            jax.ShapeDtypeStruct((snaps, 3, radial, nodes), BF16),
            jax.ShapeDtypeStruct((snaps, snaps), F32),
            jax.ShapeDtypeStruct((snaps, snaps - 1), F32),
        ),
        in_specs=[vmem, hbm],
        out_specs=(vmem, vmem, vmem),
        scratch_shapes=[
            pltpu.VMEM((fields, 2 * snaps, nodes), BF16),
            pltpu.VMEM((nodes // 128, fields * snaps, 128), F32),
            dma(()),
        ],
        compiler_params=pltpu.CompilerParams(vmem_limit_bytes=limit),
        name="basis",
    )(total, rows)
    return q.reshape(velocity.shape), r, dmd


def solution(mesh):
    return jax.shard_map(
        functools.partial(shards, mesh.shape["wide"], mesh.shape["narrow"]),
        mesh=mesh,
        in_specs=(P(None, None, "wide", "narrow", None, None), P(None, "wide", "narrow", None)),
        out_specs=(P(None, None, "wide", "narrow", None, None), P(), P()),
        check_vma=False,
    )
```

```python
import functools
import math

import jax
import jax.numpy as jnp
import ml_dtypes
import numpy as np
from jax import lax
from jax.experimental import pallas as pl
from jax.experimental.pallas import tpu as pltpu
from jax.sharding import PartitionSpec as P

MESH = pl.DeviceIdType.MESH
F32 = jnp.float32
BF16 = jnp.bfloat16


def gll_tables():
    degree = 7
    node_count = 8
    gll_nodes = np.cos(np.pi * np.arange(node_count) / degree)
    legendre = np.zeros((node_count, node_count))
    for sweep_index in range(60):
        previous = gll_nodes.copy()
        legendre[:, 0] = 1.0
        legendre[:, 1] = previous
        for power in range(2, node_count):
            legendre[:, power] = (
                (2 * power - 1) * previous * legendre[:, power - 1]
                - (power - 1) * legendre[:, power - 2]
            ) / power
        gll_nodes = previous - (previous * legendre[:, degree] - legendre[:, degree - 1]) / (
            node_count * legendre[:, degree]
        )
    legendre[:, 0] = 1.0
    legendre[:, 1] = gll_nodes
    for power in range(2, node_count):
        legendre[:, power] = (
            (2 * power - 1) * gll_nodes * legendre[:, power - 1]
            - (power - 1) * legendre[:, power - 2]
        ) / power
    top_poly = legendre[:, degree][::-1]
    weights = (2.0 / (degree * node_count * legendre[:, degree] ** 2))[::-1]
    ordered = gll_nodes[::-1]
    unit_diag = np.eye(node_count)
    spacing = ordered[:, None] - ordered[None, :] + unit_diag
    derivative = top_poly[:, None] / top_poly[None, :] / spacing
    derivative = derivative * (1.0 - unit_diag)
    derivative[0, 0] = -degree * node_count / 4.0
    derivative[-1, -1] = degree * node_count / 4.0
    return (derivative, weights)


def tables():
    derivative, weights = gll_tables()
    d8 = derivative.astype(np.float32).astype(ml_dtypes.bfloat16).astype(np.float32)
    i8, i64 = np.eye(8, dtype=np.float32), np.eye(64, dtype=np.float32)
    full = [
        np.kron(d8, i64).T,
        np.kron(i8, np.kron(d8, i8)).T,
        np.kron(i64, d8).T,
    ]
    node = np.arange(512)
    i2, i3 = (node // 8) % 8, node % 8
    picks = np.concatenate([node[i3 == 0], node[i3 == 7], node[i2 == 0], node[i2 == 7]])
    faces = np.stack(
        [
            np.concatenate([table[:, picks[first : first + 128]] for table in full], axis=0)
            for first in (0, 128)
        ]
    )
    spread = np.zeros((2, 128, 512), np.float32)
    for which in range(2):
        spread[which, np.arange(128), picks[128 * which : 128 * which + 128]] = 1.0
    spread = np.concatenate([spread, spread], axis=1)
    cube = weights[:, None, None] * weights[None, :, None] * weights[None, None, :] * 64.0
    root = np.sqrt(cube).reshape(1, 512).astype(np.float32)
    half = lambda table: table.astype(ml_dtypes.bfloat16)
    return (
        half(full[0]),
        half(np.stack([full[1][:256, :256], full[2][:256, :256]])),
        half(faces),
        half(spread),
        root,
        np.concatenate([root[:, picks[:64]]] * 2, axis=1),
    )


def dot(left, right):
    return jnp.dot(left, right, preferred_element_type=F32)


def split(value):
    high = value.astype(BF16)
    low = (value - high.astype(F32)).astype(BF16)
    return high, low


def kernel(
    wide_count,
    narrow_count,
    vel_in,
    ext_in,
    first_in,
    near_in,
    face_in,
    spread_in,
    root_in,
    edge_root_in,
    z_out,
    total_ref,
    vel_ref,
    ext_ref,
    first_ref,
    near_ref,
    face_ref,
    spread_ref,
    root_ref,
    edge_root_ref,
    load_sem,
    rows_ref,
    vb_ref,
    z_ref,
    z_sem,
    send_narrow,
    recv_narrow,
    send_wide,
    recv_wide,
    send_edge,
    recv_edge,
    sums_ref,
    face_send_sem,
    face_recv_sem,
    edge_send_sem,
    edge_recv_sem,
    sum_send_sem,
    sum_recv_sem,
):
    snaps, _, radial, nodes = vel_ref.shape
    fields = 3 * radial
    blocks = fields + 2 - fields % 2
    pairs = blocks // 2
    me_w, me_n = lax.axis_index("wide"), lax.axis_index("narrow")
    wrapped = lambda place, size: jnp.where(place >= size, place - size, place)
    wide_at = lambda step: (wrapped(me_w + step, wide_count), me_n)
    narrow_at = lambda step: (me_w, wrapped(me_n + step, narrow_count))
    turns = sorted({1, narrow_count - 1})
    corner_at = lambda step, turn: (
        wrapped(me_w + step, wide_count),
        wrapped(me_n + turn, narrow_count),
    )
    ways = (1, wide_count - 1)

    loads = [
        pltpu.make_async_copy(source, target, load_sem.at[i])
        for i, (source, target) in enumerate(
            [
                (vel_in, vel_ref),
                (ext_in, ext_ref),
                (face_in.at[0], face_ref.at[0]),
                (face_in.at[1], face_ref.at[1]),
                (first_in, first_ref),
                (near_in, near_ref),
                (spread_in, spread_ref),
                (root_in, root_ref),
                (edge_root_in, edge_root_ref),
            ]
        )
    ]
    for load in loads[:3]:
        load.start()

    barrier = pltpu.get_barrier_semaphore()
    count = wide_count * narrow_count
    me = me_w * narrow_count + me_n

    def each_peer(action):
        steps = sorted(range(wide_count), key=lambda step: abs(2 * step - wide_count))
        if count <= 64:
            for step in steps:
                for turn in range(narrow_count):
                    if step or turn:
                        action(corner_at(step, turn))
        else:

            def one_step(step, carry):
                for turn in range(narrow_count):
                    action(corner_at(step, turn))
                return carry

            lax.fori_loop(1, wide_count, one_step, 0)
            for turn in range(1, narrow_count):
                action(narrow_at(turn))

    each_peer(
        lambda peer: pl.semaphore_signal(barrier, inc=1, device_id=peer, device_id_type=MESH)
    )
    loads[0].wait()
    for s in range(snaps):
        for c in range(3):
            value = vel_ref[s, c].astype(F32)
            for j in range(nodes // 128):
                rows_ref[j, pl.ds((s * 3 + c) * radial, radial), :] = value[
                    :, 128 * j : 128 * j + 128
                ]
    for b in range(fields):
        for j in range(nodes // 128):
            vb_ref[pl.ds(b * snaps, snaps), pl.ds(128 * j, 128)] = rows_ref[
                j, pl.ds(b, snaps, stride=fields), :
            ].astype(BF16)
    part = radial * snaps
    comp = lambda c: vb_ref[pl.ds(c * part, part), :]
    pair = [
        jnp.concatenate([comp((k + 1) % 3), comp((k + 2) % 3)], axis=0) for k in range(3)
    ]

    loads[1].wait()
    extent = [[ext_ref[k, 0, 0, e] for e in range(radial)] for k in range(3)]
    volume = [extent[0][e] * extent[1][e] * extent[2][e] for e in range(radial)]

    def curl(grads):
        out = []
        for a in range(3):
            b, c = (a + 1) % 3, (a + 2) % 3
            for e in range(radial):
                one = grads[b][e * snaps : (e + 1) * snaps]
                two = grads[c][part + e * snaps : part + (e + 1) * snaps]
                lead = 2.0 * extent[a][e]
                out.append((lead * extent[c][e]) * one - (lead * extent[b][e]) * two)
        return out

    lane = lax.broadcasted_iota(jnp.int32, (snaps, 128), 1)
    place = lane % 64
    at_low, at_high = place < 8, place >= 56
    blank = jnp.zeros((snaps, 128), F32)

    def make_faces(which):
        grads = [dot(pair[k], face_ref[which, pl.ds(k * nodes, nodes), :]) for k in range(3)]
        cut = curl(grads)
        out = []
        for a in range(3):
            for e in range(radial):
                value = cut[a * radial + e]
                if e > 0:
                    value += jnp.where(at_low, pltpu.roll(cut[a * radial + e - 1], 72, 1), 0.0)
                if e < radial - 1:
                    value += jnp.where(at_high, pltpu.roll(cut[a * radial + e + 1], 56, 1), 0.0)
                out.append(value)
        out.append(mass)
        return out + [blank] * (blocks - len(out))

    line = lax.broadcasted_iota(jnp.int32, (snaps, 128), 0)
    mass = jnp.zeros((snaps, 128), F32)
    for e in range(radial):
        row = jnp.full((snaps, 128), volume[e], F32)
        if e > 0:
            row += jnp.where(at_low, volume[e - 1], 0.0)
        if e < radial - 1:
            row += jnp.where(at_high, volume[e + 1], 0.0)
        mass = jnp.where(line == e, row, mass)
    loads[2].wait()
    for load in loads[3:]:
        load.start()
    faces = {0: make_faces(0)}
    left = lane < 64

    def packed(which, p):
        one, two = faces[which][p], faces[which][p + pairs]
        low = jnp.where(left, one, pltpu.roll(two, 64, 1))
        high = jnp.where(left, pltpu.roll(one, 64, 1), two)
        return low, high

    groups_of = -(-pairs // 4)
    residue = lane % 8
    edge_of = [
        jnp.logical_or(residue == 2 * r, residue == (2 * r + 7) % 8) for r in range(4)
    ]
    for g in range(groups_of):
        edges = [blank, blank]
        for r in range(4):
            p = 4 * g + r
            if p >= pairs:
                continue
            low, high = packed(0, p)
            send_wide[0, p] = high
            send_wide[1, p] = low
            for way, value in enumerate((high, low)):
                if r:
                    value = pltpu.roll(value, 2 * r, 1)
                edges[way] = jnp.where(edge_of[r], value, edges[way])
        for way in range(2):
            send_edge[way, g] = edges[way]

    pl.semaphore_wait(barrier, count - 1)

    def face_copies(source, target, at, count, first):
        return [
            pltpu.make_async_remote_copy(
                src_ref=source.at[way],
                dst_ref=target.at[way],
                send_sem=face_send_sem.at[first + way],
                recv_sem=face_recv_sem.at[first + way],
                device_id=at(1 if way == 0 else count - 1),
                device_id_type=MESH,
            )
            for way in range(2)
        ]

    wide_copies = face_copies(send_wide, recv_wide, wide_at, wide_count, 2)
    edge_copies = [
        pltpu.make_async_remote_copy(
            src_ref=send_edge.at[way],
            dst_ref=recv_edge.at[way, i],
            send_sem=edge_send_sem.at[way, i],
            recv_sem=edge_recv_sem.at[way, i],
            device_id=corner_at(ways[way], turn),
            device_id_type=MESH,
        )
        for way in range(2)
        for i, turn in enumerate(turns)
    ]
    for copy in wide_copies + edge_copies:
        copy.start()
    loads[3].wait()
    faces[1] = make_faces(1)
    for p in range(pairs):
        low, high = packed(1, p)
        send_narrow[0, p] = high
        send_narrow[1, p] = low
    narrow_copies = face_copies(send_narrow, recv_narrow, narrow_at, narrow_count, 0)
    for copy in narrow_copies:
        copy.start()

    for load in loads[4:]:
        load.wait()
    near = [near_ref[0], near_ref[1]]
    whole = [dot(pair[0], first_ref[...])]
    for k in range(2):
        whole.append(
            jnp.concatenate(
                [dot(pair[k + 1][:, :256], near[k]), dot(pair[k + 1][:, 256:], near[k])], axis=1
            )
        )
    raw = curl(whole)
    right = jnp.logical_not(left)
    field = []
    for a in range(3):
        for e in range(radial):
            value = raw[a * radial + e]
            head, tail = value[:, :128], value[:, nodes - 128 :]
            if e > 0:
                last = raw[a * radial + e - 1][:, nodes - 128 :]
                head = head + jnp.where(left, pltpu.roll(last, 64, 1), 0.0)
            if e < radial - 1:
                first = raw[a * radial + e + 1][:, :128]
                tail = tail + jnp.where(right, pltpu.roll(first, 64, 1), 0.0)
            field.append(jnp.concatenate([head, value[:, 128 : nodes - 128], tail], axis=1))
    long_lane = lax.broadcasted_iota(jnp.int32, (snaps, nodes), 1)
    long_line = lax.broadcasted_iota(jnp.int32, (snaps, nodes), 0)
    mass = jnp.ones((snaps, nodes), F32)
    root = jnp.zeros((snaps, nodes), F32)
    for e in range(radial):
        row = jnp.full((snaps, nodes), volume[e], F32)
        size = row
        if e > 0:
            row += jnp.where(long_lane < 64, volume[e - 1], 0.0)
        if e < radial - 1:
            row += jnp.where(long_lane >= nodes - 64, volume[e + 1], 0.0)
        mass = jnp.where(long_line == e, row, mass)
        root = jnp.where(long_line == e, size, root)
    root = jnp.sqrt(root) * root_ref[...]
    field.append(mass)

    edge_low, edge_high = residue == 0, residue == 7

    for copy in narrow_copies:
        copy.wait()
    highs, lows = [], []
    for part_of in range(2):
        for p in range(pairs):
            below, above = recv_narrow[0, p], recv_narrow[1, p]
            if part_of == 0:
                both = jnp.where(left, below, pltpu.roll(above, 64, 1))
            else:
                both = jnp.where(left, pltpu.roll(below, 64, 1), above)
            high, low = split(both)
            highs.append(high)
            lows.append(low)
    stacked = jnp.concatenate(
        [jnp.concatenate(highs, axis=0), jnp.concatenate(lows, axis=0)], axis=1
    )
    extra = dot(stacked, spread_ref[1])
    field = [value + extra[b * snaps : (b + 1) * snaps] for b, value in enumerate(field)]
    inner = jnp.logical_and(long_lane % 8 != 0, long_lane % 8 != 7)
    scale = jnp.where(inner, root / field[fields], 0.0)
    for b in range(fields):
        e = b % radial
        high, low = split(field[b] * scale[e : e + 1, :])
        z_ref[b, 0:snaps, :] = high
        z_ref[b, snaps : 2 * snaps, :] = low

    def products(chunks):
        size = 2 * snaps
        stack = jnp.concatenate(chunks, axis=0)
        grid = lax.dot_general(
            stack, stack, (((1,), (1,)), ((), ())), preferred_element_type=F32
        )
        out = None
        for i in range(len(chunks)):
            first = i * size // 128 * 128
            block = grid[i * size : (i + 1) * size, first : min(first + 128, grid.shape[1])]
            if block.shape[1] < 128:
                rest = jnp.zeros((size, 128 - block.shape[1]), F32)
                block = jnp.concatenate([block, rest], axis=1)
            if i * size > first:
                block = pltpu.roll(block, 128 - (i * size - first), 1)
            out = block if out is None else out + block
        return out

    at_once = max(1, 8 * fields // 48)
    while fields % at_once:
        at_once -= 1
    inside = products(
        [
            jnp.concatenate([z_ref[b] for b in range(first, first + at_once)], axis=1)
            for first in range(0, fields, at_once)
        ]
    )
    own = [[], []]
    for p in range(pairs):
        below, above = recv_narrow[0, p], recv_narrow[1, p]
        own[0].append(
            send_wide[1, p]
            + jnp.where(edge_low, below, 0.0)
            + jnp.where(edge_high, pltpu.roll(above, 7, 1), 0.0)
        )
        own[1].append(
            send_wide[0, p]
            + jnp.where(edge_high, above, 0.0)
            + jnp.where(edge_low, pltpu.roll(below, 121, 1), 0.0)
        )
    edge_size = jnp.zeros((snaps, 128), F32)
    for e in range(radial):
        edge_size = jnp.where(line == e, jnp.full((snaps, 128), volume[e], F32), edge_size)
    edge_root = jnp.sqrt(edge_size) * edge_root_ref[...]

    for copy in edge_copies + wide_copies:
        copy.wait()

    def arrived(way, p):
        g, r = p // 4, p % 4
        pieces = []
        for slot, places, shift in ((0, edge_low, 121), (len(turns) - 1, edge_high, 7)):
            piece = pltpu.roll(recv_edge[way, slot, g], (shift - 2 * r) % 128, 1)
            pieces.append(jnp.where(places, piece, 0.0))
        return own[way][p] + (recv_wide[way, p] + (pieces[0] + pieces[1]))

    mass_pair, mass_left = fields % pairs, fields < pairs
    ends = [[], []]
    for way in range(2):
        values = [arrived(way, p) for p in range(pairs)]
        mass = values[mass_pair]
        turned = pltpu.roll(mass, 64, 1)
        mass = jnp.where(left, mass, turned) if mass_left else jnp.where(left, turned, mass)
        scale = edge_root / mass
        for p in range(pairs):
            one, two = p % radial, (p + pairs) % radial
            factor = jnp.where(left, scale[one : one + 1, :], scale[two : two + 1, :])
            if p >= fields:
                factor = jnp.zeros_like(factor)
            elif p + pairs >= fields:
                factor = jnp.where(left, factor, 0.0)
            ends[way].append(split(values[p] * factor))
    ends = ends[0] + ends[1]
    stacks = [jnp.concatenate(end, axis=0) for end in ends]
    product = inside + products(
        [
            jnp.concatenate(stacks[first : first + 2], axis=1)
            for first in range(0, len(stacks), 2)
        ]
    )
    top = product[:snaps]
    gram = top + pltpu.roll(top, 128 - snaps, 1) + product[snaps:]
    gram = jnp.where(lane < snaps, gram, 0.0)
    groups = snaps // 8
    for g in range(groups):
        piece = pltpu.roll(gram[8 * g : 8 * g + 8], 0, 1, stride=snaps, stride_axis=0)
        sums_ref[me, g : g + 1, :] = jnp.sum(piece, axis=0, keepdims=True)

    def sum_copy(peer):
        return pltpu.make_async_remote_copy(
            src_ref=sums_ref.at[me],
            dst_ref=sums_ref.at[me],
            send_sem=sum_send_sem,
            recv_sem=sum_recv_sem,
            device_id=peer,
            device_id_type=MESH,
        )

    each_peer(lambda peer: sum_copy(peer).start())

    def whole_rows():
        for i in range(2):
            values = []
            for b in range(fields):
                p, two = b % pairs, b >= pairs
                low, high = ends[p][i].astype(F32), ends[pairs + p][i].astype(F32)
                if two:
                    low = pltpu.roll(low, 64, 1)
                else:
                    high = pltpu.roll(high, 64, 1)
                values.append(jnp.where(left, low, high))
            rows = dot(jnp.concatenate(values, axis=0).astype(BF16), spread_ref[0, 0:128, :])
            for b in range(fields):
                at = (b, pl.ds(i * snaps, snaps), slice(None))
                kept = z_ref[at].astype(F32)
                z_ref[at] = (kept + rows[b * snaps : (b + 1) * snaps]).astype(BF16)
        copy = pltpu.make_async_copy(z_ref, z_out, z_sem)
        copy.start()
        return copy

    copy = whole_rows()
    others = sums_ref.at[pl.ds(0, count - 1)]
    pltpu.make_async_copy(others, others, sum_recv_sem).wait()
    pltpu.make_async_copy(others, others, sum_send_sem).wait()
    terms = [sums_ref[i] for i in range(count)]
    while len(terms) > 1:
        terms = [
            terms[i] + terms[i + 1] if i + 1 < len(terms) else terms[i]
            for i in range(0, len(terms), 2)
        ]
    total_ref[...] = terms[0]
    copy.wait()


def basis_kernel(
    row_count, radial, total_ref, z_in, q_ref, r_ref, dmd_ref, z_ref, z_sem
):
    snaps, nodes = q_ref.shape[0], q_ref.shape[3]
    fields = 3 * radial
    load = pltpu.make_async_copy(z_in, z_ref, z_sem)
    load.start()
    lane = lax.broadcasted_iota(jnp.int32, (snaps, 128), 1)
    line = lax.broadcasted_iota(jnp.int32, (snaps, 128), 0)
    lines = []
    for g in range(snaps // 8):
        whole = jnp.broadcast_to(total_ref[g : g + 1, :], (8, 128))
        piece = whole
        for i in range(1, 8):
            piece = jnp.where(line[:8] == i, pltpu.roll(whole, 128 - snaps * i, 1), piece)
        lines.append(piece)
    work = jnp.concatenate(lines, axis=0)
    unit = jnp.logical_and(lane % snaps == line, lane < 4 * snaps)
    work = jnp.where(lane < snaps, work, jnp.where(unit, 1.0, 0.0))
    for k in range(0, snaps - 1, 2):
        row_a, row_b = work[k : k + 1, :], work[k + 1 : k + 2, :]
        col_a, col_b = work[:, k : k + 1], work[:, k + 1 : k + 2]
        inv_a = 1.0 / work[k : k + 1, k : k + 1]
        cross = work[k : k + 1, k + 1 : k + 2]
        ratio = cross * inv_a
        inv_b = 1.0 / (work[k + 1 : k + 2, k + 1 : k + 2] - cross * ratio)
        row_b = row_b - ratio * row_a
        col_b = col_b - ratio * col_a
        after = work - col_a * (inv_a * row_a) - col_b * (inv_b * row_b)
        work = jnp.where(line > k + 1, after, jnp.where(line == k + 1, row_b, work))
    pivot = jnp.sum(jnp.where(lane == line, work, 0.0), axis=1, keepdims=True)
    work = work * (1.0 / jnp.sqrt(pivot))
    norm = math.sqrt(row_count)
    inverse = pltpu.roll(work, 128 - snaps, 1)
    big, small = split(inverse * norm)
    weights = jnp.where(lane < 2 * snaps, big.astype(F32), small.astype(F32))
    weights = jnp.where(lane < 4 * snaps, weights, 0.0)
    turned = pltpu.roll(weights, 4 * snaps, 1)
    both = jnp.where(lane < 4 * snaps, weights, turned)
    rows = []
    for s in range(snaps):
        rows.append(jnp.broadcast_to(both[s : s + 1, :], (radial, 128)))
    rows = jnp.concatenate(rows, axis=0)
    wide_line = lax.broadcasted_iota(jnp.int32, rows.shape, 0) % radial
    wide_lane = lax.broadcasted_iota(jnp.int32, rows.shape, 1) // (4 * snaps)
    per = 128 // (4 * snaps)
    expanded = jnp.concatenate(
        [
            jnp.where(wide_line == wide_lane + per * i, rows, 0.0).astype(BF16)
            for i in range(radial // per)
        ],
        axis=1,
    )
    load.wait()
    for c in range(3):
        held = [z_ref[c * radial + e] for e in range(radial)]
        basis = dot(expanded, jnp.concatenate([h for h in held for _ in range(2)], axis=0))
        for s in range(snaps):
            q_ref[s, c] = basis[s * radial : (s + 1) * radial, :].astype(BF16)
    upper = jnp.where(jnp.logical_and(lane >= line, lane < snaps), work, 0.0)
    r_ref[...] = upper[:, :snaps] / norm
    moved = jnp.where(lane < snaps - 1, pltpu.roll(upper, 127, 1), 0.0)
    back = jnp.where(lane < snaps - 1, inverse, 0.0)
    operator = lax.dot_general(
        moved,
        back,
        (((1,), (1,)), ((), ())),
        precision=lax.Precision.HIGHEST,
        preferred_element_type=F32,
    )
    dmd_ref[...] = operator[:, : snaps - 1]


def shards(wide_count, narrow_count, velocity, extents):
    snaps, _, _, _, radial, nodes = velocity.shape
    fields = 3 * radial
    pairs = (fields + 2) // 2
    vmem = pl.BlockSpec(memory_space=pltpu.VMEM)
    operands = [
        velocity.reshape(snaps, 3, radial, nodes),
        extents,
        *[jnp.asarray(table) for table in tables()],
    ]
    corners = len({1, narrow_count - 1})
    edge = (-(-pairs // 4), snaps, 128)
    face = pltpu.VMEM((2, pairs, snaps, 128), F32)
    dma = pltpu.SemaphoreType.DMA
    limit = 60 * 1024 * 1024
    hbm = pl.BlockSpec(memory_space=pltpu.HBM)
    rows = jax.ShapeDtypeStruct((fields, 2 * snaps, nodes), BF16)
    rows, total = pl.pallas_call(
        functools.partial(kernel, wide_count, narrow_count),
        out_shape=(rows, jax.ShapeDtypeStruct((snaps // 8, 128), F32)),
        in_specs=[hbm] * len(operands),
        out_specs=(hbm, vmem),
        scratch_shapes=[
            (pltpu.SMEM if i == 1 else pltpu.VMEM)(operand.shape, operand.dtype)
            for i, operand in enumerate(operands)
        ]
        + [
            dma((len(operands) + 1,)),
            pltpu.VMEM((nodes // 128, fields * snaps, 128), F32),
            pltpu.VMEM((fields * snaps, nodes), BF16),
            pltpu.VMEM((fields, 2 * snaps, nodes), BF16),
            dma(()),
            face,
            face,
            face,
            face,
            pltpu.VMEM((2,) + edge, F32),
            pltpu.VMEM((2, corners) + edge, F32),
            pltpu.VMEM((wide_count * narrow_count, snaps // 8, 128), F32),
            dma((4,)),
            dma((4,)),
            dma((2, corners)),
            dma((2, corners)),
            dma(()),
            dma(()),
        ],
        compiler_params=pltpu.CompilerParams(
            collective_id=0, has_side_effects=True, vmem_limit_bytes=limit
        ),
        cost_estimate=pl.CostEstimate(
            flops=400_000_000, bytes_accessed=3_000_000, transcendentals=10_000
        ),
        name="pipe",
    )(*operands)
    row_count = fields * nodes * wide_count * narrow_count
    q, r, dmd = pl.pallas_call(
        functools.partial(basis_kernel, row_count, radial),
        out_shape=(
            jax.ShapeDtypeStruct((snaps, 3, radial, nodes), BF16),
            jax.ShapeDtypeStruct((snaps, snaps), F32),
            jax.ShapeDtypeStruct((snaps, snaps - 1), F32),
        ),
        in_specs=[vmem, hbm],
        out_specs=(vmem, vmem, vmem),
        scratch_shapes=[
            pltpu.VMEM((fields, 2 * snaps, nodes), BF16),
            dma(()),
        ],
        compiler_params=pltpu.CompilerParams(vmem_limit_bytes=limit),
        name="basis",
    )(total, rows)
    return q.reshape(velocity.shape), r, dmd


def solution(mesh):
    return jax.shard_map(
        functools.partial(shards, mesh.shape["wide"], mesh.shape["narrow"]),
        mesh=mesh,
        in_specs=(P(None, None, "wide", "narrow", None, None), P(None, "wide", "narrow", None)),
        out_specs=(P(None, None, "wide", "narrow", None, None), P(), P()),
        check_vma=False,
    )
```

```python
import functools
import math

import jax
import jax.numpy as jnp
import ml_dtypes
import numpy as np
from jax import lax
from jax.experimental import pallas as pl
from jax.experimental.pallas import tpu as pltpu
from jax.sharding import PartitionSpec as P

MESH = pl.DeviceIdType.MESH
F32 = jnp.float32
BF16 = jnp.bfloat16


def gll_tables():
    degree = 7
    node_count = 8
    gll_nodes = np.cos(np.pi * np.arange(node_count) / degree)
    legendre = np.zeros((node_count, node_count))
    for sweep_index in range(60):
        previous = gll_nodes.copy()
        legendre[:, 0] = 1.0
        legendre[:, 1] = previous
        for power in range(2, node_count):
            legendre[:, power] = (
                (2 * power - 1) * previous * legendre[:, power - 1]
                - (power - 1) * legendre[:, power - 2]
            ) / power
        gll_nodes = previous - (previous * legendre[:, degree] - legendre[:, degree - 1]) / (
            node_count * legendre[:, degree]
        )
    legendre[:, 0] = 1.0
    legendre[:, 1] = gll_nodes
    for power in range(2, node_count):
        legendre[:, power] = (
            (2 * power - 1) * gll_nodes * legendre[:, power - 1]
            - (power - 1) * legendre[:, power - 2]
        ) / power
    top_poly = legendre[:, degree][::-1]
    weights = (2.0 / (degree * node_count * legendre[:, degree] ** 2))[::-1]
    ordered = gll_nodes[::-1]
    unit_diag = np.eye(node_count)
    spacing = ordered[:, None] - ordered[None, :] + unit_diag
    derivative = top_poly[:, None] / top_poly[None, :] / spacing
    derivative = derivative * (1.0 - unit_diag)
    derivative[0, 0] = -degree * node_count / 4.0
    derivative[-1, -1] = degree * node_count / 4.0
    return (derivative, weights)


def tables():
    derivative, weights = gll_tables()
    d8 = derivative.astype(np.float32).astype(ml_dtypes.bfloat16).astype(np.float32)
    i8, i64 = np.eye(8, dtype=np.float32), np.eye(64, dtype=np.float32)
    full = [
        np.kron(d8, i64).T,
        np.kron(i8, np.kron(d8, i8)).T,
        np.kron(i64, d8).T,
    ]
    node = np.arange(512)
    i2, i3 = (node // 8) % 8, node % 8
    picks = np.concatenate([node[i3 == 0], node[i3 == 7], node[i2 == 0], node[i2 == 7]])
    faces = np.concatenate([table[:, picks] for table in full], axis=0)
    spread = np.zeros((2, 128, 512), np.float32)
    for which in range(2):
        spread[which, np.arange(128), picks[128 * which : 128 * which + 128]] = 1.0
    spread = np.concatenate([spread, spread], axis=1)
    cube = weights[:, None, None] * weights[None, :, None] * weights[None, None, :] * 64.0
    root = np.sqrt(cube).reshape(1, 512).astype(np.float32)
    half = lambda table: table.astype(ml_dtypes.bfloat16)
    return (
        half(full[0]),
        half(np.stack([full[1][:256, :256], full[2][:256, :256]])),
        half(faces),
        half(spread),
        root,
        np.concatenate([root[:, picks[:64]]] * 2, axis=1),
    )


def dot(left, right):
    return jnp.dot(left, right, preferred_element_type=F32)


def split(value):
    high = value.astype(BF16)
    low = (value - high.astype(F32)).astype(BF16)
    return high, low


def kernel(
    wide_count,
    narrow_count,
    vel_in,
    ext_in,
    first_in,
    near_in,
    face_in,
    spread_in,
    root_in,
    edge_root_in,
    z_out,
    total_ref,
    vel_ref,
    ext_ref,
    first_ref,
    near_ref,
    face_ref,
    spread_ref,
    root_ref,
    edge_root_ref,
    load_sem,
    rows_ref,
    vb_ref,
    z_ref,
    z_sem,
    send_narrow,
    recv_narrow,
    send_wide,
    recv_wide,
    send_edge,
    recv_edge,
    gram_ref,
    sums_ref,
    face_send_sem,
    face_recv_sem,
    edge_send_sem,
    edge_recv_sem,
    sum_send_sem,
    sum_recv_sem,
):
    snaps, _, radial, nodes = vel_ref.shape
    fields = 3 * radial
    blocks = fields + 2 - fields % 2
    pairs = blocks // 2
    me_w, me_n = lax.axis_index("wide"), lax.axis_index("narrow")
    wide_at = lambda step: (lax.rem(me_w + step, wide_count), me_n)
    narrow_at = lambda step: (me_w, lax.rem(me_n + step, narrow_count))

    loads = [
        pltpu.make_async_copy(source, target, load_sem.at[i])
        for i, (source, target) in enumerate(
            [
                (vel_in, vel_ref),
                (ext_in, ext_ref),
                (face_in, face_ref),
                (first_in, first_ref),
                (near_in, near_ref),
                (spread_in, spread_ref),
                (root_in, root_ref),
                (edge_root_in, edge_root_ref),
            ]
        )
    ]
    for load in loads[:3]:
        load.start()

    barrier = pltpu.get_barrier_semaphore()
    count = wide_count * narrow_count
    me = me_w * narrow_count + me_n

    def device(step):
        peer = lax.rem(me + step, count)
        return (peer // narrow_count, lax.rem(peer, narrow_count))

    def each_peer(action):
        if count <= 64:
            for step in range(1, count):
                action(step)
        else:
            lax.fori_loop(1, count, lambda step, carry: (action(step), carry)[1], 0)

    each_peer(
        lambda step: pl.semaphore_signal(
            barrier, inc=1, device_id=device(step), device_id_type=MESH
        )
    )
    turns = sorted({1, narrow_count - 1})
    corner_at = lambda step, turn: (
        lax.rem(me_w + step, wide_count),
        lax.rem(me_n + turn, narrow_count),
    )
    ways = (1, wide_count - 1)
    loads[0].wait()
    for s in range(snaps):
        for c in range(3):
            value = vel_ref[s, c].astype(F32)
            for j in range(nodes // 128):
                rows_ref[j, pl.ds((s * 3 + c) * radial, radial), :] = value[
                    :, 128 * j : 128 * j + 128
                ]
    for b in range(fields):
        for j in range(nodes // 128):
            vb_ref[pl.ds(b * snaps, snaps), pl.ds(128 * j, 128)] = rows_ref[
                j, pl.ds(b, snaps, stride=fields), :
            ].astype(BF16)
    gram_ref[...] = jnp.zeros_like(gram_ref)
    part = radial * snaps
    comp = lambda c: vb_ref[pl.ds(c * part, part), :]
    pair = [
        jnp.concatenate([comp((k + 1) % 3), comp((k + 2) % 3)], axis=0) for k in range(3)
    ]

    loads[1].wait()
    extent = [[ext_ref[k, 0, 0, e] for e in range(radial)] for k in range(3)]
    volume = [extent[0][e] * extent[1][e] * extent[2][e] for e in range(radial)]

    def curl(grads):
        out = []
        for a in range(3):
            b, c = (a + 1) % 3, (a + 2) % 3
            for e in range(radial):
                one = grads[b][e * snaps : (e + 1) * snaps]
                two = grads[c][part + e * snaps : part + (e + 1) * snaps]
                lead = 2.0 * extent[a][e]
                out.append((lead * extent[c][e]) * one - (lead * extent[b][e]) * two)
        return out

    loads[2].wait()
    for load in loads[3:]:
        load.start()
    grads = [dot(pair[k], face_ref[pl.ds(k * nodes, nodes), :]) for k in range(3)]
    raw = curl(grads)
    lane = lax.broadcasted_iota(jnp.int32, (snaps, 128), 1)
    place = lane % 64
    at_low, at_high = place < 8, place >= 56
    faces = [[], []]
    for which in range(2):
        cut = [block[:, 128 * which : 128 * which + 128] for block in raw]
        for a in range(3):
            for e in range(radial):
                value = cut[a * radial + e]
                if e > 0:
                    value += jnp.where(at_low, pltpu.roll(cut[a * radial + e - 1], 72, 1), 0.0)
                if e < radial - 1:
                    value += jnp.where(at_high, pltpu.roll(cut[a * radial + e + 1], 56, 1), 0.0)
                faces[which].append(value)
    line = lax.broadcasted_iota(jnp.int32, (snaps, 128), 0)
    mass = jnp.zeros((snaps, 128), F32)
    for e in range(radial):
        row = jnp.full((snaps, 128), volume[e], F32)
        if e > 0:
            row += jnp.where(at_low, volume[e - 1], 0.0)
        if e < radial - 1:
            row += jnp.where(at_high, volume[e + 1], 0.0)
        mass = jnp.where(line == e, row, mass)
    blank = jnp.zeros((snaps, 128), F32)
    for which in range(2):
        faces[which].append(mass)
        while len(faces[which]) < blocks:
            faces[which].append(blank)
    left = lane < 64

    def packed(which, p):
        one, two = faces[which][p], faces[which][p + pairs]
        low = jnp.where(left, one, pltpu.roll(two, 64, 1))
        high = jnp.where(left, pltpu.roll(one, 64, 1), two)
        return low, high

    groups_of = -(-pairs // 4)
    residue = lane % 8
    edge_of = [
        jnp.logical_or(residue == 2 * r, residue == (2 * r + 7) % 8) for r in range(4)
    ]
    for g in range(groups_of):
        edges = [blank, blank]
        for r in range(4):
            p = 4 * g + r
            if p >= pairs:
                continue
            low, high = packed(0, p)
            send_wide[0, p] = high
            send_wide[1, p] = low
            for way, value in enumerate((high, low)):
                if r:
                    value = pltpu.roll(value, 2 * r, 1)
                edges[way] = jnp.where(edge_of[r], value, edges[way])
        for way in range(2):
            send_edge[way, g] = edges[way]

    pl.semaphore_wait(barrier, count - 1)

    def face_copies(source, target, at, count, first):
        return [
            pltpu.make_async_remote_copy(
                src_ref=source.at[way],
                dst_ref=target.at[way],
                send_sem=face_send_sem.at[first + way],
                recv_sem=face_recv_sem.at[first + way],
                device_id=at(1 if way == 0 else count - 1),
                device_id_type=MESH,
            )
            for way in range(2)
        ]

    wide_copies = face_copies(send_wide, recv_wide, wide_at, wide_count, 2)
    edge_copies = [
        pltpu.make_async_remote_copy(
            src_ref=send_edge.at[way],
            dst_ref=recv_edge.at[way, i],
            send_sem=edge_send_sem.at[way, i],
            recv_sem=edge_recv_sem.at[way, i],
            device_id=corner_at(ways[way], turn),
            device_id_type=MESH,
        )
        for way in range(2)
        for i, turn in enumerate(turns)
    ]
    for copy in wide_copies + edge_copies:
        copy.start()
    for p in range(pairs):
        low, high = packed(1, p)
        send_narrow[0, p] = high
        send_narrow[1, p] = low
    narrow_copies = face_copies(send_narrow, recv_narrow, narrow_at, narrow_count, 0)
    for copy in narrow_copies:
        copy.start()

    for load in loads[3:]:
        load.wait()
    near = [near_ref[0], near_ref[1]]
    whole = [dot(pair[0], first_ref[...])]
    for k in range(2):
        whole.append(
            jnp.concatenate(
                [dot(pair[k + 1][:, :256], near[k]), dot(pair[k + 1][:, 256:], near[k])], axis=1
            )
        )
    raw = curl(whole)
    right = jnp.logical_not(left)
    field = []
    for a in range(3):
        for e in range(radial):
            value = raw[a * radial + e]
            head, tail = value[:, :128], value[:, nodes - 128 :]
            if e > 0:
                last = raw[a * radial + e - 1][:, nodes - 128 :]
                head = head + jnp.where(left, pltpu.roll(last, 64, 1), 0.0)
            if e < radial - 1:
                first = raw[a * radial + e + 1][:, :128]
                tail = tail + jnp.where(right, pltpu.roll(first, 64, 1), 0.0)
            field.append(jnp.concatenate([head, value[:, 128 : nodes - 128], tail], axis=1))
    long_lane = lax.broadcasted_iota(jnp.int32, (snaps, nodes), 1)
    long_line = lax.broadcasted_iota(jnp.int32, (snaps, nodes), 0)
    mass = jnp.ones((snaps, nodes), F32)
    root = jnp.zeros((snaps, nodes), F32)
    for e in range(radial):
        row = jnp.full((snaps, nodes), volume[e], F32)
        size = row
        if e > 0:
            row += jnp.where(long_lane < 64, volume[e - 1], 0.0)
        if e < radial - 1:
            row += jnp.where(long_lane >= nodes - 64, volume[e + 1], 0.0)
        mass = jnp.where(long_line == e, row, mass)
        root = jnp.where(long_line == e, size, root)
    root = jnp.sqrt(root) * root_ref[...]
    field.append(mass)

    edge_low, edge_high = residue == 0, residue == 7

    for copy in narrow_copies:
        copy.wait()
    highs, lows = [], []
    for part_of in range(2):
        for p in range(pairs):
            below, above = recv_narrow[0, p], recv_narrow[1, p]
            if part_of == 0:
                both = jnp.where(left, below, pltpu.roll(above, 64, 1))
            else:
                both = jnp.where(left, pltpu.roll(below, 64, 1), above)
            high, low = split(both)
            highs.append(high)
            lows.append(low)
    stacked = jnp.concatenate(
        [jnp.concatenate(highs, axis=0), jnp.concatenate(lows, axis=0)], axis=1
    )
    extra = dot(stacked, spread_ref[1])
    field = [value + extra[b * snaps : (b + 1) * snaps] for b, value in enumerate(field)]
    inner = jnp.logical_and(long_lane % 8 != 0, long_lane % 8 != 7)
    scale = jnp.where(inner, root / field[fields], 0.0)
    for b in range(fields):
        e = b % radial
        high, low = split(field[b] * scale[e : e + 1, :])
        z_ref[0:snaps, pl.ds(b * nodes, nodes)] = high
        z_ref[snaps : 2 * snaps, pl.ds(b * nodes, nodes)] = low

    def products(both):
        return lax.dot_general(
            both, both, (((1,), (1,)), ((), ())), preferred_element_type=F32
        )

    inside = products(z_ref[...])
    own = [[], []]
    for p in range(pairs):
        below, above = recv_narrow[0, p], recv_narrow[1, p]
        own[0].append(
            send_wide[1, p]
            + jnp.where(edge_low, below, 0.0)
            + jnp.where(edge_high, pltpu.roll(above, 7, 1), 0.0)
        )
        own[1].append(
            send_wide[0, p]
            + jnp.where(edge_high, above, 0.0)
            + jnp.where(edge_low, pltpu.roll(below, 121, 1), 0.0)
        )
    edge_size = jnp.zeros((snaps, 128), F32)
    for e in range(radial):
        edge_size = jnp.where(line == e, jnp.full((snaps, 128), volume[e], F32), edge_size)
    edge_root = jnp.sqrt(edge_size) * edge_root_ref[...]

    for copy in edge_copies + wide_copies:
        copy.wait()

    def arrived(way, p):
        g, r = p // 4, p % 4
        pieces = []
        for slot, places, shift in ((0, edge_low, 121), (len(turns) - 1, edge_high, 7)):
            piece = pltpu.roll(recv_edge[way, slot, g], (shift - 2 * r) % 128, 1)
            pieces.append(jnp.where(places, piece, 0.0))
        return own[way][p] + (recv_wide[way, p] + (pieces[0] + pieces[1]))

    mass_pair, mass_left = fields % pairs, fields < pairs
    ends = [[], []]
    for way in range(2):
        values = [arrived(way, p) for p in range(pairs)]
        mass = values[mass_pair]
        turned = pltpu.roll(mass, 64, 1)
        mass = jnp.where(left, mass, turned) if mass_left else jnp.where(left, turned, mass)
        scale = edge_root / mass
        for p in range(pairs):
            one, two = p % radial, (p + pairs) % radial
            factor = jnp.where(left, scale[one : one + 1, :], scale[two : two + 1, :])
            if p >= fields:
                factor = jnp.zeros_like(factor)
            elif p + pairs >= fields:
                factor = jnp.where(left, factor, 0.0)
            ends[way].append(split(values[p] * factor))
    ends = ends[0] + ends[1]
    both = jnp.concatenate(
        [jnp.concatenate([end[i] for end in ends], axis=1) for i in range(2)], axis=0
    )
    gram_ref[:, : 2 * snaps] = inside + products(both)
    product = gram_ref[...]
    top = product[:snaps]
    gram = top + pltpu.roll(top, 128 - snaps, 1) + product[snaps:]
    gram = jnp.where(lane < snaps, gram, 0.0)
    groups = snaps // 8
    for g in range(groups):
        piece = pltpu.roll(gram[8 * g : 8 * g + 8], 0, 1, stride=snaps, stride_axis=0)
        sums_ref[me, g : g + 1, :] = jnp.sum(piece, axis=0, keepdims=True)

    def sum_copy(step):
        return pltpu.make_async_remote_copy(
            src_ref=sums_ref.at[me],
            dst_ref=sums_ref.at[me],
            send_sem=sum_send_sem,
            recv_sem=sum_recv_sem,
            device_id=device(step),
            device_id_type=MESH,
        )

    each_peer(lambda step: sum_copy(step).start())

    def whole_rows():
        for i in range(2):
            values = []
            for b in range(fields):
                p, two = b % pairs, b >= pairs
                low, high = ends[p][i].astype(F32), ends[pairs + p][i].astype(F32)
                if two:
                    low = pltpu.roll(low, 64, 1)
                else:
                    high = pltpu.roll(high, 64, 1)
                values.append(jnp.where(left, low, high))
            rows = dot(jnp.concatenate(values, axis=0).astype(BF16), spread_ref[0, 0:128, :])
            for b in range(fields):
                at = (pl.ds(i * snaps, snaps), pl.ds(b * nodes, nodes))
                kept = z_ref[at].astype(F32)
                z_ref[at] = (kept + rows[b * snaps : (b + 1) * snaps]).astype(BF16)
        copy = pltpu.make_async_copy(z_ref, z_out, z_sem)
        copy.start()
        return copy

    copy = whole_rows()
    others = sums_ref.at[pl.ds(0, count - 1)]
    pltpu.make_async_copy(others, others, sum_recv_sem).wait()
    pltpu.make_async_copy(others, others, sum_send_sem).wait()
    terms = [sums_ref[i] for i in range(count)]
    while len(terms) > 1:
        terms = [
            terms[i] + terms[i + 1] if i + 1 < len(terms) else terms[i]
            for i in range(0, len(terms), 2)
        ]
    total_ref[...] = terms[0]
    copy.wait()


def basis_kernel(
    row_count, radial, total_ref, z_in, q_ref, r_ref, dmd_ref, z_ref, rows_ref, z_sem
):
    snaps, nodes = q_ref.shape[0], q_ref.shape[3]
    fields = 3 * radial
    load = pltpu.make_async_copy(z_in, z_ref, z_sem)
    load.start()
    lane = lax.broadcasted_iota(jnp.int32, (snaps, 128), 1)
    line = lax.broadcasted_iota(jnp.int32, (snaps, 128), 0)
    lines = []
    for g in range(snaps // 8):
        whole = jnp.broadcast_to(total_ref[g : g + 1, :], (8, 128))
        piece = whole
        for i in range(1, 8):
            piece = jnp.where(line[:8] == i, pltpu.roll(whole, 128 - snaps * i, 1), piece)
        lines.append(piece)
    work = jnp.concatenate(lines, axis=0)
    unit = jnp.logical_and(lane % snaps == line, lane < 4 * snaps)
    work = jnp.where(lane < snaps, work, jnp.where(unit, 1.0, 0.0))
    for k in range(0, snaps - 1, 2):
        row_a, row_b = work[k : k + 1, :], work[k + 1 : k + 2, :]
        col_a = jnp.broadcast_to(work[:, k : k + 1], work.shape)
        col_b = jnp.broadcast_to(work[:, k + 1 : k + 2], work.shape)
        inv_a = 1.0 / col_a[k : k + 1, :]
        cross = col_b[k : k + 1, :]
        ratio = cross * inv_a
        inv_b = 1.0 / (col_b[k + 1 : k + 2, :] - cross * ratio)
        row_b = row_b - ratio * row_a
        col_b = col_b - ratio * col_a
        after = work - col_a * (inv_a * row_a) - col_b * (inv_b * row_b)
        work = jnp.where(line > k + 1, after, jnp.where(line == k + 1, row_b, work))
    pivot = jnp.sum(jnp.where(lane == line, work, 0.0), axis=1, keepdims=True)
    work = work * (1.0 / jnp.sqrt(pivot))
    norm = math.sqrt(row_count)
    inverse = pltpu.roll(work, 128 - snaps, 1)
    big, small = split(inverse * norm)
    weights = jnp.where(lane < 2 * snaps, big.astype(F32), small.astype(F32))
    weights = weights[:, : 3 * snaps].astype(BF16)
    load.wait()
    basis = dot(weights, jnp.concatenate([z_ref[...], z_ref[0:snaps, :]], axis=0))
    for b in range(fields):
        for j in range(nodes // 128):
            first = b * nodes + 128 * j
            rows_ref[j, pl.ds(b, snaps, stride=fields), :] = basis[:, first : first + 128]
    for s in range(snaps):
        for c in range(3):
            value = [
                rows_ref[j, pl.ds((s * 3 + c) * radial, radial), :] for j in range(nodes // 128)
            ]
            q_ref[s, c] = jnp.concatenate(value, axis=1).astype(BF16)
    upper = jnp.where(jnp.logical_and(lane >= line, lane < snaps), work, 0.0)
    r_ref[...] = upper[:, :snaps] / norm
    moved = jnp.where(lane < snaps - 1, pltpu.roll(upper, 127, 1), 0.0)
    back = jnp.where(lane < snaps - 1, inverse, 0.0)
    operator = lax.dot_general(
        moved,
        back,
        (((1,), (1,)), ((), ())),
        precision=lax.Precision.HIGHEST,
        preferred_element_type=F32,
    )
    dmd_ref[...] = operator[:, : snaps - 1]


def shards(wide_count, narrow_count, velocity, extents):
    snaps, _, _, _, radial, nodes = velocity.shape
    fields = 3 * radial
    pairs = (fields + 2) // 2
    vmem = pl.BlockSpec(memory_space=pltpu.VMEM)
    operands = [
        velocity.reshape(snaps, 3, radial, nodes),
        extents,
        *[jnp.asarray(table) for table in tables()],
    ]
    corners = len({1, narrow_count - 1})
    edge = (-(-pairs // 4), snaps, 128)
    face = pltpu.VMEM((2, pairs, snaps, 128), F32)
    dma = pltpu.SemaphoreType.DMA
    limit = 60 * 1024 * 1024
    hbm = pl.BlockSpec(memory_space=pltpu.HBM)
    rows = jax.ShapeDtypeStruct((2 * snaps, fields * nodes), BF16)
    rows, total = pl.pallas_call(
        functools.partial(kernel, wide_count, narrow_count),
        out_shape=(rows, jax.ShapeDtypeStruct((snaps // 8, 128), F32)),
        in_specs=[hbm] * len(operands),
        out_specs=(hbm, vmem),
        scratch_shapes=[
            (pltpu.SMEM if i == 1 else pltpu.VMEM)(operand.shape, operand.dtype)
            for i, operand in enumerate(operands)
        ]
        + [
            dma((len(operands),)),
            pltpu.VMEM((nodes // 128, fields * snaps, 128), F32),
            pltpu.VMEM((fields * snaps, nodes), BF16),
            pltpu.VMEM((2 * snaps, fields * nodes), BF16),
            dma(()),
            face,
            face,
            face,
            face,
            pltpu.VMEM((2,) + edge, F32),
            pltpu.VMEM((2, corners) + edge, F32),
            pltpu.VMEM((2 * snaps, 128), F32),
            pltpu.VMEM((wide_count * narrow_count, snaps // 8, 128), F32),
            dma((4,)),
            dma((4,)),
            dma((2, corners)),
            dma((2, corners)),
            dma(()),
            dma(()),
        ],
        compiler_params=pltpu.CompilerParams(
            collective_id=0, has_side_effects=True, vmem_limit_bytes=limit
        ),
        cost_estimate=pl.CostEstimate(
            flops=400_000_000, bytes_accessed=3_000_000, transcendentals=10_000
        ),
        name="pipe",
    )(*operands)
    row_count = fields * nodes * wide_count * narrow_count
    q, r, dmd = pl.pallas_call(
        functools.partial(basis_kernel, row_count, radial),
        out_shape=(
            jax.ShapeDtypeStruct((snaps, 3, radial, nodes), BF16),
            jax.ShapeDtypeStruct((snaps, snaps), F32),
            jax.ShapeDtypeStruct((snaps, snaps - 1), F32),
        ),
        in_specs=[vmem, hbm],
        out_specs=(vmem, vmem, vmem),
        scratch_shapes=[
            pltpu.VMEM((2 * snaps, fields * nodes), BF16),
            pltpu.VMEM((nodes // 128, fields * snaps, 128), F32),
            dma(()),
        ],
        compiler_params=pltpu.CompilerParams(vmem_limit_bytes=limit),
        name="basis",
    )(total, rows)
    return q.reshape(velocity.shape), r, dmd


def solution(mesh):
    return jax.shard_map(
        functools.partial(shards, mesh.shape["wide"], mesh.shape["narrow"]),
        mesh=mesh,
        in_specs=(P(None, None, "wide", "narrow", None, None), P(None, "wide", "narrow", None)),
        out_specs=(P(None, None, "wide", "narrow", None, None), P(), P()),
        check_vma=False,
    )
```
